256 devices in a mesh: crop: 8 (over z_lo, y), dap: 32 (over z_hi, x, core).
Axes of the slice: x: 4, y: 4, z: 8 (z_hi: 4, z_lo: 2; z = z_hi * 2 + z_lo), core: 2. Of those that a mesh axis runs over, the one named last changes fastest.
Arguments:
- alignment: bfloat16 [512, 512, 256], P(('crop', 'dap')), parts along dimension 0, may hold values from -6 to 6
- alignment_mask: int32 [512, 512], P('crop'), parts along dimension 0, may hold values from 0 to 1, as said below
- cotangent: bfloat16 [4096, 512, 128], P(('crop', 'dap')), parts along dimension 0, may hold values from -6 to 6
- scales: float32 [256], replicated, may hold values from 0.1 to 1.9
- shifts: float32 [256], replicated, may hold values from -3 to 3
- projection: bfloat16 [256, 64], replicated, may hold values from -0.375 to 0.375
- offsets: float32 [64], replicated, may hold values from -3 to 3
- readout: bfloat16 [1024, 128], replicated, may hold values from -0.1875 to 0.1875
- biases: float32 [128], replicated, may hold values from -12 to 12
Outputs:
- pair_update: bfloat16 [4096, 512, 128], P(('crop', 'dap')), parts along dimension 0
- alignment_grad: bfloat16 [512, 512, 256], P(('crop', 'dap')), parts along dimension 0
- projection_grad: float32 [2048, 64], P('crop'), parts along dimension 0
- offsets_grad: float32 [512], P('crop'), parts along dimension 0
- readout_grad: float32 [8192, 128], P('crop'), parts along dimension 0
- biases_grad: float32 [1024], P('crop'), parts along dimension 0
- scales_grad: float32 [2048], P('crop'), parts along dimension 0
- shifts_grad: float32 [2048], P('crop'), parts along dimension 0
The draws below stay inside these ranges and needn't reach their ends.
There are 8 independent parts, one for each index of `crop`. The reference program is written for one: setup_inputs(seed, part) draws one part's arguments, and reference() takes and returns one part's arrays. A program takes and returns all parts, laid end to end along the dimension named above; an argument that names none is the same for every part. Nothing has to cross between parts.
Inputs may be any that keep to these rules, and one draw needn't show every extreme that they name: `alignment_mask`: sequence 0 is 1 at every residue.
All inputs are finite; a program needn't handle non-finite values.
Results may differ from the reference program's by a relative error of at most 0.03.
Values may be sent and summed in bfloat16 or wider, within the bound.
A program may use at most 128 MiB of HBM per device.

```python
import jax
import jax.numpy as jnp
from jax import lax

CM = 256
CZ = 128
CH = 32
RES_DEV = 16
SEQS = 64
RES = 512


def draw_alignment_mask(key, part):
    key = jax.random.fold_in(key, 7)
    first_key, second_key = jax.random.split(key)
    levels = jax.random.randint(first_key, (SEQS, 1), 3, 11)
    rolled = jax.random.randint(second_key, (SEQS, RES), 0, 10)
    present = (rolled < levels).astype(jnp.int32)
    row_ids = jnp.arange(SEQS, dtype=jnp.int32)[:, None]
    present = jnp.where(row_ids == 0, jnp.ones_like(present), present)
    return present.astype(jnp.int32)


def strengthened(result, key, source, target, shards_of, factor):
    owner, partner = [(jnp.arange(result.shape[axis_at]) // (result.shape[axis_at] // shards_of)).reshape([-1 if axis == axis_at else 1 for axis in range(result.ndim)]) for axis_at in (source, target)]
    chosen = jax.random.permutation(key, shards_of)[partner]
    strong = (owner == chosen) | (owner == (partner + shards_of // 2) % shards_of)
    return jnp.where(strong, factor * result, result)


def level_of(own_key, extent, pieces, smallest, high):
    gain, own = 1.0, jax.random.fold_in(own_key, 6)
    for position, blocks in pieces:
        heights = jnp.exp(jax.random.uniform(jax.random.fold_in(own, position), (blocks,), jnp.float32, smallest / len(pieces), high / len(pieces)))
        gain = gain * jnp.repeat(heights, extent[position] // blocks).reshape([-1 if axis == position else 1 for axis in range(len(extent))])
    return gain


def noise(stream_key, dims, deviation, bound, cuts=(), kind=jnp.bfloat16):
    drawn = deviation * jax.random.normal(stream_key, dims, jnp.float32)
    if cuts:
        drawn = drawn * level_of(stream_key, dims, cuts, -0.22, 0.18)
    return jnp.clip(drawn, -bound, bound).astype(kind)


def heavy_noise(own_key, extent, scale, limit, pieces, heavy, kind=jnp.bfloat16):
    result = scale * jax.random.normal(own_key, extent, jnp.float32)
    if pieces:
        result = result * level_of(own_key, extent, pieces, -0.22, 0.18)
    return jnp.clip(strengthened(result, jax.random.fold_in(own_key, 3), *heavy), -limit, limit).astype(kind)


def setup_inputs(seed: int = 0, part: int = 0) -> dict:
    key_of = jax.random.split(jax.random.key(seed), 10)
    part_splits = jax.random.split(jax.random.fold_in(key_of[9], part), 10)
    alignment = noise(part_splits[0], (SEQS, RES, CM), 1.0, 6.0, ((0, 32),))
    alignment_mask = draw_alignment_mask(jax.random.fold_in(jax.random.fold_in(key_of[9], part), 71), part)
    cotangent = heavy_noise(part_splits[2], (RES, RES, CZ), 1.0, 6.0, ((0, 32),), (0, 1, 32, 2.75))
    scales = jnp.clip(1.0 + 0.18 * jax.random.normal(key_of[3], (CM,), jnp.float32), 0.1, 1.9)
    shifts = noise(key_of[4], (CM,), 0.5, 3.0, (), jnp.float32)
    projection = noise(key_of[5], (CM, 2 * CH), CM ** -0.5, 0.375)
    offsets = noise(key_of[6], (2 * CH,), 0.5, 3.0, (), jnp.float32)
    readout = noise(key_of[7], (CH * CH, CZ), (CH * CH) ** -0.5, 0.1875)
    biases = noise(key_of[8], (CZ,), 3.0, 12.0, (), jnp.float32)
    return dict(alignment=alignment, alignment_mask=alignment_mask, cotangent=cotangent, scales=scales, shifts=shifts, projection=projection, offsets=offsets, readout=readout, biases=biases)


def layer_stats(values, scales, shifts):
    wide = values.astype(jnp.float32)
    center = lax.optimization_barrier(jnp.mean(wide, axis=-1, keepdims=True))
    spread = lax.optimization_barrier(jnp.mean(jnp.square(wide - center), axis=-1, keepdims=True))
    inverse = lax.rsqrt(spread + 1e-05)
    standard = (wide - center) * inverse
    normed = (standard * scales + shifts).astype(jnp.bfloat16)
    return (standard, inverse, normed)

def reference(alignment, alignment_mask, cotangent, scales, shifts, projection, offsets, readout, biases):
    mask_all = alignment_mask.astype(jnp.float32)
    standard, inverse, normed = layer_stats(alignment, scales, shifts)
    projected = jnp.einsum('snm,mk->snk', normed.astype(jnp.float32), projection.astype(jnp.float32)) + offsets
    both_sides = (projected * mask_all[:, :, None]).astype(jnp.bfloat16)
    left_side = both_sides[:, :, :CH].astype(jnp.float32)
    right_side = both_sides[:, :, CH:].astype(jnp.float32)
    intersection = jnp.dot(mask_all.T, mask_all, precision=lax.Precision.HIGHEST)
    divisor = 0.001 + intersection
    scaled_grad = (cotangent.astype(jnp.float32) / divisor[:, :, None]).astype(jnp.bfloat16).astype(jnp.float32)
    biases_grad = lax.optimization_barrier(jnp.sum(scaled_grad, axis=(0, 1)))
    readout_wide = readout.astype(jnp.float32)

    def step_fn(carried, begin_at):
        right_acc, readout_acc = carried
        left_piece = lax.dynamic_slice_in_dim(left_side, begin_at, RES_DEV, 1)
        products = jnp.einsum('sic,sjd->ijcd', left_piece, right_side).reshape(RES_DEV, RES, CH * CH)
        products = products.astype(jnp.bfloat16).astype(jnp.float32)
        mixed = jnp.einsum('ijk,kz->ijz', products, readout_wide) + biases
        divisor_piece = lax.dynamic_slice_in_dim(divisor, begin_at, RES_DEV, 0)
        update = (mixed / divisor_piece[:, :, None]).astype(jnp.bfloat16)
        grad_piece = lax.dynamic_slice_in_dim(scaled_grad, begin_at, RES_DEV, 0)
        readout_acc = readout_acc + jnp.einsum('ijk,ijz->kz', products, grad_piece)
        products_grad = jnp.einsum('ijz,kz->ijk', grad_piece, readout_wide).astype(jnp.bfloat16).astype(jnp.float32)
        products_grad = products_grad.reshape(RES_DEV, RES, CH, CH)
        left_piece_grad = jnp.einsum('ijcd,sjd->sic', products_grad, right_side)
        right_acc = right_acc + jnp.einsum('ijcd,sic->sjd', products_grad, left_piece)
        return ((right_acc, readout_acc), (update, left_piece_grad))
    begins = jnp.arange(RES // RES_DEV, dtype=jnp.int32) * RES_DEV
    initial = (jnp.zeros((SEQS, RES, CH), jnp.float32), jnp.zeros((CH * CH, CZ), jnp.float32))
    (right_grad, readout_grad), (updates, left_pieces) = lax.scan(step_fn, initial, begins)
    pair_update = updates.reshape(RES, RES, CZ)
    left_grad = jnp.transpose(left_pieces, (1, 0, 2, 3)).reshape(SEQS, RES, CH)
    proj_grad = (jnp.concatenate([left_grad, right_grad], axis=-1) * mask_all[:, :, None]).astype(jnp.bfloat16)
    proj_wide = proj_grad.astype(jnp.float32)
    offsets_grad = lax.optimization_barrier(jnp.sum(proj_wide, axis=(0, 1)))
    projection_grad = jnp.einsum('snm,snk->mk', normed.astype(jnp.float32), proj_wide)
    normed_grad = jnp.einsum('snk,mk->snm', proj_wide, projection.astype(jnp.float32))
    scales_grad = lax.optimization_barrier(jnp.sum(normed_grad * standard, axis=(0, 1)))
    shifts_grad = lax.optimization_barrier(jnp.sum(normed_grad, axis=(0, 1)))
    hatted = normed_grad * scales
    alignment_grad = (hatted - lax.optimization_barrier(jnp.mean(hatted, axis=-1, keepdims=True)) - standard * lax.optimization_barrier(jnp.mean(hatted * standard, axis=-1, keepdims=True))) * inverse
    alignment_grad = alignment_grad.astype(jnp.bfloat16)
    return (pair_update, alignment_grad, projection_grad, offsets_grad, readout_grad, biases_grad, scales_grad, shifts_grad)
```

```python
import jax
import jax.numpy as jnp
from jax import lax
from jax.experimental import pallas as pl
from jax.experimental.pallas import tpu as pltpu
from jax.sharding import PartitionSpec as P

F32 = jnp.float32
BF16 = jnp.bfloat16
MESH = pl.DeviceIdType.MESH


def mm(a, b):
    return lax.dot_general(a, b, (((1,), (0,)), ((), ())), preferred_element_type=F32)


def mm_nt(a, b):
    return lax.dot_general(a, b, (((1,), (1,)), ((), ())), preferred_element_type=F32)


def mm_tn(a, b):
    return lax.dot_general(a, b, (((0,), (0,)), ((), ())), preferred_element_type=F32)


def iota(shape, dim):
    return lax.broadcasted_iota(jnp.int32, shape, dim)


def kernel(
    al, mask, cot, scales, shifts, proj, offs, readout, biases,
    pair_o, al_o, pg_o, og_o, rg_o, bg_o, sg_o, hg_o,
    mcol, std, inv, normed, both, l_out, l_in, l_f, l_all, l_t, w, ro_f,
    rec, g, perm, perm_t, r_buf, r_k, r_j, t, q,
    d_buf, c_in, s1, x_in, s2, z_in,
    lg_f, lg_out, lg_in, rg_l, rg_f, rg_b, ra, rb, rc_send, rc, rh, rk,
    pb, pb_core, pb_x, pb_xs, pb_z, pb_half, pb_other, bsum,
    l_ss, l_rs, e_ss, e_rs, r_ss, r_rs, d_ss, d_rs, a_ss, a_rs, b_ss, b_rs,
):
    me = lax.axis_index("dap")
    core = lax.rem(me, 2)
    xx = lax.rem(lax.div(me, 2), 4)
    zz = lax.div(me, 8)
    sign = 1 - 2 * core
    xs, xm, xf = (lax.rem(xx + 4 + sign, 4), lax.rem(xx + 4 - sign, 4), lax.rem(xx + 2, 4))
    zs, zm, zf = (lax.rem(zz + 4 + sign, 4), lax.rem(zz + 4 - sign, 4), lax.rem(zz + 2, 4))
    other = 1 - core

    def dev(z, x, c):
        return (z * 4 + x) * 2 + c

    def slot(x, c, z):
        return (x * 2 + c) * 4 + z

    def slot_dev(s):
        return dev(lax.rem(s, 4), lax.div(s, 8), lax.rem(lax.div(s, 4), 2))

    sib = dev(zz, xx, other)
    mine = slot(xx, core, zz)

    def remote(src, dst, ss, rs, target):
        return pltpu.make_async_remote_copy(
            src_ref=src, dst_ref=dst, send_sem=ss, recv_sem=rs,
            device_id={"dap": target}, device_id_type=MESH,
        )

    barrier = pltpu.get_barrier_semaphore()

    def greet(k, carry):
        pl.semaphore_signal(
            barrier, inc=1, device_id={"dap": lax.rem(me + k, 32)}, device_id_type=MESH
        )
        return carry

    lax.fori_loop(1, 32, greet, 0)

    mask_f = mask[...].astype(F32)
    mask_t = mask_f.T
    for k in range(2):
        mcol[k * 512:(k + 1) * 512, :] = jnp.sum(
            jnp.where(iota((512, 64), 1) == 2 * me + k, mask_t, 0.0), axis=1, keepdims=True
        )

    def norm_step(b, carry):
        rows = pl.ds(pl.multiple_of(b * 128, 128), 128)
        wide = al[rows, :].astype(F32)
        center = jnp.mean(wide, axis=-1, keepdims=True)
        dev_ = wide - center
        spread = jnp.mean(dev_ * dev_, axis=-1, keepdims=True)
        inverse = lax.rsqrt(spread + 1e-05)
        standard = dev_ * inverse
        std[rows, :] = standard
        inv[rows, :] = inverse
        nb = (standard * scales[...] + shifts[...]).astype(BF16)
        normed[rows, :] = nb
        sides = (mm(nb, proj[...]) + offs[...]) * mcol[rows, :]
        both[rows, :] = sides
        return carry

    lax.fori_loop(0, 8, norm_step, 0)
    cat = jnp.concatenate([both[0:512, :], both[512:1024, :]], axis=1)
    l_out[...] = cat.astype(BF16).reshape(32, 16, 128)
    cat_t = cat.T
    r_buf[mine] = jnp.concatenate([cat_t[32:64], cat_t[96:128]], axis=0).astype(BF16)

    pl.semaphore_wait(barrier, 31)

    def r_send(s, target, k):
        remote(r_buf.at[s], r_buf.at[s], r_ss.at[k], r_rs.at[s], target).start()

    def r_wait(s):
        remote(r_buf.at[s], r_buf.at[s], r_ss.at[0], r_rs.at[s], sib).wait_recv()

    r_send(mine, dev(zs, xx, core), 0)
    r_send(mine, dev(zm, xx, core), 1)
    r_send(mine, dev(zz, xs, core), 2)
    r_send(mine, dev(zz, xm, core), 3)
    r_send(mine, sib, 4)

    def l_copy(k):
        s = lax.rem(mine + k, 32)
        p = slot_dev(s)
        return remote(l_out.at[p], l_in.at[mine], l_ss.at[k], l_rs.at[mine], p)

    def l_send(k, carry):
        l_copy(k).start()
        return carry

    lax.fori_loop(1, 32, l_send, 0)
    l_in[mine] = l_out[me]

    mask_b = mask_f.astype(BF16)
    own_cols = (iota((512, 16), 0) == 16 * me + iota((512, 16), 1)).astype(F32).astype(BF16)
    mask_own = mm(mask_b, own_cols).astype(BF16)
    recip = 1.0 / (0.001 + mm(mask_t.astype(BF16), mask_own))
    total = jnp.zeros((1, 128), F32)
    for i in range(16):
        rec_i = jnp.broadcast_to(recip[:, i:i + 1], (512, 128))
        rec[i] = rec_i
        sg = (cot[i].astype(F32) * rec_i).astype(BF16)
        g[:, i * 128:(i + 1) * 128] = sg
        total = total + jnp.sum(sg.astype(F32), axis=0, keepdims=True)
    bsum[...] = total

    ro_f[...] = readout[...].astype(F32)
    for d in range(32):
        w[:, d * 128:(d + 1) * 128] = ro_f[pl.ds(d, 32, stride=32), :].astype(BF16)

    def packed(a):
        return lax.rem(a, 8) * 64 + lax.rem(lax.div(a, 8), 2) * 32 + lax.div(a, 16)

    perm[...] = (iota((512, 512), 1) == packed(iota((512, 512), 0))).astype(F32).astype(BF16)
    perm_t[...] = (iota((512, 512), 0) == packed(iota((512, 512), 1))).astype(F32).astype(BF16)

    def l_wait(k, carry):
        s = lax.rem(mine + k, 32)
        remote(l_out.at[0], l_in.at[s], l_ss.at[k], l_rs.at[s], sib).wait_recv()
        return carry

    lax.fori_loop(1, 32, l_wait, 0)
    l_f[...] = l_in[...].reshape(512, 128).astype(F32)
    for i in range(16):
        v = l_f[pl.ds(i, 32, stride=16), :]
        parts = [v[x * 8:x * 8 + 8, k * 64:k * 64 + 32] for x in range(4) for k in range(2)]
        l_all[i * 64:(i + 1) * 64, :] = jnp.concatenate(parts, axis=0).astype(BF16)
    l_t[...] = l_all[...].astype(F32).T.astype(BF16)

    def t_step(dp, carry):
        wb = w[:, pl.ds(pl.multiple_of(dp * 256, 256), 256)]
        r = mm(l_all[...], wb).astype(BF16)
        for i in range(16):
            for dd in range(2):
                t[:, 2 * dp + dd, :, i * 128:(i + 1) * 128] = r[
                    i * 64:(i + 1) * 64, dd * 128:(dd + 1) * 128
                ].reshape(4, 16, 128)
        return carry

    lax.fori_loop(0, 16, t_step, 0)

    r_wait(slot(xx, core, zm))
    r_send(slot(xx, core, zm), dev(zs, xx, core), 5)
    for n, z_ in enumerate((zm, zs)):
        if n == 1:
            r_wait(slot(xx, core, z_))
        r_send(slot(xx, core, z_), dev(zz, xs, core), 6 + 3 * n)
        r_send(slot(xx, core, z_), dev(zz, xm, core), 7 + 3 * n)
        r_send(slot(xx, core, z_), sib, 8 + 3 * n)

    def d_group(x_, n):
        raw = mm_nt(t[x_].reshape(512, 2048), g[...]).astype(BF16)
        d_buf[x_] = mm(perm_t[...], raw).astype(BF16).reshape(2, 256, 512)
        remote(
            d_buf.at[x_, other], c_in.at[x_], d_ss.at[n], d_rs.at[x_], sib
        ).start()

    d_group(xf, 0)
    r_wait(slot(xx, core, zf))
    r_send(slot(xx, core, zf), dev(zz, xs, core), 12)
    r_send(slot(xx, core, zf), dev(zz, xm, core), 13)
    r_send(slot(xx, core, zf), sib, 14)
    r_wait(slot(xm, core, zz))
    r_send(slot(xm, core, zz), dev(zz, xs, core), 15)
    r_send(slot(xm, core, zz), sib, 16)
    r_wait(slot(xs, core, zz))
    r_send(slot(xs, core, zz), sib, 17)
    d_group(xm, 1)
    for n, z_ in enumerate((zm, zs)):
        r_wait(slot(xm, core, z_))
        r_send(slot(xm, core, z_), dev(zz, xs, core), 18 + 3 * n)
        r_send(slot(xm, core, z_), sib, 19 + 3 * n)
        r_wait(slot(xs, core, z_))
        r_send(slot(xs, core, z_), sib, 20 + 3 * n)
    d_group(xs, 2)
    r_wait(slot(xm, core, zf))
    r_send(slot(xm, core, zf), dev(zz, xs, core), 24)
    r_send(slot(xm, core, zf), sib, 25)
    r_wait(slot(xs, core, zf))
    r_send(slot(xs, core, zf), sib, 26)
    r_wait(slot(xf, core, zz))
    r_send(slot(xf, core, zz), sib, 27)
    d_group(xx, 3)

    def wide(ref):
        return ref[...].astype(F32)

    def c_wait(x_, n):
        remote(d_buf.at[x_, other], c_in.at[x_], d_ss.at[n], d_rs.at[x_], sib).wait_recv()

    def core_sum(x_):
        return d_buf[x_, core].astype(F32) + c_in[x_].astype(F32)

    def x_copy(x_, n, target_x):
        return remote(
            s1.at[x_], x_in.at[n], d_ss.at[4 + n], d_rs.at[4 + n], dev(zz, target_x, core)
        )

    c_wait(xf, 0)
    s1[xf] = core_sum(xf).astype(BF16)
    x_copy(xf, 0, xs).start()
    c_wait(xm, 1)
    s1[xm] = core_sum(xm).astype(BF16)
    x_copy(xm, 1, xm).start()

    for n, z_ in enumerate((zm, zs, zf)):
        r_wait(slot(xf, core, z_))
        r_send(slot(xf, core, z_), sib, 28 + n)

    def q_group(x_):
        for z_ in range(4):
            r_wait(slot(x_, other, z_))
        raw = r_buf[pl.ds(x_ * 8, 8)].reshape(512, 512)
        moved = mm(perm[...], raw)
        r_k[...] = moved.astype(BF16)
        r_j[x_] = moved.T.astype(BF16)

        def q_step(ib, carry):
            block = mm(r_k[...], g[:, pl.ds(pl.multiple_of(ib * 256, 256), 256)]).astype(BF16)
            for d in range(32):
                for ii in range(2):
                    q[2 * ib + ii, x_, :, d * 128:(d + 1) * 128] = block[
                        d * 16:(d + 1) * 16, ii * 128:(ii + 1) * 128
                    ]
            return carry

        lax.fori_loop(0, 8, q_step, 0)

    q_group(xx)
    x_copy(xf, 0, xs).wait_recv()
    c_wait(xs, 2)
    s1[xs] = (core_sum(xs) + x_in[0].astype(F32)).astype(BF16)
    x_copy(xs, 2, xs).start()
    q_group(xm)
    q_group(xs)
    c_wait(xx, 3)
    x_copy(xm, 1, xm).wait_recv()
    x_copy(xs, 2, xs).wait_recv()
    s2[...] = (
        core_sum(xx) + x_in[1].astype(F32) + x_in[2].astype(F32)
    ).astype(BF16).reshape(4, 64, 512)

    def z_copy(z_, n, target_z):
        return remote(
            s2.at[z_], z_in.at[n], d_ss.at[7 + n], d_rs.at[7 + n], dev(target_z, xx, core)
        )

    z_copy(zf, 0, zs).start()
    z_copy(zm, 1, zm).start()
    q_group(xf)
    z_copy(zf, 0, zs).wait_recv()
    z_copy(zf, 0, zs).wait_send()
    s2[zs] = (s2[zs].astype(F32) + z_in[0].astype(F32)).astype(BF16)
    z_copy(zs, 2, zs).start()

    def lg_step(b, carry):
        rows = q[pl.ds(pl.multiple_of(b * 4, 4), 4)].reshape(256, 4096)
        lg_f[pl.ds(pl.multiple_of(b * 256, 256), 256), 0:32] = mm_nt(rows, w[...])
        return carry

    lax.fori_loop(0, 4, lg_step, 0)
    for s in range(32):
        base = (s // 8) * 16 + s % 8
        pieces = [
            lg_f[pl.ds(base + 8 * k, 16, stride=64), :][:, 0:32] for k in range(2)
        ]
        pieces.append(jnp.zeros((16, 64), F32))
        lg_out[s] = jnp.concatenate(pieces, axis=1).astype(BF16)

    def e_copy(k):
        s = lax.rem(mine + k, 32)
        return remote(lg_out.at[s], lg_in.at[me], e_ss.at[k], e_rs.at[me], slot_dev(s))

    def e_send(k, carry):
        e_copy(k).start()
        return carry

    lax.fori_loop(1, 32, e_send, 0)
    lg_in[me] = lg_out[mine]

    def rg_step(dp, carry):
        cols = pl.ds(pl.multiple_of(dp * 256, 256), 256)
        rg_l[:, cols] = mm(l_t[...], q[:, :, :, cols].reshape(1024, 256))
        return carry

    lax.fori_loop(0, 16, rg_step, 0)
    for d in range(32):
        rg_f[pl.ds(d, 32, stride=32), :] = rg_l[:, d * 128:(d + 1) * 128]
    rg_b[...] = rg_f[...].astype(BF16).reshape(2, 512, 128)
    a0 = remote(rg_b.at[other], ra, a_ss.at[0], a_rs.at[0], sib)
    a0.start()

    def u_step(ib, carry):
        cols = pl.ds(pl.multiple_of(ib * 256, 256), 256)
        acc = mm(r_j[0], t[0, :, :, cols].reshape(512, 256))
        for x in range(1, 4):
            acc = acc + mm(r_j[x], t[x, :, :, cols].reshape(512, 256))
        for ii in range(2):
            pair_o[2 * ib + ii] = (
                (acc[:, ii * 128:(ii + 1) * 128] + biases[...]) * rec[2 * ib + ii]
            ).astype(BF16)
        return carry

    lax.fori_loop(0, 4, u_step, 0)

    a0.wait_recv()
    rb[...] = (rg_b[core].astype(F32) + ra[...].astype(F32)).astype(BF16).reshape(4, 128, 128)

    def a_x(k):
        x_ = lax.rem(xx + k, 4)
        return remote(rb.at[x_], rc.at[xx], a_ss.at[k], a_rs.at[1 + xx], dev(zz, x_, core))

    for k in range(1, 4):
        a_x(k).start()
    rc[xx] = rb[xx]

    lax.fori_loop(4, 8, u_step, 0)

    for k in range(1, 4):
        x_ = lax.rem(xx + k, 4)
        remote(rb.at[x_], rc.at[x_], a_ss.at[k], a_rs.at[1 + x_], sib).wait_recv()
    rc_send[zz] = (
        (rc[0].astype(F32) + rc[1].astype(F32)) + (rc[2].astype(F32) + rc[3].astype(F32))
    ).astype(BF16)

    def a_z(k):
        z_ = lax.rem(zz + k, 4)
        return remote(
            rc_send.at[zz], rc_send.at[zz], a_ss.at[3 + k], a_rs.at[5 + zz], dev(z_, xx, core)
        )

    for k in range(1, 4):
        a_z(k).start()

    def e_wait(k, carry):
        p = lax.rem(me + k, 32)
        remote(lg_out.at[0], lg_in.at[p], e_ss.at[k], e_rs.at[p], sib).wait_recv()
        return carry

    lax.fori_loop(1, 32, e_wait, 0)
    z_copy(zm, 1, zm).wait_recv()
    z_copy(zs, 2, zs).wait_recv()
    right = s2[zz].astype(F32) + z_in[1].astype(F32) + z_in[2].astype(F32)
    right_t = right.T
    left = lg_in[...].reshape(512, 128).astype(F32)
    for k in range(2):
        both[k * 512:(k + 1) * 512, :] = jnp.concatenate(
            [left[:, k * 32:(k + 1) * 32], right_t[:, k * 32:(k + 1) * 32]], axis=1
        ) * mcol[k * 512:(k + 1) * 512, :]

    def grad_step(b, carry):
        sc_acc, sh_acc, of_acc, pj_acc = carry
        rows = pl.ds(pl.multiple_of(b * 128, 128), 128)
        pgb = both[rows, :].astype(BF16)
        ng = mm_nt(pgb, proj[...])
        standard = std[rows, :]
        pj_acc = pj_acc + mm_tn(pgb, normed[rows, :])
        of_acc = of_acc + jnp.sum(pgb.astype(F32), axis=0, keepdims=True)
        sc_acc = sc_acc + jnp.sum(ng * standard, axis=0, keepdims=True)
        sh_acc = sh_acc + jnp.sum(ng, axis=0, keepdims=True)
        h = ng * scales[...]
        m1 = jnp.mean(h, axis=-1, keepdims=True)
        m2 = jnp.mean(h * standard, axis=-1, keepdims=True)
        al_o[rows, :] = ((h - m1 - standard * m2) * inv[rows, :]).astype(BF16)
        return (sc_acc, sh_acc, of_acc, pj_acc)

    sc_acc, sh_acc, of_acc, pj_acc = lax.fori_loop(
        0, 8, grad_step,
        (jnp.zeros((1, 256), F32), jnp.zeros((1, 256), F32), jnp.zeros((1, 64), F32),
         jnp.zeros((64, 256), F32)),
    )
    pb[0] = pj_acc[0:40]
    pb[1, 0:24] = pj_acc[40:64]
    pb[1, 24:40] = jnp.concatenate(
        [
            sc_acc, sh_acc,
            jnp.concatenate([of_acc, jnp.zeros((1, 64), F32), bsum[...]], axis=1),
            jnp.zeros((13, 256), F32),
        ],
        axis=0,
    )

    b0 = remote(pb.at[other], pb_core, b_ss.at[0], b_rs.at[0], sib)
    b0.start()

    for k in range(1, 4):
        z_ = lax.rem(zz + k, 4)
        remote(
            rc_send.at[z_], rc_send.at[z_], a_ss.at[3 + k], a_rs.at[5 + z_], sib
        ).wait_recv()
    a_z(1).wait_send()
    rh[xx] = (
        (rc_send[0].astype(F32) + rc_send[1].astype(F32))
        + (rc_send[2].astype(F32) + rc_send[3].astype(F32))
    ).astype(BF16)

    def a_g(k):
        x_ = lax.rem(xx + k, 4)
        return remote(
            rh.at[xx], rh.at[xx], a_ss.at[6 + k], a_rs.at[9 + xx], dev(zz, x_, core)
        )

    for k in range(1, 4):
        a_g(k).start()

    b0.wait_recv()
    pb_x[xx] = pb[core] + pb_core[...]

    def b_x(k):
        x_ = lax.rem(xx + k, 4)
        return remote(pb_x.at[xx], pb_x.at[xx], b_ss.at[k], b_rs.at[1 + xx], dev(zz, x_, core))

    for k in range(1, 4):
        b_x(k).start()

    for k in range(1, 4):
        x_ = lax.rem(xx + k, 4)
        remote(rh.at[x_], rh.at[x_], a_ss.at[6 + k], a_rs.at[9 + x_], sib).wait_recv()
    a_last = remote(rh, rk, a_ss.at[10], a_rs.at[13], sib)
    a_last.start()

    for k in range(1, 4):
        x_ = lax.rem(xx + k, 4)
        remote(pb_x.at[x_], pb_x.at[x_], b_ss.at[k], b_rs.at[1 + x_], sib).wait_recv()
    pb_z[zz] = (pb_x[0] + pb_x[1]) + (pb_x[2] + pb_x[3])

    def b_z(k):
        z_ = lax.rem(zz + k, 4)
        return remote(
            pb_z.at[zz], pb_z.at[zz], b_ss.at[3 + k], b_rs.at[5 + zz], dev(z_, xx, core)
        )

    for k in range(1, 4):
        b_z(k).start()

    a_last.wait_recv()
    rg_o[pl.ds(pl.multiple_of(core * 512, 512), 512), :] = rh[...].reshape(512, 128).astype(F32)
    rg_o[pl.ds(pl.multiple_of(other * 512, 512), 512), :] = rk[...].reshape(512, 128).astype(F32)

    for k in range(1, 4):
        z_ = lax.rem(zz + k, 4)
        remote(pb_z.at[z_], pb_z.at[z_], b_ss.at[3 + k], b_rs.at[5 + z_], sib).wait_recv()
    pb_half[core] = (pb_z[0] + pb_z[1]) + (pb_z[2] + pb_z[3])
    b_last = remote(pb_half.at[core], pb_half.at[core], b_ss.at[7], b_rs.at[9], sib)
    b_last.start()

    for k in range(31):
        remote(r_buf.at[0], r_buf.at[0], r_ss.at[k], r_rs.at[0], sib).wait_send()

    def drain(k, carry):
        remote(l_out.at[0], l_in.at[0], l_ss.at[k], l_rs.at[0], sib).wait_send()
        remote(lg_out.at[0], lg_in.at[0], e_ss.at[k], e_rs.at[0], sib).wait_send()
        return carry

    lax.fori_loop(1, 32, drain, 0)
    for n, x_ in enumerate((xf, xm, xs, xx)):
        remote(d_buf.at[x_, other], c_in.at[x_], d_ss.at[n], d_rs.at[x_], sib).wait_send()
    x_copy(xf, 0, xs).wait_send()
    x_copy(xm, 1, xm).wait_send()
    x_copy(xs, 2, xs).wait_send()
    z_copy(zm, 1, zm).wait_send()
    z_copy(zs, 2, zs).wait_send()
    a0.wait_send()
    for k in range(1, 4):
        a_x(k).wait_send()
        a_g(k).wait_send()
        b_x(k).wait_send()
        b_z(k).wait_send()
    a_z(2).wait_send()
    a_z(3).wait_send()
    a_last.wait_send()
    b0.wait_send()

    remote(
        pb_half.at[other], pb_half.at[other], b_ss.at[7], b_rs.at[9], sib
    ).wait_recv()
    b_last.wait_send()
    pj = jnp.concatenate([pb_half[0], pb_half[1, 0:24]], axis=0)
    pg_o[...] = pj.T
    sg_o[...] = pb_half[1, 24:25, :]
    hg_o[...] = pb_half[1, 25:26, :]
    og_o[...] = pb_half[1, 26:27, 0:64]
    bg_o[...] = pb_half[1, 26:27, 128:256]


def per_device(
    alignment, alignment_mask, cotangent, scales, shifts, projection, offsets, readout, biases
):
    vmem = pl.BlockSpec(memory_space=pltpu.VMEM)
    shape = jax.ShapeDtypeStruct
    scratch = [
        pltpu.VMEM((1024, 1), F32),
        pltpu.VMEM((1024, 256), F32),
        pltpu.VMEM((1024, 1), F32),
        pltpu.VMEM((1024, 256), BF16),
        pltpu.VMEM((1024, 64), F32),
        pltpu.VMEM((32, 16, 128), BF16),
        pltpu.VMEM((32, 16, 128), BF16),
        pltpu.VMEM((512, 128), F32),
        pltpu.VMEM((1024, 32), BF16),
        pltpu.VMEM((32, 1024), BF16),
        pltpu.VMEM((32, 4096), BF16),
        pltpu.VMEM((1024, 128), F32),
        pltpu.VMEM((16, 512, 128), F32),
        pltpu.VMEM((512, 2048), BF16),
        pltpu.VMEM((512, 512), BF16),
        pltpu.VMEM((512, 512), BF16),
        pltpu.VMEM((32, 64, 512), BF16),
        pltpu.VMEM((512, 512), BF16),
        pltpu.VMEM((4, 512, 512), BF16),
        pltpu.VMEM((4, 32, 16, 2048), BF16),
        pltpu.VMEM((16, 4, 16, 4096), BF16),
        pltpu.VMEM((4, 2, 256, 512), BF16),
        pltpu.VMEM((4, 256, 512), BF16),
        pltpu.VMEM((4, 256, 512), BF16),
        pltpu.VMEM((3, 256, 512), BF16),
        pltpu.VMEM((4, 64, 512), BF16),
        pltpu.VMEM((3, 64, 512), BF16),
        pltpu.VMEM((1024, 128), F32),
        pltpu.VMEM((32, 16, 128), BF16),
        pltpu.VMEM((32, 16, 128), BF16),
        pltpu.VMEM((32, 4096), F32),
        pltpu.VMEM((1024, 128), F32),
        pltpu.VMEM((2, 512, 128), BF16),
        pltpu.VMEM((512, 128), BF16),
        pltpu.VMEM((4, 128, 128), BF16),
        pltpu.VMEM((4, 128, 128), BF16),
        pltpu.VMEM((4, 128, 128), BF16),
        pltpu.VMEM((4, 128, 128), BF16),
        pltpu.VMEM((4, 128, 128), BF16),
        pltpu.VMEM((2, 40, 256), F32),
        pltpu.VMEM((40, 256), F32),
        pltpu.VMEM((4, 40, 256), F32),
        pltpu.VMEM((8, 128), F32),
        pltpu.VMEM((4, 40, 256), F32),
        pltpu.VMEM((2, 40, 256), F32),
        pltpu.VMEM((8, 128), F32),
        pltpu.VMEM((1, 128), F32),
    ] + [pltpu.SemaphoreType.DMA((n,)) for n in (32, 32, 32, 32, 32, 32, 10, 10, 14, 14, 10, 10)]
    outs = pl.pallas_call(
        kernel,
        out_shape=(
            shape((16, 512, 128), BF16),
            shape((1024, 256), BF16),
            shape((256, 64), F32),
            shape((1, 64), F32),
            shape((1024, 128), F32),
            shape((1, 128), F32),
            shape((1, 256), F32),
            shape((1, 256), F32),
        ),
        in_specs=[vmem] * 9,
        out_specs=[vmem] * 8,
        scratch_shapes=scratch,
        compiler_params=pltpu.CompilerParams(
            collective_id=0, has_side_effects=True, vmem_limit_bytes=62 * 1024 * 1024
        ),
        cost_estimate=pl.CostEstimate(
            flops=16_000_000_000, bytes_accessed=6_000_000, transcendentals=0
        ),
        name="outer_product_mean",
    )(
        alignment.reshape(1024, 256),
        alignment_mask,
        cotangent,
        scales.reshape(1, 256),
        shifts.reshape(1, 256),
        projection,
        offsets.reshape(1, 64),
        readout,
        biases.reshape(1, 128),
    )
    return (
        outs[0],
        outs[1].reshape(2, 512, 256),
        outs[2],
        outs[3].reshape(64),
        outs[4],
        outs[5].reshape(128),
        outs[6].reshape(256),
        outs[7].reshape(256),
    )


def solution(mesh):
    return jax.shard_map(
        per_device,
        mesh=mesh,
        in_specs=(
            P(("crop", "dap"), None, None),
            P("crop", None),
            P(("crop", "dap"), None, None),
            P(),
            P(),
            P(),
            P(),
            P(),
            P(),
        ),
        out_specs=(
            P(("crop", "dap"), None, None),
            P(("crop", "dap"), None, None),
            P("crop", None),
            P("crop"),
            P("crop", None),
            P("crop"),
            P("crop"),
            P("crop"),
        ),
        check_vma=False,
    )
```

```python
import jax
import jax.numpy as jnp
from jax import lax
from jax.experimental import pallas as pl
from jax.experimental.pallas import tpu as pltpu
from jax.sharding import PartitionSpec as P

F32 = jnp.float32
BF16 = jnp.bfloat16
MESH = pl.DeviceIdType.MESH


def mm(a, b):
    return lax.dot_general(a, b, (((1,), (0,)), ((), ())), preferred_element_type=F32)


def mm_nt(a, b):
    return lax.dot_general(a, b, (((1,), (1,)), ((), ())), preferred_element_type=F32)


def mm_tn(a, b):
    return lax.dot_general(a, b, (((0,), (0,)), ((), ())), preferred_element_type=F32)


def iota(shape, dim):
    return lax.broadcasted_iota(jnp.int32, shape, dim)


def kernel(
    al, mask, cot, scales, shifts, proj, offs, readout, biases,
    pair_o, al_o, pg_o, og_o, rg_o, bg_o, sg_o, hg_o,
    cot_v, pair_v, al_v, mcol, std, inv, normed, both, l_out, l_in, l_f, l_all, l_t, w, ro_f,
    rec, g, perm, perm_t, r_buf, r_k, r_j, t, q,
    d_buf, c_in, s1, x_in, s2, z_in,
    lg_f, lg_out, lg_in, rg_l, rg_f, rg_b, ra, rb, rc, re, rh, rk,
    ng_s, pb, pb_core, pb_x, pb_z, pb_half, bsum,
    l_ss, l_rs, e_ss, e_rs, r_ss, r_rs, d_ss, d_rs, a_ss, a_rs, b_ss, b_rs, io,
):
    me = lax.axis_index("dap")
    core = lax.rem(me, 2)
    xx = lax.rem(lax.div(me, 2), 4)
    zz = lax.div(me, 8)
    sign = 1 - 2 * core
    xs, xm, xf = (lax.rem(xx + 4 + sign, 4), lax.rem(xx + 4 - sign, 4), lax.rem(xx + 2, 4))
    zs, zm, zf = (lax.rem(zz + 4 + sign, 4), lax.rem(zz + 4 - sign, 4), lax.rem(zz + 2, 4))
    other = 1 - core

    def dev(z, x, c):
        return (z * 4 + x) * 2 + c

    def slot(x, c, z):
        return (x * 2 + c) * 4 + z

    def slot_dev(s):
        return dev(lax.rem(s, 4), lax.div(s, 8), lax.rem(lax.div(s, 4), 2))

    sib = dev(zz, xx, other)
    mine = slot(xx, core, zz)

    def remote(src, dst, ss, rs, target):
        return pltpu.make_async_remote_copy(
            src_ref=src, dst_ref=dst, send_sem=ss, recv_sem=rs,
            device_id={"dap": target}, device_id_type=MESH,
        )

    barrier = pltpu.get_barrier_semaphore()

    def greet(k, carry):
        pl.semaphore_signal(
            barrier, inc=1, device_id={"dap": lax.rem(me + k, 32)}, device_id_type=MESH
        )
        return carry

    lax.fori_loop(1, 32, greet, 0)
    cot_copy = pltpu.make_async_copy(cot, cot_v, io.at[0])
    cot_copy.start()

    mask_f = mask[...].astype(F32)
    mask_t = mask_f.T
    for k in range(2):
        mcol[k * 512:(k + 1) * 512, :] = jnp.sum(
            jnp.where(iota((512, 64), 1) == 2 * me + k, mask_t, 0.0), axis=1, keepdims=True
        )
    for k in range(2):
        rows = slice(k * 512, (k + 1) * 512)
        wide = al[rows, :].astype(F32)
        center = jnp.mean(wide, axis=-1, keepdims=True)
        apart = wide - center
        spread = jnp.mean(apart * apart, axis=-1, keepdims=True)
        inverse = lax.rsqrt(spread + 1e-05)
        standard = apart * inverse
        std[rows, :] = standard
        inv[rows, :] = inverse
        normed[rows, :] = (standard * scales[...] + shifts[...]).astype(BF16)
    both[...] = (mm_nt(normed[...], proj[...]) + offs[...]) * mcol[...]
    cat = jnp.concatenate([both[0:512, :], both[512:1024, :]], axis=1)
    l_out[...] = cat.astype(BF16).reshape(32, 16, 128)
    cat_t = cat.T
    r_buf[mine] = jnp.concatenate([cat_t[32:64], cat_t[96:128]], axis=0).astype(BF16)

    pl.semaphore_wait(barrier, 31)

    def l_send(k, carry):
        s = lax.rem(mine + k, 32)
        p = slot_dev(s)
        remote(l_out.at[p], l_in.at[mine], l_ss.at[k], l_rs.at[mine], p).start()
        return carry

    lax.fori_loop(1, 32, l_send, 0)

    def r_send(s, target, k):
        remote(r_buf.at[s], r_buf.at[s], r_ss.at[k], r_rs.at[s], target).start()

    def r_wait(s):
        remote(r_buf.at[s], r_buf.at[s], r_ss.at[0], r_rs.at[s], sib).wait_recv()

    r_send(mine, dev(zs, xx, core), 0)
    r_send(mine, dev(zm, xx, core), 1)
    r_send(mine, dev(zz, xs, core), 2)
    r_send(mine, dev(zz, xm, core), 3)
    r_send(mine, sib, 4)
    l_in[mine] = l_out[me]

    mask_b = mask_f.astype(BF16)
    own_cols = (iota((512, 16), 0) == 16 * me + iota((512, 16), 1)).astype(F32).astype(BF16)
    mask_own = mm(mask_b, own_cols).astype(BF16)
    recip = 1.0 / (0.001 + mm(mask_t.astype(BF16), mask_own))
    total = jnp.zeros((1, 128), F32)
    cot_copy.wait()
    for i in range(16):
        rec_i = jnp.broadcast_to(recip[:, i:i + 1], (512, 128))
        rec[i] = rec_i
        sg = (cot_v[i].astype(F32) * rec_i).astype(BF16)
        g[:, i * 128:(i + 1) * 128] = sg
        total = total + jnp.sum(sg.astype(F32), axis=0, keepdims=True)
    bsum[...] = total

    ro_f[...] = readout[...].astype(F32)
    for d in range(32):
        w[:, d * 128:(d + 1) * 128] = ro_f[pl.ds(d, 32, stride=32), :].astype(BF16)

    def packed(a):
        return lax.rem(a, 8) * 64 + lax.rem(lax.div(a, 8), 2) * 32 + lax.div(a, 16)

    perm[...] = (iota((512, 512), 1) == packed(iota((512, 512), 0))).astype(F32).astype(BF16)
    perm_t[...] = (iota((512, 512), 0) == packed(iota((512, 512), 1))).astype(F32).astype(BF16)

    def l_wait(k, carry):
        s = lax.rem(mine + k, 32)
        remote(l_out.at[0], l_in.at[s], l_ss.at[k], l_rs.at[s], sib).wait_recv()
        return carry

    lax.fori_loop(1, 32, l_wait, 0)
    l_f[...] = l_in[...].reshape(512, 128).astype(F32)
    for i in range(16):
        v = l_f[pl.ds(i, 32, stride=16), :]
        for x in range(4):
            part = v[x * 8:x * 8 + 8, :]
            l_all[x * 256 + i * 16:x * 256 + (i + 1) * 16, :] = jnp.concatenate(
                [part[:, 0:32], part[:, 64:96]], axis=0
            ).astype(BF16)
    l_t[...] = l_all[...].astype(F32).T.astype(BF16)

    def t_group(x_):
        r = mm(l_all[pl.ds(pl.multiple_of(x_ * 256, 256), 256), :], w[...]).astype(BF16)
        for d in range(32):
            t[x_, :, d] = r[:, d * 128:(d + 1) * 128].reshape(16, 16, 128)

    def d_group(x_, n):
        rows = jnp.concatenate([t[x_, i].reshape(512, 128) for i in range(16)], axis=1)
        raw = mm_nt(rows, g[...]).astype(BF16)
        d_buf[x_] = mm(perm_t[...], raw).astype(BF16).reshape(2, 256, 512)
        remote(d_buf.at[x_, other], c_in.at[x_], d_ss.at[n], d_rs.at[x_], sib).start()

    def c_wait(x_, n):
        remote(d_buf.at[x_, other], c_in.at[x_], d_ss.at[n], d_rs.at[x_], sib).wait_recv()

    def core_sum(x_):
        return d_buf[x_, core].astype(F32) + c_in[x_].astype(F32)

    def x_copy(x_, n, target_x):
        return remote(
            s1.at[x_], x_in.at[n], d_ss.at[4 + n], d_rs.at[4 + n], dev(zz, target_x, core)
        )

    t_group(xf)
    r_wait(slot(xx, core, zm))
    r_send(slot(xx, core, zm), dev(zs, xx, core), 5)
    for n, z_ in enumerate((zm, zs)):
        if n == 1:
            r_wait(slot(xx, core, z_))
        r_send(slot(xx, core, z_), dev(zz, xs, core), 6 + 3 * n)
        r_send(slot(xx, core, z_), dev(zz, xm, core), 7 + 3 * n)
        r_send(slot(xx, core, z_), sib, 8 + 3 * n)
    d_group(xf, 0)
    r_wait(slot(xm, core, zz))
    r_send(slot(xm, core, zz), dev(zz, xs, core), 15)
    r_send(slot(xm, core, zz), sib, 16)
    r_wait(slot(xs, core, zz))
    r_send(slot(xs, core, zz), sib, 17)
    t_group(xm)
    r_wait(slot(xx, core, zf))
    r_send(slot(xx, core, zf), dev(zz, xs, core), 12)
    r_send(slot(xx, core, zf), dev(zz, xm, core), 13)
    r_send(slot(xx, core, zf), sib, 14)
    d_group(xm, 1)
    c_wait(xf, 0)
    s1[xf] = core_sum(xf).astype(BF16)
    x_copy(xf, 0, xs).start()
    for n, z_ in enumerate((zm, zs)):
        r_wait(slot(xm, core, z_))
        r_send(slot(xm, core, z_), dev(zz, xs, core), 18 + 3 * n)
        r_send(slot(xm, core, z_), sib, 19 + 3 * n)
        r_wait(slot(xs, core, z_))
        r_send(slot(xs, core, z_), sib, 20 + 3 * n)
    t_group(xs)
    d_group(xs, 2)
    c_wait(xm, 1)
    s1[xm] = core_sum(xm).astype(BF16)
    x_copy(xm, 1, xm).start()
    r_wait(slot(xm, core, zf))
    r_send(slot(xm, core, zf), dev(zz, xs, core), 24)
    r_send(slot(xm, core, zf), sib, 25)
    r_wait(slot(xs, core, zf))
    r_send(slot(xs, core, zf), sib, 26)
    r_wait(slot(xf, core, zz))
    r_send(slot(xf, core, zz), sib, 27)
    t_group(xx)
    d_group(xx, 3)
    for n, z_ in enumerate((zm, zs, zf)):
        r_wait(slot(xf, core, z_))
        r_send(slot(xf, core, z_), sib, 28 + n)

    def r_prep(x_):
        for z_ in range(4):
            r_wait(slot(x_, other, z_))
        raw = r_buf[pl.ds(x_ * 8, 8)].reshape(512, 512)
        moved = mm(perm[...], raw)
        r_k[...] = moved.astype(BF16)
        r_j[:, pl.ds(pl.multiple_of(x_ * 512, 512), 512)] = moved.T.astype(BF16)

    def e_copy(s, k):
        return remote(lg_out.at[s], lg_in.at[me], e_ss.at[k], e_rs.at[me], slot_dev(s))

    def q_group(x_, n):
        for h in range(2):
            block = mm(r_k[...], g[:, h * 1024:(h + 1) * 1024]).astype(BF16)
            for i in range(8):
                q[x_, h * 8 + i] = block[:, i * 128:(i + 1) * 128].reshape(32, 16, 128)
        rows = jnp.concatenate([q[x_, :, d].reshape(256, 128) for d in range(32)], axis=1)
        lg_f[:, 0:32] = mm_nt(rows, w[...])
        for c in range(8):
            pieces = [lg_f[pl.ds(c + 8 * k, 16, stride=16), :][:, 0:32] for k in range(2)]
            pieces.append(jnp.zeros((16, 64), F32))
            lg_out[x_ * 8 + c] = jnp.concatenate(pieces, axis=1).astype(BF16)
        if n == 0:
            for k in range(1, 8):
                e_copy(x_ * 8 + lax.rem(core * 4 + zz + k, 8), k).start()
            lg_in[me] = lg_out[mine]
        else:
            for k in range(8):
                e_copy(x_ * 8 + k, n * 8 + k).start()

    def z_copy(k):
        z_ = lax.rem(zz + k, 4)
        return remote(
            s2.at[z_], z_in.at[zz], d_ss.at[6 + k], d_rs.at[7 + zz], dev(z_, xx, core)
        )

    r_prep(xx)
    c_wait(xs, 2)
    x_copy(xf, 0, xs).wait_recv()
    s1[xs] = (core_sum(xs) + x_in[0].astype(F32)).astype(BF16)
    x_copy(xs, 2, xs).start()
    q_group(xx, 0)
    r_prep(xm)
    q_group(xm, 1)
    c_wait(xx, 3)
    x_copy(xm, 1, xm).wait_recv()
    x_copy(xs, 2, xs).wait_recv()
    s2[...] = (
        core_sum(xx) + x_in[1].astype(F32) + x_in[2].astype(F32)
    ).astype(BF16).reshape(4, 64, 512)
    for k in range(1, 4):
        z_copy(k).start()
    r_prep(xs)
    q_group(xs, 2)
    r_prep(xf)
    q_group(xf, 3)

    rows_q = jnp.concatenate(
        [q[:, :, d].reshape(1024, 128) for d in range(32)], axis=1
    )
    rg_l[...] = mm(l_t[...], rows_q)
    for d in range(32):
        rg_f[pl.ds(d, 32, stride=32), :] = rg_l[:, d * 128:(d + 1) * 128]
    rg_b[...] = rg_f[...].astype(BF16).reshape(2, 512, 128)
    a0 = remote(rg_b.at[other], ra, a_ss.at[0], a_rs.at[0], sib)
    a0.start()

    def pair_copy(ib):
        return pltpu.make_async_copy(
            pair_v.at[pl.ds(ib * 4, 4)], pair_o.at[pl.ds(ib * 4, 4)], io.at[ib + 1]
        )

    def u_step(ib):
        cols = jnp.concatenate(
            [t[:, ib * 4 + ii].reshape(2048, 128) for ii in range(4)], axis=1
        )
        acc = mm(r_j[...], cols)
        for ii in range(4):
            pair_v[4 * ib + ii] = (
                (acc[:, ii * 128:(ii + 1) * 128] + biases[...]) * rec[4 * ib + ii]
            ).astype(BF16)
        pair_copy(ib).start()

    u_step(0)
    u_step(1)

    a0.wait_recv()
    rb[...] = (rg_b[core].astype(F32) + ra[...].astype(F32)).astype(BF16).reshape(4, 128, 128)

    def a_x(k):
        x_ = lax.rem(xx + k, 4)
        return remote(rb.at[x_], rc.at[xx], a_ss.at[k], a_rs.at[1 + xx], dev(zz, x_, core))

    for k in range(1, 4):
        a_x(k).start()
    rc[xx] = rb[xx]

    for k in range(1, 32):
        p = lax.rem(me + k, 32)
        remote(lg_out.at[0], lg_in.at[p], e_ss.at[k], e_rs.at[p], sib).wait_recv()
    for k in range(1, 4):
        z_ = lax.rem(zz + k, 4)
        remote(s2.at[z_], z_in.at[z_], d_ss.at[6 + k], d_rs.at[7 + z_], sib).wait_recv()
    z_in[zz] = s2[zz]
    right = (z_in[0].astype(F32) + z_in[1].astype(F32)) + (
        z_in[2].astype(F32) + z_in[3].astype(F32)
    )
    right_t = right.T
    left = lg_in[...].reshape(512, 128).astype(F32)
    for k in range(2):
        both[k * 512:(k + 1) * 512, :] = jnp.concatenate(
            [left[:, k * 32:(k + 1) * 32], right_t[:, k * 32:(k + 1) * 32]], axis=1
        ) * mcol[k * 512:(k + 1) * 512, :]
    pgb = both[...].astype(BF16)
    pj_acc = mm_tn(pgb, normed[...])
    of_acc = jnp.sum(pgb.astype(F32), axis=0, keepdims=True)
    ng_s[...] = mm(pgb, proj[...])
    sc_acc = jnp.sum(ng_s[...] * std[...], axis=0, keepdims=True)
    sh_acc = jnp.sum(ng_s[...], axis=0, keepdims=True)
    pb[0] = pj_acc[0:48].astype(BF16)
    pb[1] = jnp.concatenate(
        [
            pj_acc[48:64], sc_acc, sh_acc,
            jnp.concatenate([of_acc, jnp.zeros((1, 64), F32), bsum[...]], axis=1),
            jnp.zeros((29, 256), F32),
        ],
        axis=0,
    ).astype(BF16)
    b0 = remote(pb.at[other], pb_core, b_ss.at[0], b_rs.at[0], sib)
    b0.start()

    for k in range(1, 4):
        x_ = lax.rem(xx + k, 4)
        remote(rb.at[x_], rc.at[x_], a_ss.at[k], a_rs.at[1 + x_], sib).wait_recv()

    def four(ref):
        return (ref[0].astype(F32) + ref[1].astype(F32)) + (
            ref[2].astype(F32) + ref[3].astype(F32)
        )

    re[zz] = four(rc).astype(BF16)

    def a_z(k):
        z_ = lax.rem(zz + k, 4)
        return remote(re.at[zz], re.at[zz], a_ss.at[3 + k], a_rs.at[5 + zz], dev(z_, xx, core))

    for k in range(1, 4):
        a_z(k).start()

    b0.wait_recv()
    pb_x[xx] = (pb[core].astype(F32) + pb_core[...].astype(F32)).astype(BF16)

    def b_x(k):
        x_ = lax.rem(xx + k, 4)
        return remote(pb_x.at[xx], pb_x.at[xx], b_ss.at[k], b_rs.at[1 + xx], dev(zz, x_, core))

    for k in range(1, 4):
        b_x(k).start()

    for b in range(4):
        rows = slice(b * 256, (b + 1) * 256)
        h = ng_s[rows, :] * scales[...]
        standard = std[rows, :]
        m1 = jnp.mean(h, axis=-1, keepdims=True)
        m2 = jnp.mean(h * standard, axis=-1, keepdims=True)
        al_v[rows, :] = ((h - m1 - standard * m2) * inv[rows, :]).astype(BF16)
    al_copy = pltpu.make_async_copy(al_v, al_o, io.at[5])
    al_copy.start()
    u_step(2)

    for k in range(1, 4):
        z_ = lax.rem(zz + k, 4)
        remote(re.at[z_], re.at[z_], a_ss.at[3 + k], a_rs.at[5 + z_], sib).wait_recv()
    rh[xx] = four(re).astype(BF16)

    def a_g(k):
        x_ = lax.rem(xx + k, 4)
        return remote(rh.at[xx], rh.at[xx], a_ss.at[6 + k], a_rs.at[9 + xx], dev(zz, x_, core))

    for k in range(1, 4):
        a_g(k).start()

    for k in range(1, 4):
        x_ = lax.rem(xx + k, 4)
        remote(pb_x.at[x_], pb_x.at[x_], b_ss.at[k], b_rs.at[1 + x_], sib).wait_recv()
    pb_z[zz] = four(pb_x).astype(BF16)

    def b_z(k):
        z_ = lax.rem(zz + k, 4)
        return remote(
            pb_z.at[zz], pb_z.at[zz], b_ss.at[3 + k], b_rs.at[5 + zz], dev(z_, xx, core)
        )

    for k in range(1, 4):
        b_z(k).start()
    u_step(3)

    for k in range(1, 4):
        x_ = lax.rem(xx + k, 4)
        remote(rh.at[x_], rh.at[x_], a_ss.at[6 + k], a_rs.at[9 + x_], sib).wait_recv()
    a_last = remote(rh, rk, a_ss.at[10], a_rs.at[13], sib)
    a_last.start()
    rg_o[pl.ds(pl.multiple_of(core * 512, 512), 512), :] = rh[...].reshape(512, 128).astype(F32)

    for k in range(1, 4):
        z_ = lax.rem(zz + k, 4)
        remote(pb_z.at[z_], pb_z.at[z_], b_ss.at[3 + k], b_rs.at[5 + z_], sib).wait_recv()
    pb_half[core] = four(pb_z).astype(BF16)
    b_last = remote(pb_half.at[core], pb_half.at[core], b_ss.at[7], b_rs.at[9], sib)
    b_last.start()

    def drain(k, carry):
        remote(l_out.at[0], l_in.at[0], l_ss.at[k], l_rs.at[0], sib).wait_send()
        remote(lg_out.at[0], lg_in.at[0], e_ss.at[k], e_rs.at[0], sib).wait_send()
        remote(r_buf.at[0], r_buf.at[0], r_ss.at[k - 1], r_rs.at[0], sib).wait_send()
        return carry

    lax.fori_loop(1, 32, drain, 0)
    for n, x_ in enumerate((xf, xm, xs, xx)):
        remote(d_buf.at[x_, other], c_in.at[x_], d_ss.at[n], d_rs.at[x_], sib).wait_send()
    x_copy(xf, 0, xs).wait_send()
    x_copy(xm, 1, xm).wait_send()
    x_copy(xs, 2, xs).wait_send()
    a0.wait_send()
    b0.wait_send()
    for k in range(1, 4):
        z_copy(k).wait_send()
        a_x(k).wait_send()
        a_z(k).wait_send()
        a_g(k).wait_send()
        b_x(k).wait_send()
        b_z(k).wait_send()
    for ib in range(4):
        pair_copy(ib).wait()
    al_copy.wait()
    a_last.wait()
    rg_o[pl.ds(pl.multiple_of(other * 512, 512), 512), :] = rk[...].reshape(512, 128).astype(F32)
    remote(
        pb_half.at[other], pb_half.at[other], b_ss.at[7], b_rs.at[9], sib
    ).wait_recv()
    b_last.wait_send()
    pg_o[...] = jnp.concatenate([pb_half[0], pb_half[1, 0:16]], axis=0).astype(F32)
    vec = pb_half[1, 16:32].astype(F32)
    sg_o[...] = vec[0:1, :]
    hg_o[...] = vec[1:2, :]
    og_o[...] = vec[2:3, 0:64]
    bg_o[...] = vec[2:3, 128:256]


def finish(*refs):
    srcs, dsts, sems = refs[0:8], refs[8:16], refs[16]
    copies = [
        pltpu.make_async_copy(srcs[0].at[pl.ds(4 * n, 4)], dsts[0].at[pl.ds(4 * n, 4)], sems.at[n])
        for n in range(4)
    ]
    copies += [
        pltpu.make_async_copy(srcs[n], dsts[n], sems.at[3 + n]) for n in range(1, 8)
    ]
    for copy in copies:
        copy.start()
    for copy in copies:
        copy.wait()


def per_device(
    alignment, alignment_mask, cotangent, scales, shifts, projection, offsets, readout, biases
):
    vmem = pl.BlockSpec(memory_space=pltpu.VMEM)
    shape = jax.ShapeDtypeStruct
    sizes = dict(
        cot_v=((16, 512, 128), BF16),
        pair_v=((16, 512, 128), BF16),
        al_v=((1024, 256), BF16),
        mcol=((1024, 1), F32),
        std=((1024, 256), F32),
        inv=((1024, 1), F32),
        normed=((1024, 256), BF16),
        both=((1024, 64), F32),
        l_out=((32, 16, 128), BF16),
        l_in=((32, 16, 128), BF16),
        l_f=((512, 128), F32),
        l_all=((1024, 32), BF16),
        l_t=((32, 1024), BF16),
        w=((32, 4096), BF16),
        ro_f=((1024, 128), F32),
        rec=((16, 512, 128), F32),
        g=((512, 2048), BF16),
        perm=((512, 512), BF16),
        perm_t=((512, 512), BF16),
        r_buf=((32, 64, 512), BF16),
        r_k=((512, 512), BF16),
        r_j=((512, 2048), BF16),
        t=((4, 16, 32, 16, 128), BF16),
        q=((4, 16, 32, 16, 128), BF16),
        d_buf=((4, 2, 256, 512), BF16),
        c_in=((4, 256, 512), BF16),
        s1=((4, 256, 512), BF16),
        x_in=((3, 256, 512), BF16),
        s2=((4, 64, 512), BF16),
        z_in=((4, 64, 512), BF16),
        lg_f=((256, 128), F32),
        lg_out=((32, 16, 128), BF16),
        lg_in=((32, 16, 128), BF16),
        rg_l=((32, 4096), F32),
        rg_f=((1024, 128), F32),
        rg_b=((2, 512, 128), BF16),
        ra=((512, 128), BF16),
        rb=((4, 128, 128), BF16),
        rc=((4, 128, 128), BF16),
        re=((4, 128, 128), BF16),
        rh=((4, 128, 128), BF16),
        rk=((4, 128, 128), BF16),
        ng_s=((1024, 256), F32),
        pb=((2, 48, 256), BF16),
        pb_core=((48, 256), BF16),
        pb_x=((4, 48, 256), BF16),
        pb_z=((4, 48, 256), BF16),
        pb_half=((2, 48, 256), BF16),
        bsum=((1, 128), F32),
    )
    scratch = [pltpu.VMEM(*size) for size in sizes.values()] + [
        pltpu.SemaphoreType.DMA((n,)) for n in (32, 32, 32, 32, 31, 32, 10, 11, 11, 14, 8, 10, 6)
    ]
    anywhere = pl.BlockSpec(memory_space=pl.ANY)
    outs = pl.pallas_call(
        kernel,
        out_shape=(
            shape((16, 512, 128), BF16),
            shape((1024, 256), BF16),
            shape((64, 256), F32),
            shape((1, 64), F32),
            shape((1024, 128), F32),
            shape((1, 128), F32),
            shape((1, 256), F32),
            shape((1, 256), F32),
        ),
        in_specs=[vmem] * 2 + [anywhere] + [vmem] * 6,
        out_specs=[anywhere] * 2 + [vmem] * 6,
        scratch_shapes=scratch,
        compiler_params=pltpu.CompilerParams(
            collective_id=0, has_side_effects=True, vmem_limit_bytes=62 * 1024 * 1024
        ),
        cost_estimate=pl.CostEstimate(
            flops=16_000_000_000, bytes_accessed=6_000_000, transcendentals=0
        ),
        name="outer_product_mean",
    )(
        alignment.reshape(1024, 256),
        alignment_mask,
        cotangent,
        scales.reshape(1, 256),
        shifts.reshape(1, 256),
        projection.T,
        offsets.reshape(1, 64),
        readout,
        biases.reshape(1, 128),
    )
    outs = pl.pallas_call(
        finish,
        out_shape=tuple(shape(out.shape, out.dtype) for out in outs),
        in_specs=[anywhere] * 8,
        out_specs=[anywhere] * 8,
        scratch_shapes=[pltpu.SemaphoreType.DMA((11,))],
        name="results",
    )(*outs)
    return (
        outs[0],
        outs[1].reshape(2, 512, 256),
        outs[2].T,
        outs[3].reshape(64),
        outs[4],
        outs[5].reshape(128),
        outs[6].reshape(256),
        outs[7].reshape(256),
    )


def solution(mesh):
    return jax.shard_map(
        per_device,
        mesh=mesh,
        in_specs=(
            P(("crop", "dap"), None, None),
            P("crop", None),
            P(("crop", "dap"), None, None),
            P(),
            P(),
            P(),
            P(),
            P(),
            P(),
        ),
        out_specs=(
            P(("crop", "dap"), None, None),
            P(("crop", "dap"), None, None),
            P("crop", None),
            P("crop"),
            P("crop", None),
            P("crop"),
            P("crop"),
            P("crop"),
        ),
        check_vma=False,
    )
```

```python
import jax
import jax.numpy as jnp
from jax import lax
from jax.experimental import pallas as pl
from jax.experimental.pallas import tpu as pltpu
from jax.sharding import PartitionSpec as P

F32 = jnp.float32
BF16 = jnp.bfloat16
MESH = pl.DeviceIdType.MESH


def mm(a, b):
    return lax.dot_general(a, b, (((1,), (0,)), ((), ())), preferred_element_type=F32)


def mm_nt(a, b):
    return lax.dot_general(a, b, (((1,), (1,)), ((), ())), preferred_element_type=F32)


def mm_tn(a, b):
    return lax.dot_general(a, b, (((0,), (0,)), ((), ())), preferred_element_type=F32)


def iota(shape, dim):
    return lax.broadcasted_iota(jnp.int32, shape, dim)


def kernel(
    al, mask, cot, scales, shifts, proj, offs, readout, biases,
    pair_o, al_o, pg_o, og_o, rg_o, bg_o, sg_o, hg_o,
    cot_v, pair_v, al_v, mcol, std, inv, normed, both, l_out, l_in, l_f, l_all, l_t, w, ro_f,
    rec, g, perm, perm_t, r_buf, r_k, r_j, t, q,
    d_buf, c_in, s1, x_in, s2, z_in,
    lg_f, lg_out, lg_in, rg_l, rg_f, rg_b, ra, rb, rc, re, rh, rk,
    ng_s, pb, pb_core, pb_x, pb_z, pb_half, bsum,
    l_ss, l_rs, e_ss, e_rs, r_ss, r_rs, d_ss, d_rs, a_ss, a_rs, b_ss, b_rs, io,
):
    me = lax.axis_index("dap")
    core = lax.rem(me, 2)
    xx = lax.rem(lax.div(me, 2), 4)
    zz = lax.div(me, 8)
    sign = 1 - 2 * core
    xs, xm, xf = (lax.rem(xx + 4 + sign, 4), lax.rem(xx + 4 - sign, 4), lax.rem(xx + 2, 4))
    zs, zm, zf = (lax.rem(zz + 4 + sign, 4), lax.rem(zz + 4 - sign, 4), lax.rem(zz + 2, 4))
    other = 1 - core

    def dev(z, x, c):
        return (z * 4 + x) * 2 + c

    def slot(x, c, z):
        return (x * 2 + c) * 4 + z

    def slot_dev(s):
        return dev(lax.rem(s, 4), lax.div(s, 8), lax.rem(lax.div(s, 4), 2))

    sib = dev(zz, xx, other)
    mine = slot(xx, core, zz)

    def remote(src, dst, ss, rs, target):
        return pltpu.make_async_remote_copy(
            src_ref=src, dst_ref=dst, send_sem=ss, recv_sem=rs,
            device_id={"dap": target}, device_id_type=MESH,
        )

    barrier = pltpu.get_barrier_semaphore()

    def greet(k, carry):
        pl.semaphore_signal(
            barrier, inc=1, device_id={"dap": lax.rem(me + k, 32)}, device_id_type=MESH
        )
        return carry

    lax.fori_loop(1, 32, greet, 0)
    cot_copy = pltpu.make_async_copy(cot, cot_v, io.at[0])
    cot_copy.start()

    mask_f = mask[...].astype(F32)
    mask_t = mask_f.T
    for k in range(2):
        mcol[k * 512:(k + 1) * 512, :] = jnp.sum(
            jnp.where(iota((512, 64), 1) == 2 * me + k, mask_t, 0.0), axis=1, keepdims=True
        )
    for k in range(2):
        rows = slice(k * 512, (k + 1) * 512)
        wide = al[rows, :].astype(F32)
        center = jnp.mean(wide, axis=-1, keepdims=True)
        apart = wide - center
        spread = jnp.mean(apart * apart, axis=-1, keepdims=True)
        inverse = lax.rsqrt(spread + 1e-05)
        standard = apart * inverse
        std[rows, :] = standard
        inv[rows, :] = inverse
        normed[rows, :] = (standard * scales[...] + shifts[...]).astype(BF16)
    both[...] = (mm_nt(normed[...], proj[...]) + offs[...]) * mcol[...]
    cat = jnp.concatenate([both[0:512, :], both[512:1024, :]], axis=1)
    l_out[...] = cat.astype(BF16).reshape(32, 16, 128)
    cat_t = cat.T
    r_buf[mine] = jnp.concatenate([cat_t[32:64], cat_t[96:128]], axis=0).astype(BF16)

    pl.semaphore_wait(barrier, 31)

    def l_send(k, carry):
        s = lax.rem(mine + k, 32)
        p = slot_dev(s)
        remote(l_out.at[p], l_in.at[mine], l_ss.at[k], l_rs.at[mine], p).start()
        return carry

    lax.fori_loop(1, 32, l_send, 0)

    def r_send(s, target, k):
        remote(r_buf.at[s], r_buf.at[s], r_ss.at[k], r_rs.at[s], target).start()

    def r_wait(s):
        remote(r_buf.at[s], r_buf.at[s], r_ss.at[0], r_rs.at[s], sib).wait_recv()

    r_send(mine, dev(zs, xx, core), 0)
    r_send(mine, dev(zm, xx, core), 1)
    r_send(mine, dev(zz, xs, core), 2)
    r_send(mine, dev(zz, xm, core), 3)
    r_send(mine, sib, 4)
    l_in[mine] = l_out[me]

    mask_b = mask_f.astype(BF16)
    own_cols = (iota((512, 16), 0) == 16 * me + iota((512, 16), 1)).astype(F32).astype(BF16)
    mask_own = mm(mask_b, own_cols).astype(BF16)
    recip = 1.0 / (0.001 + mm(mask_t.astype(BF16), mask_own))
    total = jnp.zeros((1, 128), F32)
    cot_copy.wait()
    for i in range(16):
        rec_i = jnp.broadcast_to(recip[:, i:i + 1], (512, 128))
        rec[i] = rec_i
        sg = (cot_v[i].astype(F32) * rec_i).astype(BF16)
        g[:, i * 128:(i + 1) * 128] = sg
        total = total + jnp.sum(sg.astype(F32), axis=0, keepdims=True)
    bsum[...] = total

    ro_f[...] = readout[...].astype(F32)
    for d in range(32):
        w[:, d * 128:(d + 1) * 128] = ro_f[pl.ds(d, 32, stride=32), :].astype(BF16)

    def packed(a):
        return lax.rem(a, 8) * 64 + lax.rem(lax.div(a, 8), 2) * 32 + lax.div(a, 16)

    perm[...] = (iota((512, 512), 1) == packed(iota((512, 512), 0))).astype(F32).astype(BF16)
    perm_t[...] = (iota((512, 512), 0) == packed(iota((512, 512), 1))).astype(F32).astype(BF16)

    def l_wait(k, carry):
        s = lax.rem(mine + k, 32)
        remote(l_out.at[0], l_in.at[s], l_ss.at[k], l_rs.at[s], sib).wait_recv()
        return carry

    lax.fori_loop(1, 32, l_wait, 0)
    l_f[...] = l_in[...].reshape(512, 128).astype(F32)
    for i in range(16):
        v = l_f[pl.ds(i, 32, stride=16), :]
        for x in range(4):
            part = v[x * 8:x * 8 + 8, :]
            l_all[x * 256 + i * 16:x * 256 + (i + 1) * 16, :] = jnp.concatenate(
                [part[:, 0:32], part[:, 64:96]], axis=0
            ).astype(BF16)
    l_t[...] = l_all[...].astype(F32).T.astype(BF16)

    def t_group(x_):
        r = mm(l_all[pl.ds(pl.multiple_of(x_ * 256, 256), 256), :], w[...]).astype(BF16)
        for d in range(32):
            t[x_, :, d] = r[:, d * 128:(d + 1) * 128].reshape(16, 16, 128)

    def d_group(x_, n):
        rows = jnp.concatenate([t[x_, i].reshape(512, 128) for i in range(16)], axis=1)
        raw = mm_nt(rows, g[...]).astype(BF16)
        d_buf[x_] = mm(perm_t[...], raw).astype(BF16).reshape(2, 256, 512)
        remote(d_buf.at[x_, other], c_in.at[x_], d_ss.at[n], d_rs.at[x_], sib).start()

    def c_wait(x_, n):
        remote(d_buf.at[x_, other], c_in.at[x_], d_ss.at[n], d_rs.at[x_], sib).wait_recv()

    def core_sum(x_):
        return d_buf[x_, core].astype(F32) + c_in[x_].astype(F32)

    def x_copy(x_, n, target_x):
        return remote(
            s1.at[x_], x_in.at[n], d_ss.at[4 + n], d_rs.at[4 + n], dev(zz, target_x, core)
        )

    t_group(xf)
    r_wait(slot(xx, core, zm))
    r_send(slot(xx, core, zm), dev(zs, xx, core), 5)
    for n, z_ in enumerate((zm, zs)):
        if n == 1:
            r_wait(slot(xx, core, z_))
        r_send(slot(xx, core, z_), dev(zz, xs, core), 6 + 3 * n)
        r_send(slot(xx, core, z_), dev(zz, xm, core), 7 + 3 * n)
        r_send(slot(xx, core, z_), sib, 8 + 3 * n)
    d_group(xf, 0)
    r_wait(slot(xm, core, zz))
    r_send(slot(xm, core, zz), dev(zz, xs, core), 15)
    r_send(slot(xm, core, zz), sib, 16)
    r_wait(slot(xs, core, zz))
    r_send(slot(xs, core, zz), sib, 17)
    t_group(xm)
    r_wait(slot(xx, core, zf))
    r_send(slot(xx, core, zf), dev(zz, xs, core), 12)
    r_send(slot(xx, core, zf), dev(zz, xm, core), 13)
    r_send(slot(xx, core, zf), sib, 14)
    d_group(xm, 1)
    c_wait(xf, 0)
    s1[xf] = core_sum(xf).astype(BF16)
    x_copy(xf, 0, xs).start()
    for n, z_ in enumerate((zm, zs)):
        r_wait(slot(xm, core, z_))
        r_send(slot(xm, core, z_), dev(zz, xs, core), 18 + 3 * n)
        r_send(slot(xm, core, z_), sib, 19 + 3 * n)
        r_wait(slot(xs, core, z_))
        r_send(slot(xs, core, z_), sib, 20 + 3 * n)
    t_group(xs)
    d_group(xs, 2)
    c_wait(xm, 1)
    s1[xm] = core_sum(xm).astype(BF16)
    x_copy(xm, 1, xm).start()
    r_wait(slot(xm, core, zf))
    r_send(slot(xm, core, zf), dev(zz, xs, core), 24)
    r_send(slot(xm, core, zf), sib, 25)
    r_wait(slot(xs, core, zf))
    r_send(slot(xs, core, zf), sib, 26)
    r_wait(slot(xf, core, zz))
    r_send(slot(xf, core, zz), sib, 27)
    t_group(xx)
    d_group(xx, 3)
    for n, z_ in enumerate((zm, zs, zf)):
        r_wait(slot(xf, core, z_))
        r_send(slot(xf, core, z_), sib, 28 + n)

    def r_prep(x_):
        for z_ in range(4):
            r_wait(slot(x_, other, z_))
        raw = r_buf[pl.ds(x_ * 8, 8)].reshape(512, 512)
        moved = mm(perm[...], raw)
        r_k[...] = moved.astype(BF16)
        r_j[:, pl.ds(pl.multiple_of(x_ * 512, 512), 512)] = moved.T.astype(BF16)

    def e_copy(s, k):
        return remote(lg_out.at[s], lg_in.at[me], e_ss.at[k], e_rs.at[me], slot_dev(s))

    def q_group(x_, n):
        for h in range(2):
            block = mm(r_k[...], g[:, h * 1024:(h + 1) * 1024]).astype(BF16)
            for i in range(8):
                q[x_, h * 8 + i] = block[:, i * 128:(i + 1) * 128].reshape(32, 16, 128)
        rows = jnp.concatenate([q[x_, :, d].reshape(256, 128) for d in range(32)], axis=1)
        lg_f[:, 0:32] = mm_nt(rows, w[...])
        for c in range(8):
            pieces = [lg_f[pl.ds(c + 8 * k, 16, stride=16), :][:, 0:32] for k in range(2)]
            pieces.append(jnp.zeros((16, 64), F32))
            lg_out[x_ * 8 + c] = jnp.concatenate(pieces, axis=1).astype(BF16)
        if n == 0:
            for k in range(1, 8):
                e_copy(x_ * 8 + lax.rem(core * 4 + zz + k, 8), k).start()
            lg_in[me] = lg_out[mine]
        else:
            for k in range(8):
                e_copy(x_ * 8 + k, n * 8 + k).start()

    def z_copy(k):
        z_ = lax.rem(zz + k, 4)
        return remote(
            s2.at[z_], z_in.at[zz], d_ss.at[6 + k], d_rs.at[7 + zz], dev(z_, xx, core)
        )

    r_prep(xx)
    c_wait(xs, 2)
    x_copy(xf, 0, xs).wait_recv()
    s1[xs] = (core_sum(xs) + x_in[0].astype(F32)).astype(BF16)
    x_copy(xs, 2, xs).start()
    q_group(xx, 0)
    r_prep(xm)
    q_group(xm, 1)
    c_wait(xx, 3)
    x_copy(xm, 1, xm).wait_recv()
    x_copy(xs, 2, xs).wait_recv()
    s2[...] = (
        core_sum(xx) + x_in[1].astype(F32) + x_in[2].astype(F32)
    ).astype(BF16).reshape(4, 64, 512)
    for k in range(1, 4):
        z_copy(k).start()
    r_prep(xs)
    q_group(xs, 2)
    r_prep(xf)
    q_group(xf, 3)

    rows_q = jnp.concatenate(
        [q[:, :, d].reshape(1024, 128) for d in range(32)], axis=1
    )
    rg_l[...] = mm(l_t[...], rows_q)
    for d in range(32):
        rg_f[pl.ds(d, 32, stride=32), :] = rg_l[:, d * 128:(d + 1) * 128]
    rg_b[...] = rg_f[...].astype(BF16).reshape(2, 512, 128)
    a0 = remote(rg_b.at[other], ra, a_ss.at[0], a_rs.at[0], sib)
    a0.start()

    def pair_copy(ib):
        return pltpu.make_async_copy(
            pair_v.at[pl.ds(ib * 4, 4)], pair_o.at[pl.ds(ib * 4, 4)], io.at[ib + 1]
        )

    def u_step(ib):
        cols = jnp.concatenate(
            [t[:, ib * 4 + ii].reshape(2048, 128) for ii in range(4)], axis=1
        )
        acc = mm(r_j[...], cols)
        for ii in range(4):
            pair_v[4 * ib + ii] = (
                (acc[:, ii * 128:(ii + 1) * 128] + biases[...]) * rec[4 * ib + ii]
            ).astype(BF16)
        pair_copy(ib).start()

    u_step(0)
    u_step(1)

    a0.wait_recv()
    rb[...] = (rg_b[core].astype(F32) + ra[...].astype(F32)).astype(BF16).reshape(4, 128, 128)

    def a_x(k):
        x_ = lax.rem(xx + k, 4)
        return remote(rb.at[x_], rc.at[xx], a_ss.at[k], a_rs.at[1 + xx], dev(zz, x_, core))

    for k in range(1, 4):
        a_x(k).start()
    rc[xx] = rb[xx]

    for k in range(1, 32):
        p = lax.rem(me + k, 32)
        remote(lg_out.at[0], lg_in.at[p], e_ss.at[k], e_rs.at[p], sib).wait_recv()
    for k in range(1, 4):
        z_ = lax.rem(zz + k, 4)
        remote(s2.at[z_], z_in.at[z_], d_ss.at[6 + k], d_rs.at[7 + z_], sib).wait_recv()
    z_in[zz] = s2[zz]
    right = (z_in[0].astype(F32) + z_in[1].astype(F32)) + (
        z_in[2].astype(F32) + z_in[3].astype(F32)
    )
    right_t = right.T
    left = lg_in[...].reshape(512, 128).astype(F32)
    for k in range(2):
        both[k * 512:(k + 1) * 512, :] = jnp.concatenate(
            [left[:, k * 32:(k + 1) * 32], right_t[:, k * 32:(k + 1) * 32]], axis=1
        ) * mcol[k * 512:(k + 1) * 512, :]
    pgb = both[...].astype(BF16)
    pj_acc = mm_tn(pgb, normed[...])
    of_acc = jnp.sum(pgb.astype(F32), axis=0, keepdims=True)
    ng_s[...] = mm(pgb, proj[...])
    sc_acc = jnp.sum(ng_s[...] * std[...], axis=0, keepdims=True)
    sh_acc = jnp.sum(ng_s[...], axis=0, keepdims=True)
    pb[0] = pj_acc[0:48].astype(BF16)
    pb[1] = jnp.concatenate(
        [
            pj_acc[48:64], sc_acc, sh_acc,
            jnp.concatenate([of_acc, jnp.zeros((1, 64), F32), bsum[...]], axis=1),
            jnp.zeros((29, 256), F32),
        ],
        axis=0,
    ).astype(BF16)
    b0 = remote(pb.at[other], pb_core, b_ss.at[0], b_rs.at[0], sib)
    b0.start()

    for k in range(1, 4):
        x_ = lax.rem(xx + k, 4)
        remote(rb.at[x_], rc.at[x_], a_ss.at[k], a_rs.at[1 + x_], sib).wait_recv()

    def four(ref):
        return (ref[0].astype(F32) + ref[1].astype(F32)) + (
            ref[2].astype(F32) + ref[3].astype(F32)
        )

    re[zz] = four(rc).astype(BF16)

    def a_z(k):
        z_ = lax.rem(zz + k, 4)
        return remote(re.at[zz], re.at[zz], a_ss.at[3 + k], a_rs.at[5 + zz], dev(z_, xx, core))

    for k in range(1, 4):
        a_z(k).start()

    b0.wait_recv()
    pb_x[xx] = (pb[core].astype(F32) + pb_core[...].astype(F32)).astype(BF16)

    def b_x(k):
        x_ = lax.rem(xx + k, 4)
        return remote(pb_x.at[xx], pb_x.at[xx], b_ss.at[k], b_rs.at[1 + xx], dev(zz, x_, core))

    for k in range(1, 4):
        b_x(k).start()

    for b in range(4):
        rows = slice(b * 256, (b + 1) * 256)
        h = ng_s[rows, :] * scales[...]
        standard = std[rows, :]
        m1 = jnp.mean(h, axis=-1, keepdims=True)
        m2 = jnp.mean(h * standard, axis=-1, keepdims=True)
        al_v[rows, :] = ((h - m1 - standard * m2) * inv[rows, :]).astype(BF16)
    al_copy = pltpu.make_async_copy(al_v, al_o, io.at[5])
    al_copy.start()
    u_step(2)

    for k in range(1, 4):
        z_ = lax.rem(zz + k, 4)
        remote(re.at[z_], re.at[z_], a_ss.at[3 + k], a_rs.at[5 + z_], sib).wait_recv()
    rh[xx] = four(re).astype(BF16)

    def a_g(k):
        x_ = lax.rem(xx + k, 4)
        return remote(rh.at[xx], rh.at[xx], a_ss.at[6 + k], a_rs.at[9 + xx], dev(zz, x_, core))

    for k in range(1, 4):
        a_g(k).start()

    for k in range(1, 4):
        x_ = lax.rem(xx + k, 4)
        remote(pb_x.at[x_], pb_x.at[x_], b_ss.at[k], b_rs.at[1 + x_], sib).wait_recv()
    pb_z[zz] = four(pb_x).astype(BF16)

    def b_z(k):
        z_ = lax.rem(zz + k, 4)
        return remote(
            pb_z.at[zz], pb_z.at[zz], b_ss.at[3 + k], b_rs.at[5 + zz], dev(z_, xx, core)
        )

    for k in range(1, 4):
        b_z(k).start()
    u_step(3)

    for k in range(1, 4):
        x_ = lax.rem(xx + k, 4)
        remote(rh.at[x_], rh.at[x_], a_ss.at[6 + k], a_rs.at[9 + x_], sib).wait_recv()
    a_last = remote(rh, rk, a_ss.at[10], a_rs.at[13], sib)
    a_last.start()
    rg_o[pl.ds(pl.multiple_of(core * 512, 512), 512), :] = rh[...].reshape(512, 128).astype(F32)

    for k in range(1, 4):
        z_ = lax.rem(zz + k, 4)
        remote(pb_z.at[z_], pb_z.at[z_], b_ss.at[3 + k], b_rs.at[5 + z_], sib).wait_recv()
    pb_half[core] = four(pb_z).astype(BF16)
    b_last = remote(pb_half.at[core], pb_half.at[core], b_ss.at[7], b_rs.at[9], sib)
    b_last.start()

    def drain(k, carry):
        remote(l_out.at[0], l_in.at[0], l_ss.at[k], l_rs.at[0], sib).wait_send()
        remote(lg_out.at[0], lg_in.at[0], e_ss.at[k], e_rs.at[0], sib).wait_send()
        remote(r_buf.at[0], r_buf.at[0], r_ss.at[k - 1], r_rs.at[0], sib).wait_send()
        return carry

    lax.fori_loop(1, 32, drain, 0)
    for n, x_ in enumerate((xf, xm, xs, xx)):
        remote(d_buf.at[x_, other], c_in.at[x_], d_ss.at[n], d_rs.at[x_], sib).wait_send()
    x_copy(xf, 0, xs).wait_send()
    x_copy(xm, 1, xm).wait_send()
    x_copy(xs, 2, xs).wait_send()
    a0.wait_send()
    b0.wait_send()
    for k in range(1, 4):
        z_copy(k).wait_send()
        a_x(k).wait_send()
        a_z(k).wait_send()
        a_g(k).wait_send()
        b_x(k).wait_send()
        b_z(k).wait_send()
    for ib in range(4):
        pair_copy(ib).wait()
    al_copy.wait()
    a_last.wait()
    rg_o[pl.ds(pl.multiple_of(other * 512, 512), 512), :] = rk[...].reshape(512, 128).astype(F32)
    remote(
        pb_half.at[other], pb_half.at[other], b_ss.at[7], b_rs.at[9], sib
    ).wait_recv()
    b_last.wait_send()
    pg_o[...] = jnp.concatenate([pb_half[0], pb_half[1, 0:16]], axis=0).astype(F32)
    vec = pb_half[1, 16:32].astype(F32)
    sg_o[...] = vec[0:1, :]
    hg_o[...] = vec[1:2, :]
    og_o[...] = vec[2:3, 0:64]
    bg_o[...] = vec[2:3, 128:256]


def finish(*refs):
    srcs, dsts, held, arrive, leave = refs[0:8], refs[8:16], refs[16:24], refs[24], refs[25]
    parts = [tuple(r[0].at[pl.ds(4 * n, 4)] for r in (srcs, held, dsts)) for n in range(4)]
    parts += [(srcs[n], held[n], dsts[n]) for n in range(1, 8)]
    fetches = [pltpu.make_async_copy(p[0], p[1], arrive.at[n]) for n, p in enumerate(parts)]
    stores = [pltpu.make_async_copy(p[1], p[2], leave.at[n]) for n, p in enumerate(parts)]
    for fetch in fetches:
        fetch.start()
    for fetch, store in zip(fetches, stores):
        fetch.wait()
        store.start()
    for store in stores:
        store.wait()


def per_device(
    alignment, alignment_mask, cotangent, scales, shifts, projection, offsets, readout, biases
):
    vmem = pl.BlockSpec(memory_space=pltpu.VMEM)
    shape = jax.ShapeDtypeStruct
    sizes = dict(
        cot_v=((16, 512, 128), BF16),
        pair_v=((16, 512, 128), BF16),
        al_v=((1024, 256), BF16),
        mcol=((1024, 1), F32),
        std=((1024, 256), F32),
        inv=((1024, 1), F32),
        normed=((1024, 256), BF16),
        both=((1024, 64), F32),
        l_out=((32, 16, 128), BF16),
        l_in=((32, 16, 128), BF16),
        l_f=((512, 128), F32),
        l_all=((1024, 32), BF16),
        l_t=((32, 1024), BF16),
        w=((32, 4096), BF16),
        ro_f=((1024, 128), F32),
        rec=((16, 512, 128), F32),
        g=((512, 2048), BF16),
        perm=((512, 512), BF16),
        perm_t=((512, 512), BF16),
        r_buf=((32, 64, 512), BF16),
        r_k=((512, 512), BF16),
        r_j=((512, 2048), BF16),
        t=((4, 16, 32, 16, 128), BF16),
        q=((4, 16, 32, 16, 128), BF16),
        d_buf=((4, 2, 256, 512), BF16),
        c_in=((4, 256, 512), BF16),
        s1=((4, 256, 512), BF16),
        x_in=((3, 256, 512), BF16),
        s2=((4, 64, 512), BF16),
        z_in=((4, 64, 512), BF16),
        lg_f=((256, 128), F32),
        lg_out=((32, 16, 128), BF16),
        lg_in=((32, 16, 128), BF16),
        rg_l=((32, 4096), F32),
        rg_f=((1024, 128), F32),
        rg_b=((2, 512, 128), BF16),
        ra=((512, 128), BF16),
        rb=((4, 128, 128), BF16),
        rc=((4, 128, 128), BF16),
        re=((4, 128, 128), BF16),
        rh=((4, 128, 128), BF16),
        rk=((4, 128, 128), BF16),
        ng_s=((1024, 256), F32),
        pb=((2, 48, 256), BF16),
        pb_core=((48, 256), BF16),
        pb_x=((4, 48, 256), BF16),
        pb_z=((4, 48, 256), BF16),
        pb_half=((2, 48, 256), BF16),
        bsum=((1, 128), F32),
    )
    scratch = [pltpu.VMEM(*size) for size in sizes.values()] + [
        pltpu.SemaphoreType.DMA((n,)) for n in (32, 32, 32, 32, 31, 32, 10, 11, 11, 14, 8, 10, 6)
    ]
    anywhere = pl.BlockSpec(memory_space=pl.ANY)
    outs = pl.pallas_call(
        kernel,
        out_shape=(
            shape((16, 512, 128), BF16),
            shape((1024, 256), BF16),
            shape((64, 256), F32),
            shape((1, 64), F32),
            shape((1024, 128), F32),
            shape((1, 128), F32),
            shape((1, 256), F32),
            shape((1, 256), F32),
        ),
        in_specs=[vmem] * 2 + [anywhere] + [vmem] * 6,
        out_specs=[anywhere] * 2 + [vmem] * 6,
        scratch_shapes=scratch,
        compiler_params=pltpu.CompilerParams(
            collective_id=0, has_side_effects=True, vmem_limit_bytes=62 * 1024 * 1024
        ),
        cost_estimate=pl.CostEstimate(
            flops=16_000_000_000, bytes_accessed=6_000_000, transcendentals=0
        ),
        name="outer_product_mean",
    )(
        alignment.reshape(1024, 256),
        alignment_mask,
        cotangent,
        scales.reshape(1, 256),
        shifts.reshape(1, 256),
        projection.T,
        offsets.reshape(1, 64),
        readout,
        biases.reshape(1, 128),
    )
    outs = pl.pallas_call(
        finish,
        out_shape=tuple(shape(out.shape, out.dtype) for out in outs),
        in_specs=[anywhere] * 8,
        out_specs=[anywhere] * 8,
        scratch_shapes=[pltpu.VMEM(out.shape, out.dtype) for out in outs]
        + [pltpu.SemaphoreType.DMA((11,))] * 2,
        name="results",
    )(*outs)
    return (
        outs[0],
        outs[1].reshape(2, 512, 256),
        outs[2].T,
        outs[3].reshape(64),
        outs[4],
        outs[5].reshape(128),
        outs[6].reshape(256),
        outs[7].reshape(256),
    )


def solution(mesh):
    return jax.shard_map(
        per_device,
        mesh=mesh,
        in_specs=(
            P(("crop", "dap"), None, None),
            P("crop", None),
            P(("crop", "dap"), None, None),
            P(),
            P(),
            P(),
            P(),
            P(),
            P(),
        ),
        out_specs=(
            P(("crop", "dap"), None, None),
            P(("crop", "dap"), None, None),
            P("crop", None),
            P("crop"),
            P("crop", None),
            P("crop"),
            P("crop"),
            P("crop"),
        ),
        check_vma=False,
    )
```

```python
import jax
import jax.numpy as jnp
from jax import lax
from jax.experimental import pallas as pl
from jax.experimental.pallas import tpu as pltpu
from jax.sharding import PartitionSpec as P

F32 = jnp.float32
BF16 = jnp.bfloat16
MESH = pl.DeviceIdType.MESH


def mm(a, b):
    return lax.dot_general(a, b, (((1,), (0,)), ((), ())), preferred_element_type=F32)


def mm_nt(a, b):
    return lax.dot_general(a, b, (((1,), (1,)), ((), ())), preferred_element_type=F32)


def mm_tn(a, b):
    return lax.dot_general(a, b, (((0,), (0,)), ((), ())), preferred_element_type=F32)


def iota(shape, dim):
    return lax.broadcasted_iota(jnp.int32, shape, dim)


def kernel(
    al_h, mask_h, cot, scales, shifts, proj, offs, readout_h, biases,
    pair_v, al_v, pg_o, og_o, rg_o, bg_o, sg_o, hg_o,
    al, mask, readout, cot_v, mcol, std, inv, normed, both, l_out, l_in, l_f, l_all, l_t, w, ro_f,
    rec, g, perm, perm_t, r_buf, r_k, r_j, t, q,
    d_buf, c_in, s1, x_in, s2, z_in,
    lg_f, lg_out, lg_in, rg_l, rg_f, rg_b, ra, rb, rc, re, rh, rk,
    ng_s, pb, pb_core, pb_x, pb_z, pb_half, bsum,
    l_ss, l_rs, e_ss, e_rs, r_ss, r_rs, d_ss, d_rs, a_ss, a_rs, b_ss, b_rs, io,
):
    me = lax.axis_index("dap")
    core = lax.rem(me, 2)
    xx = lax.rem(lax.div(me, 2), 4)
    zz = lax.div(me, 8)
    sign = 1 - 2 * core
    xs, xm, xf = (lax.rem(xx + 4 + sign, 4), lax.rem(xx + 4 - sign, 4), lax.rem(xx + 2, 4))
    zs, zm, zf = (lax.rem(zz + 4 + sign, 4), lax.rem(zz + 4 - sign, 4), lax.rem(zz + 2, 4))
    other = 1 - core

    def dev(z, x, c):
        return (z * 4 + x) * 2 + c

    def slot(x, c, z):
        return (x * 2 + c) * 4 + z

    def slot_dev(s):
        return dev(lax.rem(s, 4), lax.div(s, 8), lax.rem(lax.div(s, 4), 2))

    sib = dev(zz, xx, other)
    mine = slot(xx, core, zz)

    def remote(src, dst, ss, rs, target):
        return pltpu.make_async_remote_copy(
            src_ref=src, dst_ref=dst, send_sem=ss, recv_sem=rs,
            device_id={"dap": target}, device_id_type=MESH,
        )

    barrier = pltpu.get_barrier_semaphore()

    def greet(k, carry):
        pl.semaphore_signal(
            barrier, inc=1, device_id={"dap": lax.rem(me + k, 32)}, device_id_type=MESH
        )
        return carry

    lax.fori_loop(1, 32, greet, 0)
    al_copy = pltpu.make_async_copy(al_h, al, io.at[0])
    mask_copy = pltpu.make_async_copy(mask_h, mask, io.at[1])
    readout_copy = pltpu.make_async_copy(readout_h, readout, io.at[2])
    cot_copy = pltpu.make_async_copy(cot, cot_v, io.at[3])
    for copy in (mask_copy, al_copy, cot_copy, readout_copy):
        copy.start()
    mask_copy.wait()

    mask_f = mask[...].astype(F32)
    mask_t = mask_f.T
    for k in range(2):
        mcol[k * 512:(k + 1) * 512, :] = jnp.sum(
            jnp.where(iota((512, 64), 1) == 2 * me + k, mask_t, 0.0), axis=1, keepdims=True
        )
    al_copy.wait()
    for k in range(2):
        rows = slice(k * 512, (k + 1) * 512)
        wide = al[rows, :].astype(F32)
        center = jnp.mean(wide, axis=-1, keepdims=True)
        apart = wide - center
        spread = jnp.mean(apart * apart, axis=-1, keepdims=True)
        inverse = lax.rsqrt(spread + 1e-05)
        standard = apart * inverse
        std[rows, :] = standard
        inv[rows, :] = inverse
        normed[rows, :] = (standard * scales[...] + shifts[...]).astype(BF16)
    both[...] = (mm_nt(normed[...], proj[...]) + offs[...]) * mcol[...]
    cat = jnp.concatenate([both[0:512, :], both[512:1024, :]], axis=1)
    l_out[...] = cat.astype(BF16).reshape(32, 16, 128)
    cat_t = cat.T
    r_buf[mine] = jnp.concatenate([cat_t[32:64], cat_t[96:128]], axis=0).astype(BF16)

    pl.semaphore_wait(barrier, 31)

    def l_send(k, carry):
        s = lax.rem(mine + k, 32)
        p = slot_dev(s)
        remote(l_out.at[p], l_in.at[mine], l_ss.at[k], l_rs.at[mine], p).start()
        return carry

    lax.fori_loop(1, 32, l_send, 0)

    def r_send(s, target, k):
        remote(r_buf.at[s], r_buf.at[s], r_ss.at[k], r_rs.at[s], target).start()

    def r_wait(s):
        remote(r_buf.at[s], r_buf.at[s], r_ss.at[0], r_rs.at[s], sib).wait_recv()

    r_send(mine, dev(zs, xx, core), 0)
    r_send(mine, dev(zm, xx, core), 1)
    r_send(mine, dev(zz, xs, core), 2)
    r_send(mine, dev(zz, xm, core), 3)
    r_send(mine, sib, 4)
    l_in[mine] = l_out[me]

    mask_b = mask_f.astype(BF16)
    own_cols = (iota((512, 16), 0) == 16 * me + iota((512, 16), 1)).astype(F32).astype(BF16)
    mask_own = mm(mask_b, own_cols).astype(BF16)
    recip = 1.0 / (0.001 + mm(mask_t.astype(BF16), mask_own))
    total = jnp.zeros((1, 128), F32)
    cot_copy.wait()
    for i in range(16):
        rec_i = jnp.broadcast_to(recip[:, i:i + 1], (512, 128))
        rec[i] = rec_i
        sg = (cot_v[i].astype(F32) * rec_i).astype(BF16)
        g[:, i * 128:(i + 1) * 128] = sg
        total = total + jnp.sum(sg.astype(F32), axis=0, keepdims=True)
    bsum[...] = total

    readout_copy.wait()
    ro_f[...] = readout[...].astype(F32)
    for d in range(32):
        w[:, d * 128:(d + 1) * 128] = ro_f[pl.ds(d, 32, stride=32), :].astype(BF16)

    def packed(a):
        return lax.rem(a, 8) * 64 + lax.rem(lax.div(a, 8), 2) * 32 + lax.div(a, 16)

    perm[...] = (iota((512, 512), 1) == packed(iota((512, 512), 0))).astype(F32).astype(BF16)
    perm_t[...] = (iota((512, 512), 0) == packed(iota((512, 512), 1))).astype(F32).astype(BF16)

    def l_wait(k, carry):
        s = lax.rem(mine + k, 32)
        remote(l_out.at[0], l_in.at[s], l_ss.at[k], l_rs.at[s], sib).wait_recv()
        return carry

    lax.fori_loop(1, 32, l_wait, 0)
    l_f[...] = l_in[...].reshape(512, 128).astype(F32)
    for i in range(16):
        v = l_f[pl.ds(i, 32, stride=16), :]
        for x in range(4):
            part = v[x * 8:x * 8 + 8, :]
            l_all[x * 256 + i * 16:x * 256 + (i + 1) * 16, :] = jnp.concatenate(
                [part[:, 0:32], part[:, 64:96]], axis=0
            ).astype(BF16)
    l_t[...] = l_all[...].astype(F32).T.astype(BF16)

    def t_group(x_):
        r = mm(l_all[pl.ds(pl.multiple_of(x_ * 256, 256), 256), :], w[...]).astype(BF16)
        for d in range(32):
            t[x_, :, d] = r[:, d * 128:(d + 1) * 128].reshape(16, 16, 128)

    def d_group(x_, n):
        rows = jnp.concatenate([t[x_, i].reshape(512, 128) for i in range(16)], axis=1)
        raw = mm_nt(rows, g[...]).astype(BF16)
        d_buf[x_] = mm(perm_t[...], raw).astype(BF16).reshape(2, 256, 512)
        remote(d_buf.at[x_, other], c_in.at[x_], d_ss.at[n], d_rs.at[x_], sib).start()

    def c_wait(x_, n):
        remote(d_buf.at[x_, other], c_in.at[x_], d_ss.at[n], d_rs.at[x_], sib).wait_recv()

    def core_sum(x_):
        return d_buf[x_, core].astype(F32) + c_in[x_].astype(F32)

    def x_copy(x_, n, target_x):
        return remote(
            s1.at[x_], x_in.at[n], d_ss.at[4 + n], d_rs.at[4 + n], dev(zz, target_x, core)
        )

    t_group(xf)
    r_wait(slot(xx, core, zm))
    r_send(slot(xx, core, zm), dev(zs, xx, core), 5)
    for n, z_ in enumerate((zm, zs)):
        if n == 1:
            r_wait(slot(xx, core, z_))
        r_send(slot(xx, core, z_), dev(zz, xs, core), 6 + 3 * n)
        r_send(slot(xx, core, z_), dev(zz, xm, core), 7 + 3 * n)
        r_send(slot(xx, core, z_), sib, 8 + 3 * n)
    d_group(xf, 0)
    r_wait(slot(xm, core, zz))
    r_send(slot(xm, core, zz), dev(zz, xs, core), 15)
    r_send(slot(xm, core, zz), sib, 16)
    r_wait(slot(xs, core, zz))
    r_send(slot(xs, core, zz), sib, 17)
    t_group(xm)
    r_wait(slot(xx, core, zf))
    r_send(slot(xx, core, zf), dev(zz, xs, core), 12)
    r_send(slot(xx, core, zf), dev(zz, xm, core), 13)
    r_send(slot(xx, core, zf), sib, 14)
    d_group(xm, 1)
    c_wait(xf, 0)
    s1[xf] = core_sum(xf).astype(BF16)
    x_copy(xf, 0, xs).start()
    for n, z_ in enumerate((zm, zs)):
        r_wait(slot(xm, core, z_))
        r_send(slot(xm, core, z_), dev(zz, xs, core), 18 + 3 * n)
        r_send(slot(xm, core, z_), sib, 19 + 3 * n)
        r_wait(slot(xs, core, z_))
        r_send(slot(xs, core, z_), sib, 20 + 3 * n)
    t_group(xs)
    d_group(xs, 2)
    c_wait(xm, 1)
    s1[xm] = core_sum(xm).astype(BF16)
    x_copy(xm, 1, xm).start()
    r_wait(slot(xm, core, zf))
    r_send(slot(xm, core, zf), dev(zz, xs, core), 24)
    r_send(slot(xm, core, zf), sib, 25)
    r_wait(slot(xs, core, zf))
    r_send(slot(xs, core, zf), sib, 26)
    r_wait(slot(xf, core, zz))
    r_send(slot(xf, core, zz), sib, 27)
    t_group(xx)
    d_group(xx, 3)

    def r_prep(x_):
        for z_ in range(4):
            r_wait(slot(x_, other, z_))
        raw = r_buf[pl.ds(x_ * 8, 8)].reshape(512, 512)
        moved = mm(perm[...], raw)
        r_k[...] = moved.astype(BF16)
        r_j[:, pl.ds(pl.multiple_of(x_ * 512, 512), 512)] = moved.T.astype(BF16)

    def e_copy(s, k):
        return remote(lg_out.at[s], lg_in.at[me], e_ss.at[k], e_rs.at[me], slot_dev(s))

    def q_group(x_):
        for h in range(2):
            block = mm(r_k[...], g[:, h * 1024:(h + 1) * 1024]).astype(BF16)
            for i in range(8):
                q[x_, h * 8 + i] = block[:, i * 128:(i + 1) * 128].reshape(32, 16, 128)

    def lg_group(x_, n):
        rows = jnp.concatenate([q[x_, :, d].reshape(256, 128) for d in range(32)], axis=1)
        lg_f[:, 0:32] = mm_nt(rows, w[...])
        for c in range(8):
            pieces = [lg_f[pl.ds(c + 8 * k, 16, stride=16), :][:, 0:32] for k in range(2)]
            pieces.append(jnp.zeros((16, 64), F32))
            lg_out[x_ * 8 + c] = jnp.concatenate(pieces, axis=1).astype(BF16)
        if n == 0:
            for k in range(1, 8):
                e_copy(x_ * 8 + lax.rem(core * 4 + zz + k, 8), k).start()
            lg_in[me] = lg_out[mine]
        else:
            for k in range(8):
                e_copy(x_ * 8 + k, n * 8 + k).start()

    def z_copy(k):
        z_ = lax.rem(zz + k, 4)
        return remote(
            s2.at[z_], z_in.at[zz], d_ss.at[6 + k], d_rs.at[7 + zz], dev(z_, xx, core)
        )

    def rg_group(x_, n):
        cols = l_t[:, pl.ds(pl.multiple_of(x_ * 256, 256), 256)]
        rows = jnp.concatenate([q[x_, :, d].reshape(256, 128) for d in range(32)], axis=1)
        part = mm(cols, rows)
        rg_l[...] = part if n == 0 else rg_l[...] + part

    r_prep(xx)
    q_group(xx)
    c_wait(xs, 2)
    x_copy(xf, 0, xs).wait_recv()
    s1[xs] = (core_sum(xs) + x_in[0].astype(F32)).astype(BF16)
    x_copy(xs, 2, xs).start()
    lg_group(xx, 0)
    for n, z_ in enumerate((zm, zs, zf)):
        r_wait(slot(xf, core, z_))
        r_send(slot(xf, core, z_), sib, 28 + n)
    rg_group(xx, 0)
    r_prep(xm)
    q_group(xm)
    lg_group(xm, 1)
    rg_group(xm, 1)
    r_prep(xs)
    q_group(xs)
    c_wait(xx, 3)
    x_copy(xm, 1, xm).wait_recv()
    x_copy(xs, 2, xs).wait_recv()
    s2[...] = (
        core_sum(xx) + x_in[1].astype(F32) + x_in[2].astype(F32)
    ).astype(BF16).reshape(4, 64, 512)
    for k in range(1, 4):
        z_copy(k).start()
    lg_group(xs, 2)
    rg_group(xs, 2)
    r_prep(xf)
    q_group(xf)

    rg_group(xf, 3)
    for d in range(32):
        rg_f[pl.ds(d, 32, stride=32), :] = rg_l[:, d * 128:(d + 1) * 128]
    rg_b[...] = rg_f[...].astype(BF16).reshape(2, 512, 128)
    a0 = remote(rg_b.at[other], ra, a_ss.at[0], a_rs.at[0], sib)
    a0.start()
    lg_group(xf, 3)

    def u_step(ib):
        cols = jnp.concatenate(
            [t[:, ib * 4 + ii].reshape(2048, 128) for ii in range(4)], axis=1
        )
        acc = mm(r_j[...], cols)
        for ii in range(4):
            pair_v[4 * ib + ii] = (
                (acc[:, ii * 128:(ii + 1) * 128] + biases[...]) * rec[4 * ib + ii]
            ).astype(BF16)

    u_step(0)
    u_step(1)

    a0.wait_recv()
    rb[...] = (rg_b[core].astype(F32) + ra[...].astype(F32)).astype(BF16).reshape(4, 128, 128)

    def a_x(k):
        x_ = lax.rem(xx + k, 4)
        return remote(rb.at[x_], rc.at[xx], a_ss.at[k], a_rs.at[1 + xx], dev(zz, x_, core))

    for k in range(1, 4):
        a_x(k).start()
    rc[xx] = rb[xx]

    for k in range(1, 32):
        p = lax.rem(me + k, 32)
        remote(lg_out.at[0], lg_in.at[p], e_ss.at[k], e_rs.at[p], sib).wait_recv()
    for k in range(1, 4):
        z_ = lax.rem(zz + k, 4)
        remote(s2.at[z_], z_in.at[z_], d_ss.at[6 + k], d_rs.at[7 + z_], sib).wait_recv()
    z_in[zz] = s2[zz]
    right = (z_in[0].astype(F32) + z_in[1].astype(F32)) + (
        z_in[2].astype(F32) + z_in[3].astype(F32)
    )
    right_t = right.T
    left = lg_in[...].reshape(512, 128).astype(F32)
    for k in range(2):
        both[k * 512:(k + 1) * 512, :] = jnp.concatenate(
            [left[:, k * 32:(k + 1) * 32], right_t[:, k * 32:(k + 1) * 32]], axis=1
        ) * mcol[k * 512:(k + 1) * 512, :]
    pgb = both[...].astype(BF16)
    pj_acc = mm_tn(pgb, normed[...])
    of_acc = jnp.sum(pgb.astype(F32), axis=0, keepdims=True)
    ng_s[...] = mm(pgb, proj[...])
    sc_acc = jnp.sum(ng_s[...] * std[...], axis=0, keepdims=True)
    sh_acc = jnp.sum(ng_s[...], axis=0, keepdims=True)
    pb[0] = pj_acc[0:48].astype(BF16)
    pb[1] = jnp.concatenate(
        [
            pj_acc[48:64], sc_acc, sh_acc,
            jnp.concatenate([of_acc, jnp.zeros((1, 64), F32), bsum[...]], axis=1),
            jnp.zeros((29, 256), F32),
        ],
        axis=0,
    ).astype(BF16)
    b0 = remote(pb.at[other], pb_core, b_ss.at[0], b_rs.at[0], sib)
    b0.start()

    for k in range(1, 4):
        x_ = lax.rem(xx + k, 4)
        remote(rb.at[x_], rc.at[x_], a_ss.at[k], a_rs.at[1 + x_], sib).wait_recv()

    def four(ref):
        return (ref[0].astype(F32) + ref[1].astype(F32)) + (
            ref[2].astype(F32) + ref[3].astype(F32)
        )

    re[zz] = four(rc).astype(BF16)

    def a_z(k):
        z_ = lax.rem(zz + k, 4)
        return remote(re.at[zz], re.at[zz], a_ss.at[3 + k], a_rs.at[5 + zz], dev(z_, xx, core))

    for k in range(1, 4):
        a_z(k).start()

    b0.wait_recv()
    pb_x[xx] = (pb[core].astype(F32) + pb_core[...].astype(F32)).astype(BF16)

    def b_x(k):
        x_ = lax.rem(xx + k, 4)
        return remote(pb_x.at[xx], pb_x.at[xx], b_ss.at[k], b_rs.at[1 + xx], dev(zz, x_, core))

    for k in range(1, 4):
        b_x(k).start()

    for b in range(4):
        rows = slice(b * 256, (b + 1) * 256)
        h = ng_s[rows, :] * scales[...]
        standard = std[rows, :]
        m1 = jnp.mean(h, axis=-1, keepdims=True)
        m2 = jnp.mean(h * standard, axis=-1, keepdims=True)
        al_v[rows, :] = ((h - m1 - standard * m2) * inv[rows, :]).astype(BF16)
    u_step(2)

    for k in range(1, 4):
        z_ = lax.rem(zz + k, 4)
        remote(re.at[z_], re.at[z_], a_ss.at[3 + k], a_rs.at[5 + z_], sib).wait_recv()
    rh[xx] = four(re).astype(BF16)

    def a_g(k):
        x_ = lax.rem(xx + k, 4)
        return remote(rh.at[xx], rh.at[xx], a_ss.at[6 + k], a_rs.at[9 + xx], dev(zz, x_, core))

    for k in range(1, 4):
        a_g(k).start()

    for k in range(1, 4):
        x_ = lax.rem(xx + k, 4)
        remote(pb_x.at[x_], pb_x.at[x_], b_ss.at[k], b_rs.at[1 + x_], sib).wait_recv()
    pb_z[zz] = four(pb_x).astype(BF16)

    def b_z(k):
        z_ = lax.rem(zz + k, 4)
        return remote(
            pb_z.at[zz], pb_z.at[zz], b_ss.at[3 + k], b_rs.at[5 + zz], dev(z_, xx, core)
        )

    for k in range(1, 4):
        b_z(k).start()
    u_step(3)

    for k in range(1, 4):
        x_ = lax.rem(xx + k, 4)
        remote(rh.at[x_], rh.at[x_], a_ss.at[6 + k], a_rs.at[9 + x_], sib).wait_recv()
    a_last = remote(rh, rk, a_ss.at[10], a_rs.at[13], sib)
    a_last.start()
    rg_o[pl.ds(pl.multiple_of(core * 512, 512), 512), :] = rh[...].reshape(512, 128).astype(F32)

    for k in range(1, 4):
        z_ = lax.rem(zz + k, 4)
        remote(pb_z.at[z_], pb_z.at[z_], b_ss.at[3 + k], b_rs.at[5 + z_], sib).wait_recv()
    pb_half[core] = four(pb_z).astype(BF16)
    b_last = remote(pb_half.at[core], pb_half.at[core], b_ss.at[7], b_rs.at[9], sib)
    b_last.start()

    def drain(k, carry):
        remote(l_out.at[0], l_in.at[0], l_ss.at[k], l_rs.at[0], sib).wait_send()
        remote(lg_out.at[0], lg_in.at[0], e_ss.at[k], e_rs.at[0], sib).wait_send()
        remote(r_buf.at[0], r_buf.at[0], r_ss.at[k - 1], r_rs.at[0], sib).wait_send()
        return carry

    lax.fori_loop(1, 32, drain, 0)
    for n, x_ in enumerate((xf, xm, xs, xx)):
        remote(d_buf.at[x_, other], c_in.at[x_], d_ss.at[n], d_rs.at[x_], sib).wait_send()
    x_copy(xf, 0, xs).wait_send()
    x_copy(xm, 1, xm).wait_send()
    x_copy(xs, 2, xs).wait_send()
    a0.wait_send()
    b0.wait_send()
    for k in range(1, 4):
        z_copy(k).wait_send()
        a_x(k).wait_send()
        a_z(k).wait_send()
        a_g(k).wait_send()
        b_x(k).wait_send()
        b_z(k).wait_send()
    a_last.wait()
    rg_o[pl.ds(pl.multiple_of(other * 512, 512), 512), :] = rk[...].reshape(512, 128).astype(F32)
    remote(
        pb_half.at[other], pb_half.at[other], b_ss.at[7], b_rs.at[9], sib
    ).wait_recv()
    b_last.wait_send()
    pg_o[...] = jnp.concatenate([pb_half[0], pb_half[1, 0:16]], axis=0).astype(F32)
    vec = pb_half[1, 16:32].astype(F32)
    sg_o[...] = vec[0:1, :]
    hg_o[...] = vec[1:2, :]
    og_o[...] = vec[2:3, 0:64]
    bg_o[...] = vec[2:3, 128:256]


def finish(*refs):
    srcs, dsts, sems = refs[0:8], refs[8:16], refs[16]
    copies = [
        pltpu.make_async_copy(srcs[0].at[pl.ds(4 * n, 4)], dsts[0].at[pl.ds(4 * n, 4)], sems.at[n])
        for n in range(4)
    ]
    copies += [pltpu.make_async_copy(srcs[n], dsts[n], sems.at[3 + n]) for n in range(1, 8)]
    for copy in copies:
        copy.start()
    for copy in copies:
        copy.wait()


def per_device(
    alignment, alignment_mask, cotangent, scales, shifts, projection, offsets, readout, biases
):
    vmem = pl.BlockSpec(memory_space=pltpu.VMEM)
    shape = jax.ShapeDtypeStruct
    sizes = dict(
        al=((1024, 256), BF16),
        mask=((64, 512), jnp.int32),
        readout=((1024, 128), BF16),
        cot_v=((16, 512, 128), BF16),
        mcol=((1024, 1), F32),
        std=((1024, 256), F32),
        inv=((1024, 1), F32),
        normed=((1024, 256), BF16),
        both=((1024, 64), F32),
        l_out=((32, 16, 128), BF16),
        l_in=((32, 16, 128), BF16),
        l_f=((512, 128), F32),
        l_all=((1024, 32), BF16),
        l_t=((32, 1024), BF16),
        w=((32, 4096), BF16),
        ro_f=((1024, 128), F32),
        rec=((16, 512, 128), F32),
        g=((512, 2048), BF16),
        perm=((512, 512), BF16),
        perm_t=((512, 512), BF16),
        r_buf=((32, 64, 512), BF16),
        r_k=((512, 512), BF16),
        r_j=((512, 2048), BF16),
        t=((4, 16, 32, 16, 128), BF16),
        q=((4, 16, 32, 16, 128), BF16),
        d_buf=((4, 2, 256, 512), BF16),
        c_in=((4, 256, 512), BF16),
        s1=((4, 256, 512), BF16),
        x_in=((3, 256, 512), BF16),
        s2=((4, 64, 512), BF16),
        z_in=((4, 64, 512), BF16),
        lg_f=((256, 128), F32),
        lg_out=((32, 16, 128), BF16),
        lg_in=((32, 16, 128), BF16),
        rg_l=((32, 4096), F32),
        rg_f=((1024, 128), F32),
        rg_b=((2, 512, 128), BF16),
        ra=((512, 128), BF16),
        rb=((4, 128, 128), BF16),
        rc=((4, 128, 128), BF16),
        re=((4, 128, 128), BF16),
        rh=((4, 128, 128), BF16),
        rk=((4, 128, 128), BF16),
        ng_s=((1024, 256), F32),
        pb=((2, 48, 256), BF16),
        pb_core=((48, 256), BF16),
        pb_x=((4, 48, 256), BF16),
        pb_z=((4, 48, 256), BF16),
        pb_half=((2, 48, 256), BF16),
        bsum=((1, 128), F32),
    )
    scratch = [pltpu.VMEM(*size) for size in sizes.values()] + [
        pltpu.SemaphoreType.DMA((n,)) for n in (32, 32, 32, 32, 31, 32, 10, 11, 11, 14, 8, 10, 4)
    ]
    anywhere = pl.BlockSpec(memory_space=pl.ANY)
    outs = pl.pallas_call(
        kernel,
        out_shape=(
            pltpu.VMEM((16, 512, 128), BF16),
            pltpu.VMEM((1024, 256), BF16),
            pltpu.VMEM((64, 256), F32),
            pltpu.VMEM((1, 64), F32),
            pltpu.VMEM((1024, 128), F32),
            pltpu.VMEM((1, 128), F32),
            pltpu.VMEM((1, 256), F32),
            pltpu.VMEM((1, 256), F32),
        ),
        in_specs=[anywhere] * 3 + [vmem] * 4 + [anywhere, vmem],
        out_specs=[vmem] * 8,
        scratch_shapes=scratch,
        compiler_params=pltpu.CompilerParams(
            collective_id=0, has_side_effects=True, vmem_limit_bytes=56 * 1024 * 1024
        ),
        cost_estimate=pl.CostEstimate(
            flops=16_000_000_000, bytes_accessed=6_000_000, transcendentals=0
        ),
        name="outer_product_mean",
    )(
        alignment.reshape(1024, 256),
        alignment_mask,
        cotangent,
        scales.reshape(1, 256),
        shifts.reshape(1, 256),
        projection.T,
        offsets.reshape(1, 64),
        readout,
        biases.reshape(1, 128),
    )
    outs = pl.pallas_call(
        finish,
        out_shape=tuple(shape(out.shape, out.dtype) for out in outs),
        in_specs=[vmem] * 8,
        out_specs=[anywhere] * 8,
        scratch_shapes=[pltpu.SemaphoreType.DMA((11,))],
        name="results",
    )(*[pltpu.with_memory_space_constraint(out, pltpu.VMEM) for out in outs])
    return (
        outs[0],
        outs[1].reshape(2, 512, 256),
        outs[2].T,
        outs[3].reshape(64),
        outs[4],
        outs[5].reshape(128),
        outs[6].reshape(256),
        outs[7].reshape(256),
    )


def solution(mesh):
    return jax.shard_map(
        per_device,
        mesh=mesh,
        in_specs=(
            P(("crop", "dap"), None, None),
            P("crop", None),
            P(("crop", "dap"), None, None),
            P(),
            P(),
            P(),
            P(),
            P(),
            P(),
        ),
        out_specs=(
            P(("crop", "dap"), None, None),
            P(("crop", "dap"), None, None),
            P("crop", None),
            P("crop"),
            P("crop", None),
            P("crop"),
            P("crop"),
            P("crop"),
        ),
        check_vma=False,
    )
```

```python
import jax
import jax.numpy as jnp
from jax import lax
from jax.experimental import pallas as pl
from jax.experimental.pallas import tpu as pltpu
from jax.sharding import PartitionSpec as P

F32 = jnp.float32
BF16 = jnp.bfloat16
MESH = pl.DeviceIdType.MESH


def mm(a, b):
    return lax.dot_general(a, b, (((1,), (0,)), ((), ())), preferred_element_type=F32)


def mm_nt(a, b):
    return lax.dot_general(a, b, (((1,), (1,)), ((), ())), preferred_element_type=F32)


def mm_tn(a, b):
    return lax.dot_general(a, b, (((0,), (0,)), ((), ())), preferred_element_type=F32)


def iota(shape, dim):
    return lax.broadcasted_iota(jnp.int32, shape, dim)


def kernel(
    al_h, mask_h, cot, scales_h, shifts_h, proj_h, offs_h, readout_h, biases_h,
    pair_v, al_v, pg_o, og_o, rg_o, bg_o, sg_o, hg_o,
    al, mask, readout, scales, shifts, proj, offs, biases, cot_v, mcol, std, inv, normed, both, l_out, l_in, l_f, l_all, l_t, w, ro_f,
    rec, g, perm, perm_t, r_buf, r_k, r_j, t, q,
    d_buf, c_in, s1, x_in, s2, z_in,
    lg_f, lg_out, lg_in, rg_l, rg_f, rg_b, ra, rb, rc, re, rh, rk,
    ng_s, pb, pb_core, pb_x, pb_z, pb_half, bsum,
    l_ss, l_rs, e_ss, e_rs, r_ss, r_rs, d_ss, d_rs, a_ss, a_rs, b_ss, b_rs, io,
):
    me = lax.axis_index("dap")
    core = lax.rem(me, 2)
    xx = lax.rem(lax.div(me, 2), 4)
    zz = lax.div(me, 8)
    sign = 1 - 2 * core
    xs, xm, xf = (lax.rem(xx + 4 + sign, 4), lax.rem(xx + 4 - sign, 4), lax.rem(xx + 2, 4))
    zs, zm, zf = (lax.rem(zz + 4 + sign, 4), lax.rem(zz + 4 - sign, 4), lax.rem(zz + 2, 4))
    other = 1 - core

    def dev(z, x, c):
        return (z * 4 + x) * 2 + c

    def slot(x, c, z):
        return (x * 2 + c) * 4 + z

    def slot_dev(s):
        return dev(lax.rem(s, 4), lax.div(s, 8), lax.rem(lax.div(s, 4), 2))

    sib = dev(zz, xx, other)
    mine = slot(xx, core, zz)

    def remote(src, dst, ss, rs, target):
        return pltpu.make_async_remote_copy(
            src_ref=src, dst_ref=dst, send_sem=ss, recv_sem=rs,
            device_id={"dap": target}, device_id_type=MESH,
        )

    barrier = pltpu.get_barrier_semaphore()

    def greet(k, carry):
        pl.semaphore_signal(
            barrier, inc=1, device_id={"dap": lax.rem(me + k, 32)}, device_id_type=MESH
        )
        return carry

    lax.fori_loop(1, 32, greet, 0)
    fetches = [
        pltpu.make_async_copy(src, dst, io.at[n])
        for n, (src, dst) in enumerate((
            (mask_h, mask), (al_h, al), (scales_h, scales), (shifts_h, shifts), (proj_h, proj),
            (offs_h, offs), (cot, cot_v), (readout_h, readout), (biases_h, biases),
        ))
    ]
    for fetch in fetches:
        fetch.start()
    fetches[0].wait()

    mask_f = mask[...].astype(F32)
    mask_t = mask_f.T
    for k in range(2):
        mcol[k * 512:(k + 1) * 512, :] = jnp.sum(
            jnp.where(iota((512, 64), 1) == 2 * me + k, mask_t, 0.0), axis=1, keepdims=True
        )
    for fetch in fetches[1:6]:
        fetch.wait()
    for k in range(2):
        rows = slice(k * 512, (k + 1) * 512)
        wide = al[rows, :].astype(F32)
        center = jnp.mean(wide, axis=-1, keepdims=True)
        apart = wide - center
        spread = jnp.mean(apart * apart, axis=-1, keepdims=True)
        inverse = lax.rsqrt(spread + 1e-05)
        standard = apart * inverse
        std[rows, :] = standard
        inv[rows, :] = inverse
        normed[rows, :] = (standard * scales[...] + shifts[...]).astype(BF16)
    both[...] = (mm_nt(normed[...], proj[...]) + offs[...]) * mcol[...]
    cat = jnp.concatenate([both[0:512, :], both[512:1024, :]], axis=1)
    l_out[...] = cat.astype(BF16).reshape(32, 16, 128)
    cat_t = cat.T
    r_buf[mine] = jnp.concatenate([cat_t[32:64], cat_t[96:128]], axis=0).astype(BF16)

    pl.semaphore_wait(barrier, 31)

    def l_copy(s, k):
        p = slot_dev(s)
        return remote(l_out.at[p], l_in.at[mine], l_ss.at[k], l_rs.at[mine], p)

    for n, x_ in enumerate((xf, xs, xm)):
        for k in range(8):
            l_copy(x_ * 8 + k, n * 8 + k).start()
    for k in range(1, 8):
        l_copy(xx * 8 + lax.rem(core * 4 + zz + k, 8), 24 + k).start()

    def r_send(s, target, k):
        remote(r_buf.at[s], r_buf.at[s], r_ss.at[k], r_rs.at[s], target).start()

    def r_wait(s):
        remote(r_buf.at[s], r_buf.at[s], r_ss.at[0], r_rs.at[s], sib).wait_recv()

    r_send(mine, dev(zs, xx, core), 0)
    r_send(mine, dev(zm, xx, core), 1)
    r_send(mine, dev(zz, xs, core), 2)
    r_send(mine, dev(zz, xm, core), 3)
    r_send(mine, sib, 4)
    l_in[mine] = l_out[me]

    mask_b = mask_f.astype(BF16)
    own_cols = (iota((512, 16), 0) == 16 * me + iota((512, 16), 1)).astype(F32).astype(BF16)
    mask_own = mm(mask_b, own_cols).astype(BF16)
    recip = 1.0 / (0.001 + mm(mask_t.astype(BF16), mask_own))
    total = jnp.zeros((1, 128), F32)
    fetches[6].wait()
    for i in range(16):
        rec_i = jnp.broadcast_to(recip[:, i:i + 1], (512, 128))
        rec[i] = rec_i
        sg = (cot_v[i].astype(F32) * rec_i).astype(BF16)
        g[:, i * 128:(i + 1) * 128] = sg
        total = total + jnp.sum(sg.astype(F32), axis=0, keepdims=True)
    bsum[...] = total

    fetches[7].wait()
    fetches[8].wait()
    ro_f[...] = readout[...].astype(F32)
    for d in range(32):
        w[:, d * 128:(d + 1) * 128] = ro_f[pl.ds(d, 32, stride=32), :].astype(BF16)

    def packed(a):
        return lax.rem(a, 8) * 64 + lax.rem(lax.div(a, 8), 2) * 32 + lax.div(a, 16)

    perm[...] = (iota((512, 512), 1) == packed(iota((512, 512), 0))).astype(F32).astype(BF16)
    perm_t[...] = (iota((512, 512), 0) == packed(iota((512, 512), 1))).astype(F32).astype(BF16)

    def t_group(x_, own=False):
        for k in range(1 if own else 0, 8):
            s = x_ * 8 + (lax.rem(core * 4 + zz + k, 8) if own else k)
            remote(l_out.at[0], l_in.at[s], l_ss.at[0], l_rs.at[s], sib).wait_recv()
        l_f[...] = l_in[pl.ds(x_ * 8, 8)].reshape(128, 128).astype(F32)
        for i in range(16):
            part = l_f[pl.ds(i, 8, stride=16), :]
            l_all[x_, i] = jnp.concatenate([part[:, 0:32], part[:, 64:96]], axis=0).astype(BF16)
        rows = l_all[x_].reshape(256, 32)
        l_t[x_] = rows.astype(F32).T.astype(BF16)
        r = mm(rows, w[...]).astype(BF16)
        for d in range(32):
            t[x_, :, d] = r[:, d * 128:(d + 1) * 128].reshape(16, 16, 128)

    def d_group(x_, n):
        rows = jnp.concatenate([t[x_, i].reshape(512, 128) for i in range(16)], axis=1)
        raw = mm_nt(rows, g[...]).astype(BF16)
        d_buf[x_] = mm(perm_t[...], raw).astype(BF16).reshape(2, 256, 512)
        remote(d_buf.at[x_, other], c_in.at[x_], d_ss.at[n], d_rs.at[x_], sib).start()

    def c_wait(x_, n):
        remote(d_buf.at[x_, other], c_in.at[x_], d_ss.at[n], d_rs.at[x_], sib).wait_recv()

    def core_sum(x_):
        return d_buf[x_, core].astype(F32) + c_in[x_].astype(F32)

    def x_copy(x_, n, target_x):
        return remote(
            s1.at[x_], x_in.at[n], d_ss.at[4 + n], d_rs.at[4 + n], dev(zz, target_x, core)
        )

    r_wait(slot(xx, core, zm))
    r_send(slot(xx, core, zm), dev(zs, xx, core), 5)
    for n, z_ in enumerate((zm, zs)):
        if n == 1:
            r_wait(slot(xx, core, z_))
        r_send(slot(xx, core, z_), dev(zz, xs, core), 6 + 3 * n)
        r_send(slot(xx, core, z_), dev(zz, xm, core), 7 + 3 * n)
        r_send(slot(xx, core, z_), sib, 8 + 3 * n)
    t_group(xf)
    r_wait(slot(xm, core, zz))
    r_send(slot(xm, core, zz), dev(zz, xs, core), 15)
    r_send(slot(xm, core, zz), sib, 16)
    r_wait(slot(xs, core, zz))
    r_send(slot(xs, core, zz), sib, 17)
    d_group(xf, 0)
    t_group(xm)
    r_wait(slot(xx, core, zf))
    r_send(slot(xx, core, zf), dev(zz, xs, core), 12)
    r_send(slot(xx, core, zf), dev(zz, xm, core), 13)
    r_send(slot(xx, core, zf), sib, 14)
    d_group(xm, 1)
    c_wait(xf, 0)
    s1[xf] = core_sum(xf).astype(BF16)
    x_copy(xf, 0, xs).start()
    for n, z_ in enumerate((zm, zs)):
        r_wait(slot(xm, core, z_))
        r_send(slot(xm, core, z_), dev(zz, xs, core), 18 + 3 * n)
        r_send(slot(xm, core, z_), sib, 19 + 3 * n)
        r_wait(slot(xs, core, z_))
        r_send(slot(xs, core, z_), sib, 20 + 3 * n)
    t_group(xs)
    d_group(xs, 2)
    c_wait(xm, 1)
    s1[xm] = core_sum(xm).astype(BF16)
    x_copy(xm, 1, xm).start()
    r_wait(slot(xf, core, zz))
    r_send(slot(xf, core, zz), sib, 27)
    t_group(xx, own=True)
    r_wait(slot(xm, core, zf))
    r_send(slot(xm, core, zf), dev(zz, xs, core), 24)
    r_send(slot(xm, core, zf), sib, 25)
    r_wait(slot(xs, core, zf))
    r_send(slot(xs, core, zf), sib, 26)
    d_group(xx, 3)

    def r_prep(x_):
        for z_ in range(4):
            r_wait(slot(x_, other, z_))
        raw = r_buf[pl.ds(x_ * 8, 8)].reshape(512, 512)
        moved = mm(perm[...], raw)
        r_k[...] = moved.astype(BF16)
        r_j[:, pl.ds(pl.multiple_of(x_ * 512, 512), 512)] = moved.T.astype(BF16)

    def e_copy(s, k):
        return remote(lg_out.at[s], lg_in.at[me], e_ss.at[k], e_rs.at[me], slot_dev(s))

    def q_group(x_):
        for h in range(2):
            block = mm(r_k[...], g[:, h * 1024:(h + 1) * 1024]).astype(BF16)
            for i in range(8):
                q[x_, h * 8 + i] = block[:, i * 128:(i + 1) * 128].reshape(32, 16, 128)

    def lg_group(x_, n):
        rows = jnp.concatenate([q[x_, :, d].reshape(256, 128) for d in range(32)], axis=1)
        lg_f[:, 0:32] = mm_nt(rows, w[...])
        for c in range(8):
            pieces = [lg_f[pl.ds(c + 8 * k, 16, stride=16), :][:, 0:32] for k in range(2)]
            pieces.append(jnp.zeros((16, 64), F32))
            lg_out[x_ * 8 + c] = jnp.concatenate(pieces, axis=1).astype(BF16)
        if n == 0:
            for k in range(1, 8):
                e_copy(x_ * 8 + lax.rem(core * 4 + zz + k, 8), k).start()
            lg_in[me] = lg_out[mine]
        else:
            for k in range(8):
                e_copy(x_ * 8 + k, n * 8 + k).start()

    def z_copy(k):
        z_ = lax.rem(zz + k, 4)
        return remote(
            s2.at[z_], z_in.at[zz], d_ss.at[6 + k], d_rs.at[7 + zz], dev(z_, xx, core)
        )

    def rg_group(x_, n):
        rows = jnp.concatenate([q[x_, :, d].reshape(256, 128) for d in range(32)], axis=1)
        part = mm(l_t[x_], rows)
        rg_l[...] = part if n == 0 else rg_l[...] + part

    r_prep(xx)
    q_group(xx)
    c_wait(xs, 2)
    x_copy(xf, 0, xs).wait_recv()
    s1[xs] = (core_sum(xs) + x_in[0].astype(F32)).astype(BF16)
    x_copy(xs, 2, xs).start()
    for n, z_ in enumerate((zm, zs)):
        r_wait(slot(xf, core, z_))
        r_send(slot(xf, core, z_), sib, 28 + n)
    lg_group(xx, 0)
    rg_group(xx, 0)
    r_wait(slot(xf, core, zf))
    r_send(slot(xf, core, zf), sib, 30)
    r_prep(xm)
    q_group(xm)
    lg_group(xm, 1)
    rg_group(xm, 1)
    r_prep(xs)
    q_group(xs)
    c_wait(xx, 3)
    x_copy(xm, 1, xm).wait_recv()
    x_copy(xs, 2, xs).wait_recv()
    s2[...] = (
        core_sum(xx) + x_in[1].astype(F32) + x_in[2].astype(F32)
    ).astype(BF16).reshape(4, 64, 512)
    for k in range(1, 4):
        z_copy(k).start()
    lg_group(xs, 2)
    rg_group(xs, 2)
    r_prep(xf)
    q_group(xf)

    rg_group(xf, 3)
    for d in range(32):
        rg_f[pl.ds(d, 32, stride=32), :] = rg_l[:, d * 128:(d + 1) * 128]
    rg_b[...] = rg_f[...].astype(BF16).reshape(2, 512, 128)
    a0 = remote(rg_b.at[other], ra, a_ss.at[0], a_rs.at[0], sib)
    a0.start()
    lg_group(xf, 3)

    def u_step(ib):
        cols = jnp.concatenate(
            [t[:, ib * 4 + ii].reshape(2048, 128) for ii in range(4)], axis=1
        )
        acc = mm(r_j[...], cols)
        for ii in range(4):
            pair_v[4 * ib + ii] = (
                (acc[:, ii * 128:(ii + 1) * 128] + biases[...]) * rec[4 * ib + ii]
            ).astype(BF16)

    u_step(0)
    a0.wait_recv()
    rb[...] = (rg_b[core].astype(F32) + ra[...].astype(F32)).astype(BF16).reshape(4, 128, 128)

    def a_x(k):
        x_ = lax.rem(xx + k, 4)
        return remote(rb.at[x_], rc.at[xx], a_ss.at[k], a_rs.at[1 + xx], dev(zz, x_, core))

    for k in range(1, 4):
        a_x(k).start()
    rc[xx] = rb[xx]
    u_step(1)

    for k in range(1, 32):
        p = lax.rem(me + k, 32)
        remote(lg_out.at[0], lg_in.at[p], e_ss.at[k], e_rs.at[p], sib).wait_recv()
    for k in range(1, 4):
        z_ = lax.rem(zz + k, 4)
        remote(s2.at[z_], z_in.at[z_], d_ss.at[6 + k], d_rs.at[7 + z_], sib).wait_recv()
    z_in[zz] = s2[zz]
    right = (z_in[0].astype(F32) + z_in[1].astype(F32)) + (
        z_in[2].astype(F32) + z_in[3].astype(F32)
    )
    right_t = right.T
    left = lg_in[...].reshape(512, 128).astype(F32)
    for k in range(2):
        both[k * 512:(k + 1) * 512, :] = jnp.concatenate(
            [left[:, k * 32:(k + 1) * 32], right_t[:, k * 32:(k + 1) * 32]], axis=1
        ) * mcol[k * 512:(k + 1) * 512, :]
    pgb = both[...].astype(BF16)
    pj_acc = mm_tn(pgb, normed[...])
    of_acc = jnp.sum(pgb.astype(F32), axis=0, keepdims=True)
    ng_s[...] = mm(pgb, proj[...])
    sc_acc = jnp.sum(ng_s[...] * std[...], axis=0, keepdims=True)
    sh_acc = jnp.sum(ng_s[...], axis=0, keepdims=True)
    pb[0] = pj_acc[0:48].astype(BF16)
    pb[1] = jnp.concatenate(
        [
            pj_acc[48:64], sc_acc, sh_acc,
            jnp.concatenate([of_acc, jnp.zeros((1, 64), F32), bsum[...]], axis=1),
            jnp.zeros((29, 256), F32),
        ],
        axis=0,
    ).astype(BF16)
    b0 = remote(pb.at[other], pb_core, b_ss.at[0], b_rs.at[0], sib)
    b0.start()

    for k in range(1, 4):
        x_ = lax.rem(xx + k, 4)
        remote(rb.at[x_], rc.at[x_], a_ss.at[k], a_rs.at[1 + x_], sib).wait_recv()

    def four(ref):
        return (ref[0].astype(F32) + ref[1].astype(F32)) + (
            ref[2].astype(F32) + ref[3].astype(F32)
        )

    re[zz] = four(rc).astype(BF16)

    def a_z(k):
        z_ = lax.rem(zz + k, 4)
        return remote(re.at[zz], re.at[zz], a_ss.at[3 + k], a_rs.at[5 + zz], dev(z_, xx, core))

    for k in range(1, 4):
        a_z(k).start()

    b0.wait_recv()
    pb_x[xx] = (pb[core].astype(F32) + pb_core[...].astype(F32)).astype(BF16)

    def b_x(k):
        x_ = lax.rem(xx + k, 4)
        return remote(pb_x.at[xx], pb_x.at[xx], b_ss.at[k], b_rs.at[1 + xx], dev(zz, x_, core))

    for k in range(1, 4):
        b_x(k).start()

    for b in range(4):
        rows = slice(b * 256, (b + 1) * 256)
        h = ng_s[rows, :] * scales[...]
        standard = std[rows, :]
        m1 = jnp.mean(h, axis=-1, keepdims=True)
        m2 = jnp.mean(h * standard, axis=-1, keepdims=True)
        al_v[rows, :] = ((h - m1 - standard * m2) * inv[rows, :]).astype(BF16)
    u_step(2)

    for k in range(1, 4):
        z_ = lax.rem(zz + k, 4)
        remote(re.at[z_], re.at[z_], a_ss.at[3 + k], a_rs.at[5 + z_], sib).wait_recv()
    rh[xx] = four(re).astype(BF16)

    def a_g(k):
        x_ = lax.rem(xx + k, 4)
        return remote(rh.at[xx], rh.at[xx], a_ss.at[6 + k], a_rs.at[9 + xx], dev(zz, x_, core))

    for k in range(1, 4):
        a_g(k).start()

    for k in range(1, 4):
        x_ = lax.rem(xx + k, 4)
        remote(pb_x.at[x_], pb_x.at[x_], b_ss.at[k], b_rs.at[1 + x_], sib).wait_recv()
    pb_z[zz] = four(pb_x).astype(BF16)

    def b_z(k):
        z_ = lax.rem(zz + k, 4)
        return remote(
            pb_z.at[zz], pb_z.at[zz], b_ss.at[3 + k], b_rs.at[5 + zz], dev(z_, xx, core)
        )

    for k in range(1, 4):
        b_z(k).start()
    u_step(3)

    for k in range(1, 4):
        x_ = lax.rem(xx + k, 4)
        remote(rh.at[x_], rh.at[x_], a_ss.at[6 + k], a_rs.at[9 + x_], sib).wait_recv()
    a_last = remote(rh, rk, a_ss.at[10], a_rs.at[13], sib)
    a_last.start()
    rg_o[pl.ds(pl.multiple_of(core * 512, 512), 512), :] = rh[...].reshape(512, 128).astype(F32)

    for k in range(1, 4):
        z_ = lax.rem(zz + k, 4)
        remote(pb_z.at[z_], pb_z.at[z_], b_ss.at[3 + k], b_rs.at[5 + z_], sib).wait_recv()
    pb_half[core] = four(pb_z).astype(BF16)
    b_last = remote(pb_half.at[core], pb_half.at[core], b_ss.at[7], b_rs.at[9], sib)
    b_last.start()

    def drain(k, carry):
        remote(lg_out.at[0], lg_in.at[0], e_ss.at[k], e_rs.at[0], sib).wait_send()
        remote(r_buf.at[0], r_buf.at[0], r_ss.at[k - 1], r_rs.at[0], sib).wait_send()
        return carry

    lax.fori_loop(1, 32, drain, 0)
    for k in range(32):
        if k != 24:
            remote(l_out.at[0], l_in.at[0], l_ss.at[k], l_rs.at[0], sib).wait_send()
    for n, x_ in enumerate((xf, xm, xs, xx)):
        remote(d_buf.at[x_, other], c_in.at[x_], d_ss.at[n], d_rs.at[x_], sib).wait_send()
    x_copy(xf, 0, xs).wait_send()
    x_copy(xm, 1, xm).wait_send()
    x_copy(xs, 2, xs).wait_send()
    a0.wait_send()
    b0.wait_send()
    for k in range(1, 4):
        z_copy(k).wait_send()
        a_x(k).wait_send()
        a_z(k).wait_send()
        a_g(k).wait_send()
        b_x(k).wait_send()
        b_z(k).wait_send()
    a_last.wait()
    rg_o[pl.ds(pl.multiple_of(other * 512, 512), 512), :] = rk[...].reshape(512, 128).astype(F32)
    remote(
        pb_half.at[other], pb_half.at[other], b_ss.at[7], b_rs.at[9], sib
    ).wait_recv()
    b_last.wait_send()
    pg_o[...] = jnp.concatenate([pb_half[0], pb_half[1, 0:16]], axis=0).astype(F32)
    vec = pb_half[1, 16:32].astype(F32)
    sg_o[...] = vec[0:1, :]
    hg_o[...] = vec[1:2, :]
    og_o[...] = vec[2:3, 0:64]
    bg_o[...] = vec[2:3, 128:256]


def finish(*refs):
    srcs, dsts, sems = refs[0:8], refs[8:16], refs[16]
    copies = [
        pltpu.make_async_copy(srcs[0].at[pl.ds(4 * n, 4)], dsts[0].at[pl.ds(4 * n, 4)], sems.at[n])
        for n in range(4)
    ]
    copies += [pltpu.make_async_copy(srcs[n], dsts[n], sems.at[3 + n]) for n in range(1, 8)]
    for copy in copies:
        copy.start()
    for copy in copies:
        copy.wait()


def per_device(
    alignment, alignment_mask, cotangent, scales, shifts, projection, offsets, readout, biases
):
    vmem = pl.BlockSpec(memory_space=pltpu.VMEM)
    shape = jax.ShapeDtypeStruct
    sizes = dict(
        al=((1024, 256), BF16),
        mask=((64, 512), jnp.int32),
        readout=((1024, 128), BF16),
        scales=((1, 256), F32),
        shifts=((1, 256), F32),
        proj=((64, 256), BF16),
        offs=((1, 64), F32),
        biases=((1, 128), F32),
        cot_v=((16, 512, 128), BF16),
        mcol=((1024, 1), F32),
        std=((1024, 256), F32),
        inv=((1024, 1), F32),
        normed=((1024, 256), BF16),
        both=((1024, 64), F32),
        l_out=((32, 16, 128), BF16),
        l_in=((32, 16, 128), BF16),
        l_f=((128, 128), F32),
        l_all=((4, 16, 16, 32), BF16),
        l_t=((4, 32, 256), BF16),
        w=((32, 4096), BF16),
        ro_f=((1024, 128), F32),
        rec=((16, 512, 128), F32),
        g=((512, 2048), BF16),
        perm=((512, 512), BF16),
        perm_t=((512, 512), BF16),
        r_buf=((32, 64, 512), BF16),
        r_k=((512, 512), BF16),
        r_j=((512, 2048), BF16),
        t=((4, 16, 32, 16, 128), BF16),
        q=((4, 16, 32, 16, 128), BF16),
        d_buf=((4, 2, 256, 512), BF16),
        c_in=((4, 256, 512), BF16),
        s1=((4, 256, 512), BF16),
        x_in=((3, 256, 512), BF16),
        s2=((4, 64, 512), BF16),
        z_in=((4, 64, 512), BF16),
        lg_f=((256, 128), F32),
        lg_out=((32, 16, 128), BF16),
        lg_in=((32, 16, 128), BF16),
        rg_l=((32, 4096), F32),
        rg_f=((1024, 128), F32),
        rg_b=((2, 512, 128), BF16),
        ra=((512, 128), BF16),
        rb=((4, 128, 128), BF16),
        rc=((4, 128, 128), BF16),
        re=((4, 128, 128), BF16),
        rh=((4, 128, 128), BF16),
        rk=((4, 128, 128), BF16),
        ng_s=((1024, 256), F32),
        pb=((2, 48, 256), BF16),
        pb_core=((48, 256), BF16),
        pb_x=((4, 48, 256), BF16),
        pb_z=((4, 48, 256), BF16),
        pb_half=((2, 48, 256), BF16),
        bsum=((1, 128), F32),
    )
    scratch = [pltpu.VMEM(*size) for size in sizes.values()] + [
        pltpu.SemaphoreType.DMA((n,)) for n in (32, 32, 32, 32, 31, 32, 10, 11, 11, 14, 8, 10, 9)
    ]
    anywhere = pl.BlockSpec(memory_space=pl.ANY)
    outs = pl.pallas_call(
        kernel,
        out_shape=(
            pltpu.VMEM((16, 512, 128), BF16),
            pltpu.VMEM((1024, 256), BF16),
            pltpu.VMEM((64, 256), F32),
            pltpu.VMEM((1, 64), F32),
            pltpu.VMEM((1024, 128), F32),
            pltpu.VMEM((1, 128), F32),
            pltpu.VMEM((1, 256), F32),
            pltpu.VMEM((1, 256), F32),
        ),
        in_specs=[anywhere] * 9,
        out_specs=[vmem] * 8,
        scratch_shapes=scratch,
        compiler_params=pltpu.CompilerParams(
            collective_id=0, has_side_effects=True, vmem_limit_bytes=56 * 1024 * 1024
        ),
        cost_estimate=pl.CostEstimate(
            flops=16_000_000_000, bytes_accessed=6_000_000, transcendentals=0
        ),
        name="outer_product_mean",
    )(
        alignment.reshape(1024, 256),
        alignment_mask,
        cotangent,
        scales.reshape(1, 256),
        shifts.reshape(1, 256),
        projection.T,
        offsets.reshape(1, 64),
        readout,
        biases.reshape(1, 128),
    )
    outs = pl.pallas_call(
        finish,
        out_shape=tuple(shape(out.shape, out.dtype) for out in outs),
        in_specs=[vmem] * 8,
        out_specs=[anywhere] * 8,
        scratch_shapes=[pltpu.SemaphoreType.DMA((11,))],
        name="results",
    )(*[pltpu.with_memory_space_constraint(out, pltpu.VMEM) for out in outs])
    return (
        outs[0],
        outs[1].reshape(2, 512, 256),
        outs[2].T,
        outs[3].reshape(64),
        outs[4],
        outs[5].reshape(128),
        outs[6].reshape(256),
        outs[7].reshape(256),
    )


def solution(mesh):
    return jax.shard_map(
        per_device,
        mesh=mesh,
        in_specs=(
            P(("crop", "dap"), None, None),
            P("crop", None),
            P(("crop", "dap"), None, None),
            P(),
            P(),
            P(),
            P(),
            P(),
            P(),
        ),
        out_specs=(
            P(("crop", "dap"), None, None),
            P(("crop", "dap"), None, None),
            P("crop", None),
            P("crop"),
            P("crop", None),
            P("crop"),
            P("crop"),
            P("crop"),
        ),
        check_vma=False,
    )
```

```python
import jax
import jax.numpy as jnp
from jax import lax
from jax.experimental import pallas as pl
from jax.experimental.pallas import tpu as pltpu
from jax.sharding import PartitionSpec as P

F32 = jnp.float32
BF16 = jnp.bfloat16
MESH = pl.DeviceIdType.MESH


def mm(a, b):
    return lax.dot_general(a, b, (((1,), (0,)), ((), ())), preferred_element_type=F32)


def mm_nt(a, b):
    return lax.dot_general(a, b, (((1,), (1,)), ((), ())), preferred_element_type=F32)


def mm_tn(a, b):
    return lax.dot_general(a, b, (((0,), (0,)), ((), ())), preferred_element_type=F32)


def iota(shape, dim):
    return lax.broadcasted_iota(jnp.int32, shape, dim)


def kernel(
    al_h, mask_h, cot, scales_h, shifts_h, proj_h, offs_h, readout_h, biases_h,
    pair_v, al_v, pg_o, og_o, rg_o, bg_o, sg_o, hg_o,
    al, mask, readout, scales, shifts, proj, offs, biases, cot_v,
    mcol, std, inv, normed, both, l_out, l_in, l_f, l_all, l_t, w, ro_f,
    rec, g, perm, perm_t, r_buf, r_k, r_j, t, q,
    d_buf, c_in, s1, x_in, s2, z_in, right_out, right_in,
    lg_f, lg_out, lg_in, rg_l, rg_f, rg_b, ra, rb, rc, re, rh, rk,
    ng_s, pb, pb_core, pb_x, pb_z, pb_half, bsum,
    l_ss, l_rs, e_ss, e_rs, r_ss, r_rs, d_ss, d_rs, a_ss, a_rs, b_ss, b_rs, io,
):
    me = lax.axis_index("dap")
    core = lax.rem(me, 2)
    xx = lax.rem(lax.div(me, 2), 4)
    zz = lax.div(me, 8)
    sign = 1 - 2 * core
    xs, xm, xf = (lax.rem(xx + 4 + sign, 4), lax.rem(xx + 4 - sign, 4), lax.rem(xx + 2, 4))
    zs, zm, zf = (lax.rem(zz + 4 + sign, 4), lax.rem(zz + 4 - sign, 4), lax.rem(zz + 2, 4))
    other = 1 - core

    def dev(z, x, c):
        return (z * 4 + x) * 2 + c

    def slot(x, c, z):
        return (x * 2 + c) * 4 + z

    def slot_dev(s):
        return dev(lax.rem(s, 4), lax.div(s, 8), lax.rem(lax.div(s, 4), 2))

    sib = dev(zz, xx, other)
    mine = slot(xx, core, zz)

    def remote(src, dst, ss, rs, target):
        return pltpu.make_async_remote_copy(
            src_ref=src, dst_ref=dst, send_sem=ss, recv_sem=rs,
            device_id={"dap": target}, device_id_type=MESH,
        )

    barrier = pltpu.get_barrier_semaphore()

    def greet(k, carry):
        pl.semaphore_signal(
            barrier, inc=1, device_id={"dap": lax.rem(me + k, 32)}, device_id_type=MESH
        )
        return carry

    lax.fori_loop(1, 32, greet, 0)
    fetches = [
        pltpu.make_async_copy(src, dst, io.at[n])
        for n, (src, dst) in enumerate((
            (mask_h, mask), (al_h, al), (scales_h, scales), (shifts_h, shifts), (proj_h, proj),
            (offs_h, offs), (cot, cot_v), (readout_h, readout), (biases_h, biases),
        ))
    ]
    for fetch in fetches:
        fetch.start()
    fetches[0].wait()

    mask_f = mask[...].astype(F32)
    mask_t = mask_f.T
    for k in range(2):
        mcol[k * 512:(k + 1) * 512, :] = jnp.sum(
            jnp.where(iota((512, 64), 1) == 2 * me + k, mask_t, 0.0), axis=1, keepdims=True
        )
    for fetch in fetches[1:6]:
        fetch.wait()
    for k in range(2):
        rows = slice(k * 512, (k + 1) * 512)
        wide = al[rows, :].astype(F32)
        center = jnp.mean(wide, axis=-1, keepdims=True)
        apart = wide - center
        spread = jnp.mean(apart * apart, axis=-1, keepdims=True)
        inverse = lax.rsqrt(spread + 1e-05)
        standard = apart * inverse
        std[rows, :] = standard
        inv[rows, :] = inverse
        normed[rows, :] = (standard * scales[...] + shifts[...]).astype(BF16)
    both[...] = (mm_nt(normed[...], proj[...]) + offs[...]) * mcol[...]
    cat = jnp.concatenate([both[0:512, :], both[512:1024, :]], axis=1)
    l_out[...] = cat.astype(BF16).reshape(32, 16, 128)
    cat_t = cat.T
    r_buf[mine] = jnp.concatenate([cat_t[32:64], cat_t[96:128]], axis=0).astype(BF16)

    pl.semaphore_wait(barrier, 31)

    def l_copy(s, k):
        p = slot_dev(s)
        return remote(l_out.at[p], l_in.at[mine], l_ss.at[k], l_rs.at[mine], p)

    for n, x_ in enumerate((xf, xs, xm)):
        for k in range(8):
            l_copy(x_ * 8 + k, n * 8 + k).start()
    for k in range(1, 8):
        l_copy(xx * 8 + lax.rem(core * 4 + zz + k, 8), 24 + k).start()

    def r_send(s, target, k):
        remote(r_buf.at[s], r_buf.at[s], r_ss.at[k], r_rs.at[s], target).start()

    def r_wait(s):
        remote(r_buf.at[s], r_buf.at[s], r_ss.at[0], r_rs.at[s], sib).wait_recv()

    r_send(mine, dev(zs, xx, core), 0)
    r_send(mine, dev(zm, xx, core), 1)
    r_send(mine, dev(zz, xs, core), 2)
    r_send(mine, dev(zz, xm, core), 3)
    r_send(mine, sib, 4)
    l_in[mine] = l_out[me]

    mask_b = mask_f.astype(BF16)
    own_cols = (iota((512, 16), 0) == 16 * me + iota((512, 16), 1)).astype(F32).astype(BF16)
    mask_own = mm(mask_b, own_cols).astype(BF16)
    recip = 1.0 / (0.001 + mm(mask_t.astype(BF16), mask_own))
    total = jnp.zeros((1, 128), F32)
    fetches[6].wait()
    for i in range(16):
        rec_i = jnp.broadcast_to(recip[:, i:i + 1], (512, 128))
        rec[i] = rec_i
        sg = (cot_v[i].astype(F32) * rec_i).astype(BF16)
        g[:, i * 128:(i + 1) * 128] = sg
        total = total + jnp.sum(sg.astype(F32), axis=0, keepdims=True)
    bsum[...] = total

    fetches[7].wait()
    fetches[8].wait()
    ro_f[...] = readout[...].astype(F32)
    for d in range(32):
        w[:, d * 128:(d + 1) * 128] = ro_f[pl.ds(d, 32, stride=32), :].astype(BF16)

    def packed(a):
        return lax.rem(a, 8) * 64 + lax.rem(lax.div(a, 8), 2) * 32 + lax.div(a, 16)

    perm[...] = (iota((512, 512), 1) == packed(iota((512, 512), 0))).astype(F32).astype(BF16)
    perm_t[...] = (iota((512, 512), 0) == packed(iota((512, 512), 1))).astype(F32).astype(BF16)

    def t_group(x_, own=False):
        for k in range(1 if own else 0, 8):
            s = x_ * 8 + (lax.rem(core * 4 + zz + k, 8) if own else k)
            remote(l_out.at[0], l_in.at[s], l_ss.at[0], l_rs.at[s], sib).wait_recv()
        l_f[...] = l_in[pl.ds(x_ * 8, 8)].reshape(128, 128).astype(F32)
        for i in range(16):
            part = l_f[pl.ds(i, 8, stride=16), :]
            l_all[x_, i] = jnp.concatenate([part[:, 0:32], part[:, 64:96]], axis=0).astype(BF16)
        rows = l_all[x_].reshape(256, 32)
        l_t[x_] = rows.astype(F32).T.astype(BF16)
        r = mm(rows, w[...]).astype(BF16)
        for d in range(32):
            t[x_, :, d] = r[:, d * 128:(d + 1) * 128].reshape(16, 16, 128)

    def d_group(x_, n):
        rows = jnp.concatenate([t[x_, i].reshape(512, 128) for i in range(16)], axis=1)
        raw = mm_nt(rows, g[...]).astype(BF16)
        for h in range(2):
            d_buf[x_, h] = raw[:, h * 256:(h + 1) * 256]
        remote(d_buf.at[x_, other], c_in.at[x_], d_ss.at[n], d_rs.at[x_], sib).start()

    def c_wait(x_, n):
        remote(d_buf.at[x_, other], c_in.at[x_], d_ss.at[n], d_rs.at[x_], sib).wait_recv()

    def core_sum(x_):
        return d_buf[x_, core].astype(F32) + c_in[x_].astype(F32)

    def x_copy(x_, n, target_x):
        return remote(
            s1.at[x_], x_in.at[n], d_ss.at[4 + n], d_rs.at[4 + n], dev(zz, target_x, core)
        )

    r_wait(slot(xx, core, zm))
    r_send(slot(xx, core, zm), dev(zs, xx, core), 5)
    for n, z_ in enumerate((zm, zs)):
        if n == 1:
            r_wait(slot(xx, core, z_))
        r_send(slot(xx, core, z_), dev(zz, xs, core), 6 + 3 * n)
        r_send(slot(xx, core, z_), dev(zz, xm, core), 7 + 3 * n)
        r_send(slot(xx, core, z_), sib, 8 + 3 * n)
    t_group(xf)
    r_wait(slot(xm, core, zz))
    r_send(slot(xm, core, zz), dev(zz, xs, core), 15)
    r_send(slot(xm, core, zz), sib, 16)
    r_wait(slot(xs, core, zz))
    r_send(slot(xs, core, zz), sib, 17)
    d_group(xf, 0)
    t_group(xm)
    r_wait(slot(xx, core, zf))
    r_send(slot(xx, core, zf), dev(zz, xs, core), 12)
    r_send(slot(xx, core, zf), dev(zz, xm, core), 13)
    r_send(slot(xx, core, zf), sib, 14)
    d_group(xm, 1)
    c_wait(xf, 0)
    s1[xf] = core_sum(xf).astype(BF16)
    x_copy(xf, 0, xs).start()
    for n, z_ in enumerate((zm, zs)):
        r_wait(slot(xm, core, z_))
        r_send(slot(xm, core, z_), dev(zz, xs, core), 18 + 3 * n)
        r_send(slot(xm, core, z_), sib, 19 + 3 * n)
        r_wait(slot(xs, core, z_))
        r_send(slot(xs, core, z_), sib, 20 + 3 * n)
    t_group(xs)
    d_group(xs, 2)
    c_wait(xm, 1)
    s1[xm] = core_sum(xm).astype(BF16)
    x_copy(xm, 1, xm).start()
    r_wait(slot(xf, core, zz))
    r_send(slot(xf, core, zz), sib, 27)
    t_group(xx, own=True)
    r_wait(slot(xm, core, zf))
    r_send(slot(xm, core, zf), dev(zz, xs, core), 24)
    r_send(slot(xm, core, zf), sib, 25)
    r_wait(slot(xs, core, zf))
    r_send(slot(xs, core, zf), sib, 26)
    d_group(xx, 3)

    def r_prep(x_):
        for z_ in range(4):
            r_wait(slot(x_, other, z_))
        raw = r_buf[pl.ds(x_ * 8, 8)].reshape(512, 512)
        moved = mm(perm[...], raw)
        r_k[...] = moved.astype(BF16)
        r_j[:, pl.ds(pl.multiple_of(x_ * 512, 512), 512)] = moved.T.astype(BF16)

    def e_copy(s, k):
        return remote(lg_out.at[s], lg_in.at[me], e_ss.at[k], e_rs.at[me], slot_dev(s))

    def q_group(x_):
        for h in range(2):
            block = mm(r_k[...], g[:, h * 1024:(h + 1) * 1024]).astype(BF16)
            for i in range(8):
                q[x_, h * 8 + i] = block[:, i * 128:(i + 1) * 128].reshape(32, 16, 128)

    def lg_group(x_, n):
        rows = jnp.concatenate([q[x_, :, d].reshape(256, 128) for d in range(32)], axis=1)
        lg_f[:, 0:32] = mm_nt(rows, w[...])
        for c in range(8):
            pieces = [lg_f[pl.ds(c + 8 * k, 16, stride=16), :][:, 0:32] for k in range(2)]
            pieces.append(jnp.zeros((16, 64), F32))
            lg_out[x_ * 8 + c] = jnp.concatenate(pieces, axis=1).astype(BF16)
        if n == 0:
            for k in range(1, 8):
                e_copy(x_ * 8 + lax.rem(core * 4 + zz + k, 8), k).start()
            lg_in[me] = lg_out[mine]
        else:
            for k in range(8):
                e_copy(x_ * 8 + k, n * 8 + k).start()

    def z_copy(k):
        z_ = lax.rem(zz + k, 4)
        return remote(
            s2.at[z_], z_in.at[zz], d_ss.at[6 + k], d_rs.at[7 + zz], dev(z_, xx, core)
        )

    def rg_group(x_, n):
        rows = jnp.concatenate([q[x_, :, d].reshape(256, 128) for d in range(32)], axis=1)
        part = mm(l_t[x_], rows)
        rg_l[...] = part if n == 0 else rg_l[...] + part

    r_prep(xx)
    q_group(xx)
    c_wait(xs, 2)
    x_copy(xf, 0, xs).wait_recv()
    s1[xs] = (core_sum(xs) + x_in[0].astype(F32)).astype(BF16)
    x_copy(xs, 2, xs).start()
    for n, z_ in enumerate((zm, zs)):
        r_wait(slot(xf, core, z_))
        r_send(slot(xf, core, z_), sib, 28 + n)
    lg_group(xx, 0)
    rg_group(xx, 0)
    r_wait(slot(xf, core, zf))
    r_send(slot(xf, core, zf), sib, 30)
    r_prep(xm)
    q_group(xm)
    lg_group(xm, 1)
    rg_group(xm, 1)
    r_prep(xs)
    q_group(xs)
    c_wait(xx, 3)
    x_copy(xm, 1, xm).wait_recv()
    x_copy(xs, 2, xs).wait_recv()
    own_sum = (core_sum(xx) + x_in[1].astype(F32) + x_in[2].astype(F32)).astype(BF16)
    own_rows = mm(perm_t[...], own_sum).astype(BF16).reshape(2, 4, 64, 256)
    for c in range(2):
        s2[:, c] = own_rows[c]
    for k in range(1, 4):
        z_copy(k).start()
    lg_group(xs, 2)
    rg_group(xs, 2)
    r_prep(xf)
    q_group(xf)

    rg_group(xf, 3)
    for d in range(32):
        rg_f[pl.ds(d, 32, stride=32), :] = rg_l[:, d * 128:(d + 1) * 128]
    rg_b[...] = rg_f[...].astype(BF16).reshape(2, 512, 128)
    a0 = remote(rg_b.at[other], ra, a_ss.at[0], a_rs.at[0], sib)
    a0.start()
    lg_group(xf, 3)

    def u_step(ib):
        cols = jnp.concatenate(
            [t[:, ib * 4 + ii].reshape(2048, 128) for ii in range(4)], axis=1
        )
        acc = mm(r_j[...], cols)
        for ii in range(4):
            pair_v[4 * ib + ii] = (
                (acc[:, ii * 128:(ii + 1) * 128] + biases[...]) * rec[4 * ib + ii]
            ).astype(BF16)

    u_step(0)
    a0.wait_recv()
    rb[...] = (rg_b[core].astype(F32) + ra[...].astype(F32)).astype(BF16).reshape(4, 128, 128)

    def a_x(k):
        x_ = lax.rem(xx + k, 4)
        return remote(rb.at[x_], rc.at[xx], a_ss.at[k], a_rs.at[1 + xx], dev(zz, x_, core))

    for k in range(1, 4):
        a_x(k).start()
    rc[xx] = rb[xx]
    u_step(1)

    for k in range(1, 4):
        z_ = lax.rem(zz + k, 4)
        remote(s2.at[z_], z_in.at[z_], d_ss.at[6 + k], d_rs.at[7 + z_], sib).wait_recv()
    z_in[zz] = s2[zz]
    right_out[...] = (
        (z_in[0].astype(F32) + z_in[1].astype(F32))
        + (z_in[2].astype(F32) + z_in[3].astype(F32))
    ).astype(BF16)
    f_copy = remote(right_out.at[other], right_in.at[core], d_ss.at[10], d_rs.at[11], sib)
    f_copy.start()
    right_in[core] = right_out[core]
    for k in range(1, 32):
        p = lax.rem(me + k, 32)
        remote(lg_out.at[0], lg_in.at[p], e_ss.at[k], e_rs.at[p], sib).wait_recv()
    remote(
        right_out.at[other], right_in.at[other], d_ss.at[10], d_rs.at[11], sib
    ).wait_recv()
    right_t = jnp.concatenate(
        [right_in[0].astype(F32).T, right_in[1].astype(F32).T], axis=0
    )
    left = lg_in[...].reshape(512, 128).astype(F32)
    for k in range(2):
        both[k * 512:(k + 1) * 512, :] = jnp.concatenate(
            [left[:, k * 32:(k + 1) * 32], right_t[:, k * 32:(k + 1) * 32]], axis=1
        ) * mcol[k * 512:(k + 1) * 512, :]
    pgb = both[...].astype(BF16)
    pj_acc = mm_tn(pgb, normed[...])
    of_acc = jnp.sum(pgb.astype(F32), axis=0, keepdims=True)
    ng_s[...] = mm(pgb, proj[...])
    sc_acc = jnp.sum(ng_s[...] * std[...], axis=0, keepdims=True)
    sh_acc = jnp.sum(ng_s[...], axis=0, keepdims=True)
    pb[0] = pj_acc[0:48].astype(BF16)
    pb[1] = jnp.concatenate(
        [
            pj_acc[48:64], sc_acc, sh_acc,
            jnp.concatenate([of_acc, jnp.zeros((1, 64), F32), bsum[...]], axis=1),
            jnp.zeros((29, 256), F32),
        ],
        axis=0,
    ).astype(BF16)
    b0 = remote(pb.at[other], pb_core, b_ss.at[0], b_rs.at[0], sib)
    b0.start()

    for k in range(1, 4):
        x_ = lax.rem(xx + k, 4)
        remote(rb.at[x_], rc.at[x_], a_ss.at[k], a_rs.at[1 + x_], sib).wait_recv()

    def four(ref):
        return (ref[0].astype(F32) + ref[1].astype(F32)) + (
            ref[2].astype(F32) + ref[3].astype(F32)
        )

    re[zz] = four(rc).astype(BF16)

    def a_z(k):
        z_ = lax.rem(zz + k, 4)
        return remote(re.at[zz], re.at[zz], a_ss.at[3 + k], a_rs.at[5 + zz], dev(z_, xx, core))

    for k in range(1, 4):
        a_z(k).start()

    b0.wait_recv()
    pb_x[xx] = (pb[core].astype(F32) + pb_core[...].astype(F32)).astype(BF16)

    def b_x(k):
        x_ = lax.rem(xx + k, 4)
        return remote(pb_x.at[xx], pb_x.at[xx], b_ss.at[k], b_rs.at[1 + xx], dev(zz, x_, core))

    for k in range(1, 4):
        b_x(k).start()

    for b in range(4):
        rows = slice(b * 256, (b + 1) * 256)
        h = ng_s[rows, :] * scales[...]
        standard = std[rows, :]
        m1 = jnp.mean(h, axis=-1, keepdims=True)
        m2 = jnp.mean(h * standard, axis=-1, keepdims=True)
        al_v[rows, :] = ((h - m1 - standard * m2) * inv[rows, :]).astype(BF16)
    u_step(2)

    for k in range(1, 4):
        z_ = lax.rem(zz + k, 4)
        remote(re.at[z_], re.at[z_], a_ss.at[3 + k], a_rs.at[5 + z_], sib).wait_recv()
    rh[xx] = four(re).astype(BF16)

    def a_g(k):
        x_ = lax.rem(xx + k, 4)
        return remote(rh.at[xx], rh.at[xx], a_ss.at[6 + k], a_rs.at[9 + xx], dev(zz, x_, core))

    for k in range(1, 4):
        a_g(k).start()

    for k in range(1, 4):
        x_ = lax.rem(xx + k, 4)
        remote(pb_x.at[x_], pb_x.at[x_], b_ss.at[k], b_rs.at[1 + x_], sib).wait_recv()
    pb_z[zz] = four(pb_x).astype(BF16)

    def b_z(k):
        z_ = lax.rem(zz + k, 4)
        return remote(
            pb_z.at[zz], pb_z.at[zz], b_ss.at[3 + k], b_rs.at[5 + zz], dev(z_, xx, core)
        )

    for k in range(1, 4):
        b_z(k).start()
    u_step(3)

    for k in range(1, 4):
        x_ = lax.rem(xx + k, 4)
        remote(rh.at[x_], rh.at[x_], a_ss.at[6 + k], a_rs.at[9 + x_], sib).wait_recv()
    a_last = remote(rh, rk, a_ss.at[10], a_rs.at[13], sib)
    a_last.start()
    rg_o[pl.ds(pl.multiple_of(core * 512, 512), 512), :] = rh[...].reshape(512, 128).astype(F32)

    for k in range(1, 4):
        z_ = lax.rem(zz + k, 4)
        remote(pb_z.at[z_], pb_z.at[z_], b_ss.at[3 + k], b_rs.at[5 + z_], sib).wait_recv()
    pb_half[core] = four(pb_z).astype(BF16)
    b_last = remote(pb_half.at[core], pb_half.at[core], b_ss.at[7], b_rs.at[9], sib)
    b_last.start()

    def drain(k, carry):
        remote(lg_out.at[0], lg_in.at[0], e_ss.at[k], e_rs.at[0], sib).wait_send()
        remote(r_buf.at[0], r_buf.at[0], r_ss.at[k - 1], r_rs.at[0], sib).wait_send()
        return carry

    lax.fori_loop(1, 32, drain, 0)
    for k in range(32):
        if k != 24:
            remote(l_out.at[0], l_in.at[0], l_ss.at[k], l_rs.at[0], sib).wait_send()
    for n, x_ in enumerate((xf, xm, xs, xx)):
        remote(d_buf.at[x_, other], c_in.at[x_], d_ss.at[n], d_rs.at[x_], sib).wait_send()
    x_copy(xf, 0, xs).wait_send()
    x_copy(xm, 1, xm).wait_send()
    x_copy(xs, 2, xs).wait_send()
    a0.wait_send()
    b0.wait_send()
    f_copy.wait_send()
    for k in range(1, 4):
        z_copy(k).wait_send()
        a_x(k).wait_send()
        a_z(k).wait_send()
        a_g(k).wait_send()
        b_x(k).wait_send()
        b_z(k).wait_send()
    a_last.wait()
    rg_o[pl.ds(pl.multiple_of(other * 512, 512), 512), :] = rk[...].reshape(512, 128).astype(F32)
    remote(
        pb_half.at[other], pb_half.at[other], b_ss.at[7], b_rs.at[9], sib
    ).wait_recv()
    b_last.wait_send()
    pg_o[...] = jnp.concatenate([pb_half[0], pb_half[1, 0:16]], axis=0).astype(F32)
    vec = pb_half[1, 16:32].astype(F32)
    sg_o[...] = vec[0:1, :]
    hg_o[...] = vec[1:2, :]
    og_o[...] = vec[2:3, 0:64]
    bg_o[...] = vec[2:3, 128:256]


def finish(*refs):
    srcs, dsts, sems = refs[0:8], refs[8:16], refs[16]
    copies = [
        pltpu.make_async_copy(srcs[0].at[pl.ds(4 * n, 4)], dsts[0].at[pl.ds(4 * n, 4)], sems.at[n])
        for n in range(4)
    ]
    copies += [pltpu.make_async_copy(srcs[n], dsts[n], sems.at[3 + n]) for n in range(1, 8)]
    for copy in copies:
        copy.start()
    for copy in copies:
        copy.wait()


def per_device(
    alignment, alignment_mask, cotangent, scales, shifts, projection, offsets, readout, biases
):
    vmem = pl.BlockSpec(memory_space=pltpu.VMEM)
    shape = jax.ShapeDtypeStruct
    sizes = dict(
        al=((1024, 256), BF16),
        mask=((64, 512), jnp.int32),
        readout=((1024, 128), BF16),
        scales=((1, 256), F32),
        shifts=((1, 256), F32),
        proj=((64, 256), BF16),
        offs=((1, 64), F32),
        biases=((1, 128), F32),
        cot_v=((16, 512, 128), BF16),
        mcol=((1024, 1), F32),
        std=((1024, 256), F32),
        inv=((1024, 1), F32),
        normed=((1024, 256), BF16),
        both=((1024, 64), F32),
        l_out=((32, 16, 128), BF16),
        l_in=((32, 16, 128), BF16),
        l_f=((128, 128), F32),
        l_all=((4, 16, 16, 32), BF16),
        l_t=((4, 32, 256), BF16),
        w=((32, 4096), BF16),
        ro_f=((1024, 128), F32),
        rec=((16, 512, 128), F32),
        g=((512, 2048), BF16),
        perm=((512, 512), BF16),
        perm_t=((512, 512), BF16),
        r_buf=((32, 64, 512), BF16),
        r_k=((512, 512), BF16),
        r_j=((512, 2048), BF16),
        t=((4, 16, 32, 16, 128), BF16),
        q=((4, 16, 32, 16, 128), BF16),
        d_buf=((4, 2, 512, 256), BF16),
        c_in=((4, 512, 256), BF16),
        s1=((4, 512, 256), BF16),
        x_in=((3, 512, 256), BF16),
        s2=((4, 2, 64, 256), BF16),
        z_in=((4, 2, 64, 256), BF16),
        right_out=((2, 64, 256), BF16),
        right_in=((2, 64, 256), BF16),
        lg_f=((256, 128), F32),
        lg_out=((32, 16, 128), BF16),
        lg_in=((32, 16, 128), BF16),
        rg_l=((32, 4096), F32),
        rg_f=((1024, 128), F32),
        rg_b=((2, 512, 128), BF16),
        ra=((512, 128), BF16),
        rb=((4, 128, 128), BF16),
        rc=((4, 128, 128), BF16),
        re=((4, 128, 128), BF16),
        rh=((4, 128, 128), BF16),
        rk=((4, 128, 128), BF16),
        ng_s=((1024, 256), F32),
        pb=((2, 48, 256), BF16),
        pb_core=((48, 256), BF16),
        pb_x=((4, 48, 256), BF16),
        pb_z=((4, 48, 256), BF16),
        pb_half=((2, 48, 256), BF16),
        bsum=((1, 128), F32),
    )
    scratch = [pltpu.VMEM(*size) for size in sizes.values()] + [
        pltpu.SemaphoreType.DMA((n,)) for n in (32, 32, 32, 32, 31, 32, 11, 12, 11, 14, 8, 10, 9)
    ]
    anywhere = pl.BlockSpec(memory_space=pl.ANY)
    outs = pl.pallas_call(
        kernel,
        out_shape=(
            pltpu.VMEM((16, 512, 128), BF16),
            pltpu.VMEM((1024, 256), BF16),
            pltpu.VMEM((64, 256), F32),
            pltpu.VMEM((1, 64), F32),
            pltpu.VMEM((1024, 128), F32),
            pltpu.VMEM((1, 128), F32),
            pltpu.VMEM((1, 256), F32),
            pltpu.VMEM((1, 256), F32),
        ),
        in_specs=[anywhere] * 9,
        out_specs=[vmem] * 8,
        scratch_shapes=scratch,
        compiler_params=pltpu.CompilerParams(
            collective_id=0, has_side_effects=True, vmem_limit_bytes=56 * 1024 * 1024
        ),
        cost_estimate=pl.CostEstimate(
            flops=16_000_000_000, bytes_accessed=6_000_000, transcendentals=0
        ),
        name="outer_product_mean",
    )(
        alignment.reshape(1024, 256),
        alignment_mask,
        cotangent,
        scales.reshape(1, 256),
        shifts.reshape(1, 256),
        projection.T,
        offsets.reshape(1, 64),
        readout,
        biases.reshape(1, 128),
    )
    outs = pl.pallas_call(
        finish,
        out_shape=tuple(shape(out.shape, out.dtype) for out in outs),
        in_specs=[vmem] * 8,
        out_specs=[anywhere] * 8,
        scratch_shapes=[pltpu.SemaphoreType.DMA((11,))],
        name="results",
    )(*[pltpu.with_memory_space_constraint(out, pltpu.VMEM) for out in outs])
    return (
        outs[0],
        outs[1].reshape(2, 512, 256),
        outs[2].T,
        outs[3].reshape(64),
        outs[4],
        outs[5].reshape(128),
        outs[6].reshape(256),
        outs[7].reshape(256),
    )


def solution(mesh):
    return jax.shard_map(
        per_device,
        mesh=mesh,
        in_specs=(
            P(("crop", "dap"), None, None),
            P("crop", None),
            P(("crop", "dap"), None, None),
            P(),
            P(),
            P(),
            P(),
            P(),
            P(),
        ),
        out_specs=(
            P(("crop", "dap"), None, None),
            P(("crop", "dap"), None, None),
            P("crop", None),
            P("crop"),
            P("crop", None),
            P("crop"),
            P("crop"),
            P("crop"),
        ),
        check_vma=False,
    )
```

```python
import jax
import jax.numpy as jnp
from jax import lax
from jax.experimental import pallas as pl
from jax.experimental.pallas import tpu as pltpu
from jax.sharding import PartitionSpec as P

F32 = jnp.float32
BF16 = jnp.bfloat16
MESH = pl.DeviceIdType.MESH


def mm(a, b):
    return lax.dot_general(a, b, (((1,), (0,)), ((), ())), preferred_element_type=F32)


def mm_nt(a, b):
    return lax.dot_general(a, b, (((1,), (1,)), ((), ())), preferred_element_type=F32)


def mm_tn(a, b):
    return lax.dot_general(a, b, (((0,), (0,)), ((), ())), preferred_element_type=F32)


def iota(shape, dim):
    return lax.broadcasted_iota(jnp.int32, shape, dim)


def kernel(
    al_h, mask_h, cot, scales_h, shifts_h, proj_h, offs_h, readout_h, biases_h,
    pair_v, al_v, pg_o, og_o, rg_o, bg_o, sg_o, hg_o,
    al, mask, readout, scales, shifts, proj, offs, biases, cot_v,
    mcol, std, inv, normed, both, l_out, l_in, l_f, l_all, l_t, w, ro_f,
    rec, g, perm, perm_t, r_buf, r_k, r_j, t, q,
    d_buf, c_in, s1, x_in, s2, z_in, right_out, right_in,
    lg_f, lg_out, lg_in, rg_l, rg_f, rg_b, ra, rb, rc, re, rh, rk,
    ng_s, pb, pb_core, pb_x, pb_z, pb_half, bsum,
    l_ss, l_rs, e_ss, e_rs, r_ss, r_rs, d_ss, d_rs, a_ss, a_rs, b_ss, b_rs, io,
):
    me = lax.axis_index("dap")
    core = lax.rem(me, 2)
    xx = lax.rem(lax.div(me, 2), 4)
    zz = lax.div(me, 8)
    sign = 1 - 2 * core
    xs, xm, xf = (lax.rem(xx + 4 + sign, 4), lax.rem(xx + 4 - sign, 4), lax.rem(xx + 2, 4))
    zs, zm, zf = (lax.rem(zz + 4 + sign, 4), lax.rem(zz + 4 - sign, 4), lax.rem(zz + 2, 4))
    other = 1 - core

    def dev(z, x, c):
        return (z * 4 + x) * 2 + c

    def slot(x, c, z):
        return (x * 2 + c) * 4 + z

    def slot_dev(s):
        return dev(lax.rem(s, 4), lax.div(s, 8), lax.rem(lax.div(s, 4), 2))

    sib = dev(zz, xx, other)
    mine = slot(xx, core, zz)

    def remote(src, dst, ss, rs, target):
        return pltpu.make_async_remote_copy(
            src_ref=src, dst_ref=dst, send_sem=ss, recv_sem=rs,
            device_id={"dap": target}, device_id_type=MESH,
        )

    barrier = pltpu.get_barrier_semaphore()

    def greet(k, carry):
        pl.semaphore_signal(
            barrier, inc=1, device_id={"dap": lax.rem(me + k, 32)}, device_id_type=MESH
        )
        return carry

    lax.fori_loop(1, 32, greet, 0)
    fetches = [
        pltpu.make_async_copy(src, dst, io.at[n])
        for n, (src, dst) in enumerate((
            (mask_h, mask), (al_h, al), (scales_h, scales), (shifts_h, shifts), (proj_h, proj),
            (offs_h, offs), (cot, cot_v), (readout_h, readout), (biases_h, biases),
        ))
    ]
    for fetch in fetches:
        fetch.start()
    fetches[0].wait()

    mask_f = mask[...].astype(F32)
    mask_t = mask_f.T
    for k in range(2):
        mcol[k * 512:(k + 1) * 512, :] = jnp.sum(
            jnp.where(iota((512, 64), 1) == 2 * me + k, mask_t, 0.0), axis=1, keepdims=True
        )
    for fetch in fetches[1:6]:
        fetch.wait()
    for k in range(2):
        rows = slice(k * 512, (k + 1) * 512)
        wide = al[rows, :].astype(F32)
        center = jnp.mean(wide, axis=-1, keepdims=True)
        apart = wide - center
        spread = jnp.mean(apart * apart, axis=-1, keepdims=True)
        inverse = lax.rsqrt(spread + 1e-05)
        standard = apart * inverse
        std[rows, :] = standard
        inv[rows, :] = inverse
        normed[rows, :] = (standard * scales[...] + shifts[...]).astype(BF16)
    both[...] = (mm_nt(normed[...], proj[...]) + offs[...]) * mcol[...]
    cat = jnp.concatenate([both[0:512, :], both[512:1024, :]], axis=1)
    l_out[...] = cat.astype(BF16).reshape(32, 16, 128)
    cat_t = cat.T
    r_buf[mine] = jnp.concatenate([cat_t[32:64], cat_t[96:128]], axis=0).astype(BF16)

    pl.semaphore_wait(barrier, 31)

    def l_copy(s, k):
        p = slot_dev(s)
        return remote(l_out.at[p], l_in.at[mine], l_ss.at[k], l_rs.at[mine], p)

    def r_send(s, target, k):
        remote(r_buf.at[s], r_buf.at[s], r_ss.at[k], r_rs.at[s], target).start()

    def r_wait(s):
        remote(r_buf.at[s], r_buf.at[s], r_ss.at[0], r_rs.at[s], sib).wait_recv()

    for k in range(8):
        l_copy(xf * 8 + k, k).start()
    r_send(mine, dev(zs, xx, core), 0)
    r_send(mine, dev(zm, xx, core), 1)
    r_send(mine, dev(zz, xs, core), 2)
    r_send(mine, dev(zz, xm, core), 3)
    r_send(mine, sib, 4)
    for n, x_ in ((1, xs), (2, xm)):
        for k in range(8):
            l_copy(x_ * 8 + k, n * 8 + k).start()
    for k in range(1, 8):
        l_copy(xx * 8 + lax.rem(core * 4 + zz + k, 8), 24 + k).start()
    l_in[mine] = l_out[me]

    mask_b = mask_f.astype(BF16)
    own_cols = (iota((512, 16), 0) == 16 * me + iota((512, 16), 1)).astype(F32).astype(BF16)
    mask_own = mm(mask_b, own_cols).astype(BF16)
    recip = 1.0 / (0.001 + mm(mask_t.astype(BF16), mask_own))
    total = jnp.zeros((1, 128), F32)
    fetches[6].wait()
    for i in range(16):
        rec_i = jnp.broadcast_to(recip[:, i:i + 1], (512, 128))
        rec[i] = rec_i
        sg = (cot_v[i].astype(F32) * rec_i).astype(BF16)
        g[:, i * 128:(i + 1) * 128] = sg
        total = total + jnp.sum(sg.astype(F32), axis=0, keepdims=True)
    bsum[...] = total

    fetches[7].wait()
    fetches[8].wait()
    ro_f[...] = readout[...].astype(F32)
    for d in range(32):
        w[:, d * 128:(d + 1) * 128] = ro_f[pl.ds(d, 32, stride=32), :].astype(BF16)

    def packed(a):
        return lax.rem(a, 8) * 64 + lax.rem(lax.div(a, 8), 2) * 32 + lax.div(a, 16)

    perm[...] = (iota((512, 512), 1) == packed(iota((512, 512), 0))).astype(F32).astype(BF16)
    perm_t[...] = (iota((512, 512), 0) == packed(iota((512, 512), 1))).astype(F32).astype(BF16)

    def t_group(x_, own=False):
        for k in range(1 if own else 0, 8):
            s = x_ * 8 + (lax.rem(core * 4 + zz + k, 8) if own else k)
            remote(l_out.at[0], l_in.at[s], l_ss.at[0], l_rs.at[s], sib).wait_recv()
        l_f[...] = l_in[pl.ds(x_ * 8, 8)].reshape(128, 128).astype(F32)
        for i in range(16):
            part = l_f[pl.ds(i, 8, stride=16), :]
            l_all[x_, i] = jnp.concatenate([part[:, 0:32], part[:, 64:96]], axis=0).astype(BF16)
        rows = l_all[x_].reshape(256, 32)
        l_t[x_] = rows.astype(F32).T.astype(BF16)
        r = mm(rows, w[...]).astype(BF16)
        for d in range(32):
            t[x_, :, d] = r[:, d * 128:(d + 1) * 128].reshape(16, 16, 128)

    def d_group(x_, n):
        rows = jnp.concatenate([t[x_, i].reshape(512, 128) for i in range(16)], axis=1)
        raw = mm_nt(rows, g[...]).astype(BF16)
        for h in range(2):
            d_buf[x_, h] = raw[:, h * 256:(h + 1) * 256]
        remote(d_buf.at[x_, other], c_in.at[x_], d_ss.at[n], d_rs.at[x_], sib).start()

    def c_wait(x_, n):
        remote(d_buf.at[x_, other], c_in.at[x_], d_ss.at[n], d_rs.at[x_], sib).wait_recv()

    def core_sum(x_):
        return d_buf[x_, core].astype(F32) + c_in[x_].astype(F32)

    def x_copy(x_, n, target_x):
        return remote(
            s1.at[x_], x_in.at[n], d_ss.at[4 + n], d_rs.at[4 + n], dev(zz, target_x, core)
        )

    r_wait(slot(xx, core, zm))
    r_send(slot(xx, core, zm), dev(zs, xx, core), 5)
    for n, z_ in enumerate((zm, zs)):
        if n == 1:
            r_wait(slot(xx, core, z_))
        r_send(slot(xx, core, z_), dev(zz, xs, core), 6 + 3 * n)
        r_send(slot(xx, core, z_), dev(zz, xm, core), 7 + 3 * n)
        r_send(slot(xx, core, z_), sib, 8 + 3 * n)
    t_group(xf)
    r_wait(slot(xm, core, zz))
    r_send(slot(xm, core, zz), dev(zz, xs, core), 15)
    r_send(slot(xm, core, zz), sib, 16)
    r_wait(slot(xs, core, zz))
    r_send(slot(xs, core, zz), sib, 17)
    d_group(xf, 0)
    t_group(xm)
    r_wait(slot(xx, core, zf))
    r_send(slot(xx, core, zf), dev(zz, xs, core), 12)
    r_send(slot(xx, core, zf), dev(zz, xm, core), 13)
    r_send(slot(xx, core, zf), sib, 14)
    d_group(xm, 1)
    c_wait(xf, 0)
    s1[xf] = core_sum(xf).astype(BF16)
    x_copy(xf, 0, xs).start()
    for n, z_ in enumerate((zm, zs)):
        r_wait(slot(xm, core, z_))
        r_send(slot(xm, core, z_), dev(zz, xs, core), 18 + 3 * n)
        r_send(slot(xm, core, z_), sib, 19 + 3 * n)
        r_wait(slot(xs, core, z_))
        r_send(slot(xs, core, z_), sib, 20 + 3 * n)
    t_group(xs)
    d_group(xs, 2)
    c_wait(xm, 1)
    s1[xm] = core_sum(xm).astype(BF16)
    x_copy(xm, 1, xm).start()
    r_wait(slot(xf, core, zz))
    r_send(slot(xf, core, zz), sib, 27)
    t_group(xx, own=True)
    r_wait(slot(xm, core, zf))
    r_send(slot(xm, core, zf), dev(zz, xs, core), 24)
    r_send(slot(xm, core, zf), sib, 25)
    r_wait(slot(xs, core, zf))
    r_send(slot(xs, core, zf), sib, 26)
    d_group(xx, 3)

    def r_prep(x_):
        for z_ in range(4):
            r_wait(slot(x_, other, z_))
        raw = r_buf[pl.ds(x_ * 8, 8)].reshape(512, 512)
        moved = mm(perm[...], raw)
        r_k[...] = moved.astype(BF16)
        r_j[:, pl.ds(pl.multiple_of(x_ * 512, 512), 512)] = moved.T.astype(BF16)

    def e_copy(s, k):
        return remote(lg_out.at[s], lg_in.at[me], e_ss.at[k], e_rs.at[me], slot_dev(s))

    def q_group(x_):
        for h in range(2):
            block = mm(r_k[...], g[:, h * 1024:(h + 1) * 1024]).astype(BF16)
            for i in range(8):
                q[x_, h * 8 + i] = block[:, i * 128:(i + 1) * 128].reshape(32, 16, 128)

    def lg_group(x_, n):
        rows = jnp.concatenate([q[x_, :, d].reshape(256, 128) for d in range(32)], axis=1)
        lg_f[:, 0:32] = mm_nt(rows, w[...])
        for c in range(8):
            pieces = [lg_f[pl.ds(c + 8 * k, 16, stride=16), :][:, 0:32] for k in range(2)]
            pieces.append(jnp.zeros((16, 64), F32))
            lg_out[x_ * 8 + c] = jnp.concatenate(pieces, axis=1).astype(BF16)
        if n == 0:
            for k in range(1, 8):
                e_copy(x_ * 8 + lax.rem(core * 4 + zz + k, 8), k).start()
            lg_in[me] = lg_out[mine]
        else:
            for k in range(8):
                e_copy(x_ * 8 + k, n * 8 + k).start()

    def z_copy(k):
        z_ = lax.rem(zz + k, 4)
        return remote(
            s2.at[z_], z_in.at[zz], d_ss.at[6 + k], d_rs.at[7 + zz], dev(z_, xx, core)
        )

    def rg_group(x_, n):
        rows = jnp.concatenate([q[x_, :, d].reshape(256, 128) for d in range(32)], axis=1)
        part = mm(l_t[x_], rows)
        rg_l[...] = part if n == 0 else rg_l[...] + part

    r_prep(xx)
    q_group(xx)
    c_wait(xs, 2)
    x_copy(xf, 0, xs).wait_recv()
    s1[xs] = (core_sum(xs) + x_in[0].astype(F32)).astype(BF16)
    x_copy(xs, 2, xs).start()
    for n, z_ in enumerate((zm, zs)):
        r_wait(slot(xf, core, z_))
        r_send(slot(xf, core, z_), sib, 28 + n)
    lg_group(xx, 0)
    rg_group(xx, 0)
    r_wait(slot(xf, core, zf))
    r_send(slot(xf, core, zf), sib, 30)
    r_prep(xm)
    q_group(xm)
    lg_group(xm, 1)
    rg_group(xm, 1)
    r_prep(xs)
    q_group(xs)
    c_wait(xx, 3)
    x_copy(xm, 1, xm).wait_recv()
    x_copy(xs, 2, xs).wait_recv()
    own_sum = (core_sum(xx) + x_in[1].astype(F32) + x_in[2].astype(F32)).astype(BF16)
    own_rows = mm(perm_t[...], own_sum).astype(BF16).reshape(2, 4, 64, 256)
    for c in range(2):
        s2[:, c] = own_rows[c]
    for k in range(1, 4):
        z_copy(k).start()
    lg_group(xs, 2)
    rg_group(xs, 2)
    r_prep(xf)
    q_group(xf)

    rg_group(xf, 3)
    for d in range(32):
        rg_f[pl.ds(d, 32, stride=32), :] = rg_l[:, d * 128:(d + 1) * 128]
    rg_b[...] = rg_f[...].astype(BF16).reshape(2, 512, 128)
    a0 = remote(rg_b.at[other], ra, a_ss.at[0], a_rs.at[0], sib)
    a0.start()
    lg_group(xf, 3)

    def u_step(ib):
        cols = jnp.concatenate(
            [t[:, ib * 4 + ii].reshape(2048, 128) for ii in range(4)], axis=1
        )
        acc = mm(r_j[...], cols)
        for ii in range(4):
            pair_v[4 * ib + ii] = (
                (acc[:, ii * 128:(ii + 1) * 128] + biases[...]) * rec[4 * ib + ii]
            ).astype(BF16)

    u_step(0)
    a0.wait_recv()
    rb[...] = (rg_b[core].astype(F32) + ra[...].astype(F32)).astype(BF16).reshape(4, 128, 128)

    def a_x(k):
        x_ = lax.rem(xx + k, 4)
        return remote(rb.at[x_], rc.at[xx], a_ss.at[k], a_rs.at[1 + xx], dev(zz, x_, core))

    for k in range(1, 4):
        a_x(k).start()
    rc[xx] = rb[xx]
    u_step(1)

    for k in range(1, 4):
        z_ = lax.rem(zz + k, 4)
        remote(s2.at[z_], z_in.at[z_], d_ss.at[6 + k], d_rs.at[7 + z_], sib).wait_recv()
    z_in[zz] = s2[zz]
    right_out[...] = (
        (z_in[0].astype(F32) + z_in[1].astype(F32))
        + (z_in[2].astype(F32) + z_in[3].astype(F32))
    ).astype(BF16)
    f_copy = remote(right_out.at[other], right_in.at[core], d_ss.at[10], d_rs.at[11], sib)
    f_copy.start()
    right_in[core] = right_out[core]
    for k in range(1, 32):
        p = lax.rem(me + k, 32)
        remote(lg_out.at[0], lg_in.at[p], e_ss.at[k], e_rs.at[p], sib).wait_recv()
    remote(
        right_out.at[other], right_in.at[other], d_ss.at[10], d_rs.at[11], sib
    ).wait_recv()
    right_t = jnp.concatenate(
        [right_in[0].astype(F32).T, right_in[1].astype(F32).T], axis=0
    )
    left = lg_in[...].reshape(512, 128).astype(F32)
    for k in range(2):
        both[k * 512:(k + 1) * 512, :] = jnp.concatenate(
            [left[:, k * 32:(k + 1) * 32], right_t[:, k * 32:(k + 1) * 32]], axis=1
        ) * mcol[k * 512:(k + 1) * 512, :]
    pgb = both[...].astype(BF16)
    pj_acc = mm_tn(pgb, normed[...])
    of_acc = jnp.sum(pgb.astype(F32), axis=0, keepdims=True)
    ng_s[...] = mm(pgb, proj[...])
    sc_acc = jnp.sum(ng_s[...] * std[...], axis=0, keepdims=True)
    sh_acc = jnp.sum(ng_s[...], axis=0, keepdims=True)
    pb[0] = pj_acc[0:48].astype(BF16)
    pb[1] = jnp.concatenate(
        [
            pj_acc[48:64], sc_acc, sh_acc,
            jnp.concatenate([of_acc, jnp.zeros((1, 64), F32), bsum[...]], axis=1),
            jnp.zeros((29, 256), F32),
        ],
        axis=0,
    ).astype(BF16)
    b0 = remote(pb.at[other], pb_core, b_ss.at[0], b_rs.at[0], sib)
    b0.start()

    for k in range(1, 4):
        x_ = lax.rem(xx + k, 4)
        remote(rb.at[x_], rc.at[x_], a_ss.at[k], a_rs.at[1 + x_], sib).wait_recv()

    def four(ref):
        return (ref[0].astype(F32) + ref[1].astype(F32)) + (
            ref[2].astype(F32) + ref[3].astype(F32)
        )

    re[zz] = four(rc).astype(BF16)

    def a_z(k):
        z_ = lax.rem(zz + k, 4)
        return remote(re.at[zz], re.at[zz], a_ss.at[3 + k], a_rs.at[5 + zz], dev(z_, xx, core))

    for k in range(1, 4):
        a_z(k).start()

    b0.wait_recv()
    pb_x[xx] = (pb[core].astype(F32) + pb_core[...].astype(F32)).astype(BF16)

    def b_x(k):
        x_ = lax.rem(xx + k, 4)
        return remote(pb_x.at[xx], pb_x.at[xx], b_ss.at[k], b_rs.at[1 + xx], dev(zz, x_, core))

    for k in range(1, 4):
        b_x(k).start()

    for b in range(4):
        rows = slice(b * 256, (b + 1) * 256)
        h = ng_s[rows, :] * scales[...]
        standard = std[rows, :]
        m1 = jnp.mean(h, axis=-1, keepdims=True)
        m2 = jnp.mean(h * standard, axis=-1, keepdims=True)
        al_v[rows, :] = ((h - m1 - standard * m2) * inv[rows, :]).astype(BF16)
    u_step(2)

    for k in range(1, 4):
        z_ = lax.rem(zz + k, 4)
        remote(re.at[z_], re.at[z_], a_ss.at[3 + k], a_rs.at[5 + z_], sib).wait_recv()
    rh[xx] = four(re).astype(BF16)

    def a_g(k):
        x_ = lax.rem(xx + k, 4)
        return remote(rh.at[xx], rh.at[xx], a_ss.at[6 + k], a_rs.at[9 + xx], dev(zz, x_, core))

    for k in range(1, 4):
        a_g(k).start()

    for k in range(1, 4):
        x_ = lax.rem(xx + k, 4)
        remote(pb_x.at[x_], pb_x.at[x_], b_ss.at[k], b_rs.at[1 + x_], sib).wait_recv()
    pb_z[zz] = four(pb_x).astype(BF16)

    def b_z(k):
        z_ = lax.rem(zz + k, 4)
        return remote(
            pb_z.at[zz], pb_z.at[zz], b_ss.at[3 + k], b_rs.at[5 + zz], dev(z_, xx, core)
        )

    for k in range(1, 4):
        b_z(k).start()
    u_step(3)

    def drain(k, carry):
        remote(lg_out.at[0], lg_in.at[0], e_ss.at[k], e_rs.at[0], sib).wait_send()
        remote(r_buf.at[0], r_buf.at[0], r_ss.at[k - 1], r_rs.at[0], sib).wait_send()
        return carry

    lax.fori_loop(1, 32, drain, 0)
    for k in range(32):
        if k != 24:
            remote(l_out.at[0], l_in.at[0], l_ss.at[k], l_rs.at[0], sib).wait_send()
    for n, x_ in enumerate((xf, xm, xs, xx)):
        remote(d_buf.at[x_, other], c_in.at[x_], d_ss.at[n], d_rs.at[x_], sib).wait_send()
    x_copy(xf, 0, xs).wait_send()
    x_copy(xm, 1, xm).wait_send()
    x_copy(xs, 2, xs).wait_send()
    for k in range(1, 4):
        z_copy(k).wait_send()
        a_x(k).wait_send()
        a_z(k).wait_send()
        b_x(k).wait_send()
    a0.wait_send()
    b0.wait_send()
    f_copy.wait_send()

    for k in range(1, 4):
        x_ = lax.rem(xx + k, 4)
        remote(rh.at[x_], rh.at[x_], a_ss.at[6 + k], a_rs.at[9 + x_], sib).wait_recv()
    a_last = remote(rh, rk, a_ss.at[10], a_rs.at[13], sib)
    a_last.start()
    rg_o[pl.ds(pl.multiple_of(core * 512, 512), 512), :] = rh[...].reshape(512, 128).astype(F32)

    for k in range(1, 4):
        z_ = lax.rem(zz + k, 4)
        remote(pb_z.at[z_], pb_z.at[z_], b_ss.at[3 + k], b_rs.at[5 + z_], sib).wait_recv()
    pb_half[core] = four(pb_z).astype(BF16)
    b_last = remote(pb_half.at[core], pb_half.at[core], b_ss.at[7], b_rs.at[9], sib)
    b_last.start()
    for k in range(1, 4):
        a_g(k).wait_send()
        b_z(k).wait_send()
    a_last.wait()
    rg_o[pl.ds(pl.multiple_of(other * 512, 512), 512), :] = rk[...].reshape(512, 128).astype(F32)
    remote(
        pb_half.at[other], pb_half.at[other], b_ss.at[7], b_rs.at[9], sib
    ).wait_recv()
    b_last.wait_send()
    pg_o[...] = jnp.concatenate([pb_half[0], pb_half[1, 0:16]], axis=0).astype(F32)
    vec = pb_half[1, 16:32].astype(F32)
    sg_o[...] = vec[0:1, :]
    hg_o[...] = vec[1:2, :]
    og_o[...] = vec[2:3, 0:64]
    bg_o[...] = vec[2:3, 128:256]


def finish(*refs):
    srcs, dsts, sems = refs[0:8], refs[8:16], refs[16]
    copies = [
        pltpu.make_async_copy(srcs[0].at[pl.ds(4 * n, 4)], dsts[0].at[pl.ds(4 * n, 4)], sems.at[n])
        for n in range(4)
    ]
    copies += [pltpu.make_async_copy(srcs[n], dsts[n], sems.at[3 + n]) for n in range(1, 8)]
    for copy in copies:
        copy.start()
    for copy in copies:
        copy.wait()


def per_device(
    alignment, alignment_mask, cotangent, scales, shifts, projection, offsets, readout, biases
):
    vmem = pl.BlockSpec(memory_space=pltpu.VMEM)
    shape = jax.ShapeDtypeStruct
    sizes = dict(
        al=((1024, 256), BF16),
        mask=((64, 512), jnp.int32),
        readout=((1024, 128), BF16),
        scales=((1, 256), F32),
        shifts=((1, 256), F32),
        proj=((64, 256), BF16),
        offs=((1, 64), F32),
        biases=((1, 128), F32),
        cot_v=((16, 512, 128), BF16),
        mcol=((1024, 1), F32),
        std=((1024, 256), F32),
        inv=((1024, 1), F32),
        normed=((1024, 256), BF16),
        both=((1024, 64), F32),
        l_out=((32, 16, 128), BF16),
        l_in=((32, 16, 128), BF16),
        l_f=((128, 128), F32),
        l_all=((4, 16, 16, 32), BF16),
        l_t=((4, 32, 256), BF16),
        w=((32, 4096), BF16),
        ro_f=((1024, 128), F32),
        rec=((16, 512, 128), F32),
        g=((512, 2048), BF16),
        perm=((512, 512), BF16),
        perm_t=((512, 512), BF16),
        r_buf=((32, 64, 512), BF16),
        r_k=((512, 512), BF16),
        r_j=((512, 2048), BF16),
        t=((4, 16, 32, 16, 128), BF16),
        q=((4, 16, 32, 16, 128), BF16),
        d_buf=((4, 2, 512, 256), BF16),
        c_in=((4, 512, 256), BF16),
        s1=((4, 512, 256), BF16),
        x_in=((3, 512, 256), BF16),
        s2=((4, 2, 64, 256), BF16),
        z_in=((4, 2, 64, 256), BF16),
        right_out=((2, 64, 256), BF16),
        right_in=((2, 64, 256), BF16),
        lg_f=((256, 128), F32),
        lg_out=((32, 16, 128), BF16),
        lg_in=((32, 16, 128), BF16),
        rg_l=((32, 4096), F32),
        rg_f=((1024, 128), F32),
        rg_b=((2, 512, 128), BF16),
        ra=((512, 128), BF16),
        rb=((4, 128, 128), BF16),
        rc=((4, 128, 128), BF16),
        re=((4, 128, 128), BF16),
        rh=((4, 128, 128), BF16),
        rk=((4, 128, 128), BF16),
        ng_s=((1024, 256), F32),
        pb=((2, 48, 256), BF16),
        pb_core=((48, 256), BF16),
        pb_x=((4, 48, 256), BF16),
        pb_z=((4, 48, 256), BF16),
        pb_half=((2, 48, 256), BF16),
        bsum=((1, 128), F32),
    )
    scratch = [pltpu.VMEM(*size) for size in sizes.values()] + [
        pltpu.SemaphoreType.DMA((n,)) for n in (32, 32, 32, 32, 31, 32, 11, 12, 11, 14, 8, 10, 9)
    ]
    anywhere = pl.BlockSpec(memory_space=pl.ANY)
    outs = pl.pallas_call(
        kernel,
        out_shape=(
            pltpu.VMEM((16, 512, 128), BF16),
            pltpu.VMEM((1024, 256), BF16),
            pltpu.VMEM((64, 256), F32),
            pltpu.VMEM((1, 64), F32),
            pltpu.VMEM((1024, 128), F32),
            pltpu.VMEM((1, 128), F32),
            pltpu.VMEM((1, 256), F32),
            pltpu.VMEM((1, 256), F32),
        ),
        in_specs=[anywhere] * 9,
        out_specs=[vmem] * 8,
        scratch_shapes=scratch,
        compiler_params=pltpu.CompilerParams(
            collective_id=0, has_side_effects=True, vmem_limit_bytes=56 * 1024 * 1024
        ),
        cost_estimate=pl.CostEstimate(
            flops=16_000_000_000, bytes_accessed=6_000_000, transcendentals=0
        ),
        name="outer_product_mean",
    )(
        alignment.reshape(1024, 256),
        alignment_mask,
        cotangent,
        scales.reshape(1, 256),
        shifts.reshape(1, 256),
        projection.T,
        offsets.reshape(1, 64),
        readout,
        biases.reshape(1, 128),
    )
    outs = pl.pallas_call(
        finish,
        out_shape=tuple(shape(out.shape, out.dtype) for out in outs),
        in_specs=[vmem] * 8,
        out_specs=[anywhere] * 8,
        scratch_shapes=[pltpu.SemaphoreType.DMA((11,))],
        name="results",
    )(*[pltpu.with_memory_space_constraint(out, pltpu.VMEM) for out in outs])
    return (
        outs[0],
        outs[1].reshape(2, 512, 256),
        outs[2].T,
        outs[3].reshape(64),
        outs[4],
        outs[5].reshape(128),
        outs[6].reshape(256),
        outs[7].reshape(256),
    )


def solution(mesh):
    return jax.shard_map(
        per_device,
        mesh=mesh,
        in_specs=(
            P(("crop", "dap"), None, None),
            P("crop", None),
            P(("crop", "dap"), None, None),
            P(),
            P(),
            P(),
            P(),
            P(),
            P(),
        ),
        out_specs=(
            P(("crop", "dap"), None, None),
            P(("crop", "dap"), None, None),
            P("crop", None),
            P("crop"),
            P("crop", None),
            P("crop"),
            P("crop"),
            P("crop"),
        ),
        check_vma=False,
    )
```

```python
import jax
import jax.numpy as jnp
from jax import lax
from jax.experimental import pallas as pl
from jax.experimental.pallas import tpu as pltpu
from jax.sharding import PartitionSpec as P

F32 = jnp.float32
BF16 = jnp.bfloat16
MESH = pl.DeviceIdType.MESH


def mm(a, b):
    return lax.dot_general(a, b, (((1,), (0,)), ((), ())), preferred_element_type=F32)


def mm_nt(a, b):
    return lax.dot_general(a, b, (((1,), (1,)), ((), ())), preferred_element_type=F32)


def mm_tn(a, b):
    return lax.dot_general(a, b, (((0,), (0,)), ((), ())), preferred_element_type=F32)


def iota(shape, dim):
    return lax.broadcasted_iota(jnp.int32, shape, dim)


def kernel(
    al_h, mask_h, cot, scales_h, shifts_h, proj_h, offs_h, readout_h, biases_h,
    pair_v, al_v, pg_o, og_o, rg_o, bg_o, sg_o, hg_o,
    al, mask, readout, scales, shifts, proj, offs, biases, cot_v,
    mcol, std, inv, normed, both, l_out, l_in, l_f, l_all, l_t, w, ro_f,
    rec, g, perm, perm_t, r_buf, r_k, r_j, t, q,
    d_buf, c_in, s1, x_in, s2, z_in, right_out, right_in,
    lg_f, lg_out, lg_in, rg_l, rg_f, rg_b, ra, rb, rc, re, rh, rk,
    ng_s, pb, pb_core, pb_x, pb_z, pb_half, bsum,
    l_ss, l_rs, e_ss, e_rs, r_ss, r_rs, d_ss, d_rs, a_ss, a_rs, b_ss, b_rs, io,
):
    me = lax.axis_index("dap")
    core = lax.rem(me, 2)
    xx = lax.rem(lax.div(me, 2), 4)
    zz = lax.div(me, 8)
    sign = 1 - 2 * core
    xs, xm, xf = (lax.rem(xx + 4 + sign, 4), lax.rem(xx + 4 - sign, 4), lax.rem(xx + 2, 4))
    zs, zm, zf = (lax.rem(zz + 4 + sign, 4), lax.rem(zz + 4 - sign, 4), lax.rem(zz + 2, 4))
    other = 1 - core

    def dev(z, x, c):
        return (z * 4 + x) * 2 + c

    def slot(x, c, z):
        return (x * 2 + c) * 4 + z

    def slot_dev(s):
        return dev(lax.rem(s, 4), lax.div(s, 8), lax.rem(lax.div(s, 4), 2))

    sib = dev(zz, xx, other)
    mine = slot(xx, core, zz)

    def remote(src, dst, ss, rs, target):
        return pltpu.make_async_remote_copy(
            src_ref=src, dst_ref=dst, send_sem=ss, recv_sem=rs,
            device_id={"dap": target}, device_id_type=MESH,
        )

    barrier = pltpu.get_barrier_semaphore()

    def greet(k, carry):
        pl.semaphore_signal(
            barrier, inc=1, device_id={"dap": lax.rem(me + k, 32)}, device_id_type=MESH
        )
        return carry

    lax.fori_loop(1, 32, greet, 0)
    fetches = [
        pltpu.make_async_copy(src, dst, io.at[n])
        for n, (src, dst) in enumerate((
            (mask_h, mask), (al_h, al), (scales_h, scales), (shifts_h, shifts), (proj_h, proj),
            (offs_h, offs), (cot, cot_v), (readout_h, readout), (biases_h, biases),
        ))
    ]
    for fetch in fetches:
        fetch.start()
    fetches[0].wait()

    mask_f = mask[...].astype(F32)
    mask_t = mask_f.T
    for k in range(2):
        mcol[k * 512:(k + 1) * 512, :] = jnp.sum(
            jnp.where(iota((512, 64), 1) == 2 * me + k, mask_t, 0.0), axis=1, keepdims=True
        )
    for fetch in fetches[1:6]:
        fetch.wait()
    for k in range(2):
        rows = slice(k * 512, (k + 1) * 512)
        wide = al[rows, :].astype(F32)
        center = jnp.mean(wide, axis=-1, keepdims=True)
        apart = wide - center
        spread = jnp.mean(apart * apart, axis=-1, keepdims=True)
        inverse = lax.rsqrt(spread + 1e-05)
        standard = apart * inverse
        std[rows, :] = standard
        inv[rows, :] = inverse
        normed[rows, :] = (standard * scales[...] + shifts[...]).astype(BF16)
    both[...] = (mm_nt(normed[...], proj[...]) + offs[...]) * mcol[...]
    cat = jnp.concatenate([both[0:512, :], both[512:1024, :]], axis=1)
    l_out[...] = cat.astype(BF16).reshape(32, 16, 128)
    cat_t = cat.T
    r_buf[mine] = jnp.concatenate([cat_t[32:64], cat_t[96:128]], axis=0).astype(BF16)

    pl.semaphore_wait(barrier, 31)

    def l_copy(s, k):
        p = slot_dev(s)
        return remote(l_out.at[p], l_in.at[mine], l_ss.at[k], l_rs.at[mine], p)

    def r_send(s, target, k):
        remote(r_buf.at[s], r_buf.at[s], r_ss.at[k], r_rs.at[s], target).start()

    def r_wait(s):
        remote(r_buf.at[s], r_buf.at[s], r_ss.at[0], r_rs.at[s], sib).wait_recv()

    r_send(mine, dev(zs, xx, core), 0)
    r_send(mine, dev(zm, xx, core), 1)
    for k in range(8):
        l_copy(xf * 8 + k, k).start()
    r_send(mine, dev(zz, xs, core), 2)
    r_send(mine, dev(zz, xm, core), 3)
    r_send(mine, sib, 4)
    for n, x_ in ((1, xs), (2, xm)):
        for k in range(8):
            l_copy(x_ * 8 + k, n * 8 + k).start()
    for k in range(1, 8):
        l_copy(xx * 8 + lax.rem(core * 4 + zz + k, 8), 24 + k).start()
    l_in[mine] = l_out[me]

    mask_b = mask_f.astype(BF16)
    own_cols = (iota((512, 16), 0) == 16 * me + iota((512, 16), 1)).astype(F32).astype(BF16)
    mask_own = mm(mask_b, own_cols).astype(BF16)
    recip = 1.0 / (0.001 + mm(mask_t.astype(BF16), mask_own))
    total = jnp.zeros((1, 128), F32)
    fetches[6].wait()
    for i in range(16):
        rec_i = jnp.broadcast_to(recip[:, i:i + 1], (512, 128))
        rec[i] = rec_i
        sg = (cot_v[i].astype(F32) * rec_i).astype(BF16)
        g[:, i * 128:(i + 1) * 128] = sg
        total = total + jnp.sum(sg.astype(F32), axis=0, keepdims=True)
    bsum[...] = total

    fetches[7].wait()
    fetches[8].wait()
    ro_f[...] = readout[...].astype(F32)
    for d in range(32):
        w[:, d * 128:(d + 1) * 128] = ro_f[pl.ds(d, 32, stride=32), :].astype(BF16)

    def packed(a):
        return lax.rem(a, 8) * 64 + lax.rem(lax.div(a, 8), 2) * 32 + lax.div(a, 16)

    perm[...] = (iota((512, 512), 1) == packed(iota((512, 512), 0))).astype(F32).astype(BF16)
    perm_t[...] = (iota((512, 512), 0) == packed(iota((512, 512), 1))).astype(F32).astype(BF16)

    def t_group(x_, own=False):
        for k in range(1 if own else 0, 8):
            s = x_ * 8 + (lax.rem(core * 4 + zz + k, 8) if own else k)
            remote(l_out.at[0], l_in.at[s], l_ss.at[0], l_rs.at[s], sib).wait_recv()
        l_f[...] = l_in[pl.ds(x_ * 8, 8)].reshape(128, 128).astype(F32)
        for i in range(16):
            part = l_f[pl.ds(i, 8, stride=16), :]
            l_all[x_, i] = jnp.concatenate([part[:, 0:32], part[:, 64:96]], axis=0).astype(BF16)
        rows = l_all[x_].reshape(256, 32)
        l_t[x_] = rows.astype(F32).T.astype(BF16)
        r = mm(rows, w[...]).astype(BF16)
        for d in range(32):
            t[x_, :, d] = r[:, d * 128:(d + 1) * 128].reshape(16, 16, 128)

    def d_group(x_, n):
        rows = jnp.concatenate([t[x_, i].reshape(512, 128) for i in range(16)], axis=1)
        raw = mm_nt(rows, g[...]).astype(BF16)
        for h in range(2):
            d_buf[x_, h] = raw[:, h * 256:(h + 1) * 256]
        remote(d_buf.at[x_, other], c_in.at[x_], d_ss.at[n], d_rs.at[x_], sib).start()

    def c_wait(x_, n):
        remote(d_buf.at[x_, other], c_in.at[x_], d_ss.at[n], d_rs.at[x_], sib).wait_recv()

    def core_sum(x_):
        return d_buf[x_, core].astype(F32) + c_in[x_].astype(F32)

    def x_copy(x_, n, target_x):
        return remote(
            s1.at[x_], x_in.at[n], d_ss.at[4 + n], d_rs.at[4 + n], dev(zz, target_x, core)
        )

    r_wait(slot(xx, core, zm))
    r_send(slot(xx, core, zm), dev(zs, xx, core), 5)
    for n, z_ in enumerate((zm, zs)):
        if n == 1:
            r_wait(slot(xx, core, z_))
        r_send(slot(xx, core, z_), dev(zz, xs, core), 6 + 3 * n)
        r_send(slot(xx, core, z_), dev(zz, xm, core), 7 + 3 * n)
        r_send(slot(xx, core, z_), sib, 8 + 3 * n)
    t_group(xf)
    r_wait(slot(xm, core, zz))
    r_send(slot(xm, core, zz), dev(zz, xs, core), 15)
    r_send(slot(xm, core, zz), sib, 16)
    r_wait(slot(xs, core, zz))
    r_send(slot(xs, core, zz), sib, 17)
    d_group(xf, 0)
    t_group(xm)
    r_wait(slot(xx, core, zf))
    r_send(slot(xx, core, zf), dev(zz, xs, core), 12)
    r_send(slot(xx, core, zf), dev(zz, xm, core), 13)
    r_send(slot(xx, core, zf), sib, 14)
    d_group(xm, 1)
    c_wait(xf, 0)
    s1[xf] = core_sum(xf).astype(BF16)
    x_copy(xf, 0, xs).start()
    for n, z_ in enumerate((zm, zs)):
        r_wait(slot(xm, core, z_))
        r_send(slot(xm, core, z_), dev(zz, xs, core), 18 + 3 * n)
        r_send(slot(xm, core, z_), sib, 19 + 3 * n)
        r_wait(slot(xs, core, z_))
        r_send(slot(xs, core, z_), sib, 20 + 3 * n)
    t_group(xs)
    d_group(xs, 2)
    c_wait(xm, 1)
    s1[xm] = core_sum(xm).astype(BF16)
    x_copy(xm, 1, xm).start()
    r_wait(slot(xf, core, zz))
    r_send(slot(xf, core, zz), sib, 27)
    t_group(xx, own=True)
    r_wait(slot(xm, core, zf))
    r_send(slot(xm, core, zf), dev(zz, xs, core), 24)
    r_send(slot(xm, core, zf), sib, 25)
    r_wait(slot(xs, core, zf))
    r_send(slot(xs, core, zf), sib, 26)
    d_group(xx, 3)

    def r_prep(x_):
        for z_ in range(4):
            r_wait(slot(x_, other, z_))
        raw = r_buf[pl.ds(x_ * 8, 8)].reshape(512, 512)
        moved = mm(perm[...], raw)
        r_k[...] = moved.astype(BF16)
        r_j[:, pl.ds(pl.multiple_of(x_ * 512, 512), 512)] = moved.T.astype(BF16)

    def e_copy(s, k):
        return remote(lg_out.at[s], lg_in.at[me], e_ss.at[k], e_rs.at[me], slot_dev(s))

    def q_group(x_):
        for h in range(2):
            block = mm(r_k[...], g[:, h * 1024:(h + 1) * 1024]).astype(BF16)
            for i in range(8):
                q[x_, h * 8 + i] = block[:, i * 128:(i + 1) * 128].reshape(32, 16, 128)

    def lg_group(x_, n):
        rows = jnp.concatenate([q[x_, :, d].reshape(256, 128) for d in range(32)], axis=1)
        lg_f[:, 0:32] = mm_nt(rows, w[...])
        for c in range(8):
            pieces = [lg_f[pl.ds(c + 8 * k, 16, stride=16), :][:, 0:32] for k in range(2)]
            pieces.append(jnp.zeros((16, 64), F32))
            lg_out[x_ * 8 + c] = jnp.concatenate(pieces, axis=1).astype(BF16)
        if n == 0:
            for k in range(1, 8):
                e_copy(x_ * 8 + lax.rem(core * 4 + zz + k, 8), k).start()
            lg_in[me] = lg_out[mine]
        else:
            for k in range(8):
                e_copy(x_ * 8 + k, n * 8 + k).start()

    def z_copy(k):
        z_ = lax.rem(zz + k, 4)
        return remote(
            s2.at[z_], z_in.at[zz], d_ss.at[6 + k], d_rs.at[7 + zz], dev(z_, xx, core)
        )

    def rg_group(x_, n):
        rows = jnp.concatenate([q[x_, :, d].reshape(256, 128) for d in range(32)], axis=1)
        part = mm(l_t[x_], rows)
        rg_l[...] = part if n == 0 else rg_l[...] + part

    r_prep(xx)
    q_group(xx)
    c_wait(xs, 2)
    x_copy(xf, 0, xs).wait_recv()
    s1[xs] = (core_sum(xs) + x_in[0].astype(F32)).astype(BF16)
    x_copy(xs, 2, xs).start()
    for n, z_ in enumerate((zm, zs)):
        r_wait(slot(xf, core, z_))
        r_send(slot(xf, core, z_), sib, 28 + n)
    lg_group(xx, 0)
    rg_group(xx, 0)
    r_wait(slot(xf, core, zf))
    r_send(slot(xf, core, zf), sib, 30)
    r_prep(xm)
    q_group(xm)
    lg_group(xm, 1)
    rg_group(xm, 1)
    r_prep(xs)
    q_group(xs)
    c_wait(xx, 3)
    x_copy(xm, 1, xm).wait_recv()
    x_copy(xs, 2, xs).wait_recv()
    own_sum = (core_sum(xx) + x_in[1].astype(F32) + x_in[2].astype(F32)).astype(BF16)
    own_rows = mm(perm_t[...], own_sum).astype(BF16).reshape(2, 4, 64, 256)
    for c in range(2):
        s2[:, c] = own_rows[c]
    for k in range(1, 4):
        z_copy(k).start()
    lg_group(xs, 2)
    rg_group(xs, 2)
    r_prep(xf)
    q_group(xf)

    rg_group(xf, 3)
    for d in range(32):
        rg_f[pl.ds(d, 32, stride=32), :] = rg_l[:, d * 128:(d + 1) * 128]
    rg_b[...] = rg_f[...].astype(BF16).reshape(2, 512, 128)
    a0 = remote(rg_b.at[other], ra, a_ss.at[0], a_rs.at[0], sib)
    a0.start()
    lg_group(xf, 3)

    def u_step(ib):
        cols = jnp.concatenate(
            [t[:, ib * 4 + ii].reshape(2048, 128) for ii in range(4)], axis=1
        )
        acc = mm(r_j[...], cols)
        for ii in range(4):
            pair_v[4 * ib + ii] = (
                (acc[:, ii * 128:(ii + 1) * 128] + biases[...]) * rec[4 * ib + ii]
            ).astype(BF16)

    u_step(0)
    a0.wait_recv()
    rb[...] = (rg_b[core].astype(F32) + ra[...].astype(F32)).astype(BF16).reshape(4, 128, 128)

    def a_x(k):
        x_ = lax.rem(xx + k, 4)
        return remote(rb.at[x_], rc.at[xx], a_ss.at[k], a_rs.at[1 + xx], dev(zz, x_, core))

    for k in range(1, 4):
        a_x(k).start()
    rc[xx] = rb[xx]
    u_step(1)

    for k in range(1, 4):
        z_ = lax.rem(zz + k, 4)
        remote(s2.at[z_], z_in.at[z_], d_ss.at[6 + k], d_rs.at[7 + z_], sib).wait_recv()
    z_in[zz] = s2[zz]
    right_out[...] = (
        (z_in[0].astype(F32) + z_in[1].astype(F32))
        + (z_in[2].astype(F32) + z_in[3].astype(F32))
    ).astype(BF16)
    f_copy = remote(right_out.at[other], right_in.at[core], d_ss.at[10], d_rs.at[11], sib)
    f_copy.start()
    right_in[core] = right_out[core]
    for k in range(1, 32):
        p = lax.rem(me + k, 32)
        remote(lg_out.at[0], lg_in.at[p], e_ss.at[k], e_rs.at[p], sib).wait_recv()
    remote(
        right_out.at[other], right_in.at[other], d_ss.at[10], d_rs.at[11], sib
    ).wait_recv()
    right_t = jnp.concatenate(
        [right_in[0].astype(F32).T, right_in[1].astype(F32).T], axis=0
    )
    left = lg_in[...].reshape(512, 128).astype(F32)
    for k in range(2):
        both[k * 512:(k + 1) * 512, :] = jnp.concatenate(
            [left[:, k * 32:(k + 1) * 32], right_t[:, k * 32:(k + 1) * 32]], axis=1
        ) * mcol[k * 512:(k + 1) * 512, :]
    pgb = both[...].astype(BF16)
    pj_acc = mm_tn(pgb, normed[...])
    of_acc = jnp.sum(pgb.astype(F32), axis=0, keepdims=True)
    ng_s[...] = mm(pgb, proj[...])
    sc_acc = jnp.sum(ng_s[...] * std[...], axis=0, keepdims=True)
    sh_acc = jnp.sum(ng_s[...], axis=0, keepdims=True)
    pb[0] = pj_acc[0:48].astype(BF16)
    pb[1] = jnp.concatenate(
        [
            pj_acc[48:64], sc_acc, sh_acc,
            jnp.concatenate([of_acc, jnp.zeros((1, 64), F32), bsum[...]], axis=1),
            jnp.zeros((29, 256), F32),
        ],
        axis=0,
    ).astype(BF16)
    b0 = remote(pb.at[other], pb_core, b_ss.at[0], b_rs.at[0], sib)
    b0.start()

    for k in range(1, 4):
        x_ = lax.rem(xx + k, 4)
        remote(rb.at[x_], rc.at[x_], a_ss.at[k], a_rs.at[1 + x_], sib).wait_recv()

    def four(ref):
        return (ref[0].astype(F32) + ref[1].astype(F32)) + (
            ref[2].astype(F32) + ref[3].astype(F32)
        )

    re[zz] = four(rc).astype(BF16)

    def a_z(k):
        z_ = lax.rem(zz + k, 4)
        return remote(re.at[zz], re.at[zz], a_ss.at[3 + k], a_rs.at[5 + zz], dev(z_, xx, core))

    for k in range(1, 4):
        a_z(k).start()

    b0.wait_recv()
    pb_x[xx] = (pb[core].astype(F32) + pb_core[...].astype(F32)).astype(BF16)

    def b_x(k):
        x_ = lax.rem(xx + k, 4)
        return remote(pb_x.at[xx], pb_x.at[xx], b_ss.at[k], b_rs.at[1 + xx], dev(zz, x_, core))

    for k in range(1, 4):
        b_x(k).start()

    for b in range(4):
        rows = slice(b * 256, (b + 1) * 256)
        h = ng_s[rows, :] * scales[...]
        standard = std[rows, :]
        m1 = jnp.mean(h, axis=-1, keepdims=True)
        m2 = jnp.mean(h * standard, axis=-1, keepdims=True)
        al_v[rows, :] = ((h - m1 - standard * m2) * inv[rows, :]).astype(BF16)
    u_step(2)

    for k in range(1, 4):
        z_ = lax.rem(zz + k, 4)
        remote(re.at[z_], re.at[z_], a_ss.at[3 + k], a_rs.at[5 + z_], sib).wait_recv()
    rh[xx] = four(re).astype(BF16)

    def a_g(k):
        x_ = lax.rem(xx + k, 4)
        return remote(rh.at[xx], rh.at[xx], a_ss.at[6 + k], a_rs.at[9 + xx], dev(zz, x_, core))

    for k in range(1, 4):
        a_g(k).start()

    for k in range(1, 4):
        x_ = lax.rem(xx + k, 4)
        remote(pb_x.at[x_], pb_x.at[x_], b_ss.at[k], b_rs.at[1 + x_], sib).wait_recv()
    pb_z[zz] = four(pb_x).astype(BF16)

    def b_z(k):
        z_ = lax.rem(zz + k, 4)
        return remote(
            pb_z.at[zz], pb_z.at[zz], b_ss.at[3 + k], b_rs.at[5 + zz], dev(z_, xx, core)
        )

    for k in range(1, 4):
        b_z(k).start()
    u_step(3)

    def drain(k, carry):
        remote(lg_out.at[0], lg_in.at[0], e_ss.at[k], e_rs.at[0], sib).wait_send()
        remote(r_buf.at[0], r_buf.at[0], r_ss.at[k - 1], r_rs.at[0], sib).wait_send()
        return carry

    lax.fori_loop(1, 32, drain, 0)
    for k in range(32):
        if k != 24:
            remote(l_out.at[0], l_in.at[0], l_ss.at[k], l_rs.at[0], sib).wait_send()
    for n, x_ in enumerate((xf, xm, xs, xx)):
        remote(d_buf.at[x_, other], c_in.at[x_], d_ss.at[n], d_rs.at[x_], sib).wait_send()
    x_copy(xf, 0, xs).wait_send()
    x_copy(xm, 1, xm).wait_send()
    x_copy(xs, 2, xs).wait_send()
    for k in range(1, 4):
        z_copy(k).wait_send()
        a_x(k).wait_send()
        a_z(k).wait_send()
        b_x(k).wait_send()
    a0.wait_send()
    b0.wait_send()
    f_copy.wait_send()

    for k in range(1, 4):
        x_ = lax.rem(xx + k, 4)
        remote(rh.at[x_], rh.at[x_], a_ss.at[6 + k], a_rs.at[9 + x_], sib).wait_recv()
    a_last = remote(rh, rk, a_ss.at[10], a_rs.at[13], sib)
    a_last.start()
    rg_o[pl.ds(pl.multiple_of(core * 512, 512), 512), :] = rh[...].reshape(512, 128).astype(F32)

    for k in range(1, 4):
        z_ = lax.rem(zz + k, 4)
        remote(pb_z.at[z_], pb_z.at[z_], b_ss.at[3 + k], b_rs.at[5 + z_], sib).wait_recv()
    pb_half[core] = four(pb_z).astype(BF16)
    b_last = remote(pb_half.at[core], pb_half.at[core], b_ss.at[7], b_rs.at[9], sib)
    b_last.start()
    for k in range(1, 4):
        a_g(k).wait_send()
        b_z(k).wait_send()
    a_last.wait()
    rg_o[pl.ds(pl.multiple_of(other * 512, 512), 512), :] = rk[...].reshape(512, 128).astype(F32)
    remote(
        pb_half.at[other], pb_half.at[other], b_ss.at[7], b_rs.at[9], sib
    ).wait_recv()
    b_last.wait_send()
    pg_o[...] = jnp.concatenate([pb_half[0], pb_half[1, 0:16]], axis=0).astype(F32)
    vec = pb_half[1, 16:32].astype(F32)
    sg_o[...] = vec[0:1, :]
    hg_o[...] = vec[1:2, :]
    og_o[...] = vec[2:3, 0:64]
    bg_o[...] = vec[2:3, 128:256]


def finish(*refs):
    srcs, dsts, sems = refs[0:8], refs[8:16], refs[16]
    copies = [
        pltpu.make_async_copy(srcs[0].at[pl.ds(4 * n, 4)], dsts[0].at[pl.ds(4 * n, 4)], sems.at[n])
        for n in range(4)
    ]
    copies += [pltpu.make_async_copy(srcs[n], dsts[n], sems.at[3 + n]) for n in range(1, 8)]
    for copy in copies:
        copy.start()
    for copy in copies:
        copy.wait()


def per_device(
    alignment, alignment_mask, cotangent, scales, shifts, projection, offsets, readout, biases
):
    vmem = pl.BlockSpec(memory_space=pltpu.VMEM)
    shape = jax.ShapeDtypeStruct
    sizes = dict(
        al=((1024, 256), BF16),
        mask=((64, 512), jnp.int32),
        readout=((1024, 128), BF16),
        scales=((1, 256), F32),
        shifts=((1, 256), F32),
        proj=((64, 256), BF16),
        offs=((1, 64), F32),
        biases=((1, 128), F32),
        cot_v=((16, 512, 128), BF16),
        mcol=((1024, 1), F32),
        std=((1024, 256), F32),
        inv=((1024, 1), F32),
        normed=((1024, 256), BF16),
        both=((1024, 64), F32),
        l_out=((32, 16, 128), BF16),
        l_in=((32, 16, 128), BF16),
        l_f=((128, 128), F32),
        l_all=((4, 16, 16, 32), BF16),
        l_t=((4, 32, 256), BF16),
        w=((32, 4096), BF16),
        ro_f=((1024, 128), F32),
        rec=((16, 512, 128), F32),
        g=((512, 2048), BF16),
        perm=((512, 512), BF16),
        perm_t=((512, 512), BF16),
        r_buf=((32, 64, 512), BF16),
        r_k=((512, 512), BF16),
        r_j=((512, 2048), BF16),
        t=((4, 16, 32, 16, 128), BF16),
        q=((4, 16, 32, 16, 128), BF16),
        d_buf=((4, 2, 512, 256), BF16),
        c_in=((4, 512, 256), BF16),
        s1=((4, 512, 256), BF16),
        x_in=((3, 512, 256), BF16),
        s2=((4, 2, 64, 256), BF16),
        z_in=((4, 2, 64, 256), BF16),
        right_out=((2, 64, 256), BF16),
        right_in=((2, 64, 256), BF16),
        lg_f=((256, 128), F32),
        lg_out=((32, 16, 128), BF16),
        lg_in=((32, 16, 128), BF16),
        rg_l=((32, 4096), F32),
        rg_f=((1024, 128), F32),
        rg_b=((2, 512, 128), BF16),
        ra=((512, 128), BF16),
        rb=((4, 128, 128), BF16),
        rc=((4, 128, 128), BF16),
        re=((4, 128, 128), BF16),
        rh=((4, 128, 128), BF16),
        rk=((4, 128, 128), BF16),
        ng_s=((1024, 256), F32),
        pb=((2, 48, 256), BF16),
        pb_core=((48, 256), BF16),
        pb_x=((4, 48, 256), BF16),
        pb_z=((4, 48, 256), BF16),
        pb_half=((2, 48, 256), BF16),
        bsum=((1, 128), F32),
    )
    scratch = [pltpu.VMEM(*size) for size in sizes.values()] + [
        pltpu.SemaphoreType.DMA((n,)) for n in (32, 32, 32, 32, 31, 32, 11, 12, 11, 14, 8, 10, 9)
    ]
    anywhere = pl.BlockSpec(memory_space=pl.ANY)
    outs = pl.pallas_call(
        kernel,
        out_shape=(
            pltpu.VMEM((16, 512, 128), BF16),
            pltpu.VMEM((1024, 256), BF16),
            pltpu.VMEM((64, 256), F32),
            pltpu.VMEM((1, 64), F32),
            pltpu.VMEM((1024, 128), F32),
            pltpu.VMEM((1, 128), F32),
            pltpu.VMEM((1, 256), F32),
            pltpu.VMEM((1, 256), F32),
        ),
        in_specs=[anywhere] * 9,
        out_specs=[vmem] * 8,
        scratch_shapes=scratch,
        compiler_params=pltpu.CompilerParams(
            collective_id=0, has_side_effects=True, vmem_limit_bytes=56 * 1024 * 1024
        ),
        cost_estimate=pl.CostEstimate(
            flops=16_000_000_000, bytes_accessed=6_000_000, transcendentals=0
        ),
        name="outer_product_mean",
    )(
        alignment.reshape(1024, 256),
        alignment_mask,
        cotangent,
        scales.reshape(1, 256),
        shifts.reshape(1, 256),
        projection.T,
        offsets.reshape(1, 64),
        readout,
        biases.reshape(1, 128),
    )
    outs = pl.pallas_call(
        finish,
        out_shape=tuple(shape(out.shape, out.dtype) for out in outs),
        in_specs=[vmem] * 8,
        out_specs=[anywhere] * 8,
        scratch_shapes=[pltpu.SemaphoreType.DMA((11,))],
        name="results",
    )(*[pltpu.with_memory_space_constraint(out, pltpu.VMEM) for out in outs])
    return (
        outs[0],
        outs[1].reshape(2, 512, 256),
        outs[2].T,
        outs[3].reshape(64),
        outs[4],
        outs[5].reshape(128),
        outs[6].reshape(256),
        outs[7].reshape(256),
    )


def solution(mesh):
    return jax.shard_map(
        per_device,
        mesh=mesh,
        in_specs=(
            P(("crop", "dap"), None, None),
            P("crop", None),
            P(("crop", "dap"), None, None),
            P(),
            P(),
            P(),
            P(),
            P(),
            P(),
        ),
        out_specs=(
            P(("crop", "dap"), None, None),
            P(("crop", "dap"), None, None),
            P("crop", None),
            P("crop"),
            P("crop", None),
            P("crop"),
            P("crop"),
            P("crop"),
        ),
        check_vma=False,
    )
```
